32 devices in a mesh: band: 8 (over y, x, core), ga: 4 (over z).
Axes of the slice: x: 2, y: 2, z: 4, core: 2. Of those that a mesh axis runs over, the one named last changes fastest.
Arguments:
- waves: bfloat16 [2, 64, 4, 147456], P(None, 'band', None, 'ga'), as said below
- ionic_field: float32 [384, 1536], P('ga'), may hold values from -1 to 3
- point_charge: float32 [8192], P(('band', 'ga')), may hold values from -6 to 6
- charge_place: float32 [3, 8192], P(None, ('band', 'ga')), may hold values from 0 to 1
- charge_slab: int32 [8192, 1], P(('band', 'ga')), may hold values from 0 to 3; in each aligned block of 256 rows (0 to 255, 256 to 511, ...) at most 128 rows name the same one
Outputs:
- applied_waves: bfloat16 [2, 64, 4, 147456], P(None, 'band', None, 'ga')
- subspace: float32 [2, 64, 64], P(None, 'band', 'ga')
The draws below stay inside these ranges and needn't reach their ends.
Inputs may be any that keep to these rules, and one draw needn't show every extreme that they name: `waves`: entries are of order one. `charge_slab`: among the 256 rows of one device at most 128 name the same slab, and in every draw some device has exactly 128 rows naming one slab.
All inputs are finite; a program needn't handle non-finite values.
Results may differ from the reference program's by a relative error of at most 0.0073.
Values may be sent and summed in bfloat16 or wider, within the bound.
No kernel may reach another device: no remote copies, remote signals or barrier semaphores. Data moves between devices by JAX's collectives and lax.ppermute only.
A program may use at most 192 MiB of HBM per device.

```python
import math
import jax
import jax.numpy as jnp
import numpy as np
from jax import lax

NX = 384
NY = 384
P_SIZE = 4
A_DEV = 256
NB = 64
SLAB = 96
NMM = 8192
N_GA = 4


def draw_waves(key, part):
    key = jax.random.fold_in(key, 7)
    key_base, key_first, key_second = jax.random.split(key, 3)
    shape_all = (2, NB, P_SIZE, NX * NY)
    base_draw = jnp.clip(jax.random.normal(key_base, shape_all, jnp.float32), -4.0, 4.0)
    first_order = jax.random.permutation(key_first, NB)
    second_order = jax.random.permutation(key_second, NB)
    mixed_one = base_draw[:, first_order]
    turned = base_draw[:, second_order]
    turned = jnp.stack([-turned[1], turned[0]])
    return (base_draw + 0.5 * mixed_one + 0.5 * turned).astype(jnp.bfloat16)


def level_of(own_key, extent, shards, least, high):
    factor_of, own = 1.0, jax.random.fold_in(own_key, 6)
    for axis_at, parts in shards:
        steps = jnp.exp(jax.random.uniform(jax.random.fold_in(own, axis_at), (parts,), jnp.float32, least / len(shards), high / len(shards)))
        factor_of = factor_of * jnp.repeat(steps, extent[axis_at] // parts).reshape([-1 if axis == axis_at else 1 for axis in range(len(extent))])
    return factor_of


def routed_block(own_key, own, number, rows, number_of, top, limit, slope):
    ranking = jax.random.permutation(own_key, number_of)
    heavy_load, usual = load_shares(number_of, rows * top, limit, slope, True), load_shares(number_of, rows * top, limit, slope, False)
    places = jnp.arange(number_of)

    def named(lengths, turn):
        used = int((lengths > 0).sum())
        fixed = max(1, used // 4)
        moved = fixed + (places - fixed + turn * (used - fixed)) % max(1, number_of - fixed)
        return jnp.zeros((number_of,), jnp.int32).at[ranking[jnp.where(places < fixed, places, moved)]].set(jnp.asarray(lengths, jnp.int32))

    lengths = jnp.where(number % 4 == 0, named(heavy_load, number // 4), named(usual, number - number // 4 - 1))
    mixed = jax.random.permutation(jax.random.fold_in(own, 3), number_of)
    donor, taker = mixed[0:number_of // 2 * 2:2], mixed[1:number_of // 2 * 2:2]
    slack = jnp.minimum(lengths[donor] - 1, limit - lengths[taker]) // 2
    slack = jnp.where((donor == ranking[0]) | (taker == ranking[0]) | (lengths[taker] == 0), 0, jnp.maximum(slack, 0))
    moved = jax.random.randint(jax.random.fold_in(own, 4), (number_of // 2,), 0, 1 << 20) % (slack + 1)
    lengths = lengths.at[donor].add(-moved).at[taker].add(moved)
    labels = jnp.searchsorted(jnp.cumsum(lengths), jnp.arange(rows * top), side="right").astype(jnp.int32)
    table = labels.reshape(top, rows).T
    table = table[jax.random.permutation(jax.random.fold_in(own, 1), rows)]
    turn = jax.random.randint(jax.random.fold_in(own, 2), (rows, 1), 0, top)
    return jnp.take_along_axis(table, (jnp.arange(top)[None, :] + turn) % top, axis=1)


def load_shares(count, total, reach, slope, full):
    weights = [(1 << 20) // math.isqrt(rank ** slope) + 1 for rank in range(1, count + 1)]
    largest = reach if full else min(reach, max(-(-total // count), total * weights[0] // sum(weights)))
    least = 1 if total - largest >= count - 1 else 0
    counts, spare = [largest] + [least] * (count - 1), total - largest - least * (count - 1)
    while spare > 0:
        movable = [i for i in range(1, count) if counts[i] < largest] or [i for i in range(1, count) if counts[i] < reach]
        pool, left = sum([weights[i] for i in movable]), spare
        for i in movable:
            extra = min(reach - counts[i], max(1, left * weights[i] // pool), spare)
            counts[i] = counts[i] + extra
            spare = spare - extra
    return np.array(counts)


def bell_draw(stream_key, dims, spread, limit, cuts=(), kind=jnp.bfloat16):
    values = jax.random.normal(stream_key, dims, jnp.float32) * spread
    if len(cuts) > 0:
        values = level_of(stream_key, dims, cuts, -0.22, 0.18) * values
    return jnp.clip(values, min=-limit, max=limit).astype(kind)


def setup_inputs(seed: int = 0) -> dict:
    keys = jax.random.split(jax.random.key(seed), 6)
    waves = draw_waves(jax.random.fold_in(keys[5], 71), 0)
    ionic_field = jnp.clip(-1.0 + 4.0 * jax.random.uniform(keys[1], (NY, P_SIZE * NX), jnp.float32) ** level_of(keys[1], (NY, P_SIZE * NX), ((0, 4),), -0.2, 0.2), -1.0, 3.0)
    point_charge = bell_draw(keys[2], (NMM,), 1.0, 6.0, ((0, 32),), jnp.float32)
    charge_place = jnp.clip(1.0 * jax.random.uniform(keys[3], (3, NMM), jnp.float32) ** level_of(keys[3], (3, NMM), ((1, 32),), -0.2, 0.2), 0.0, 1.0)
    charge_slab_keys = jax.random.split(jax.random.fold_in(keys[4], 1), NMM // A_DEV)
    charge_slab_turns = jax.random.permutation(jax.random.fold_in(keys[4], 3), NMM // A_DEV)
    charge_slab = jax.vmap(lambda own, number: routed_block(jax.random.fold_in(keys[4], 2), own, number, A_DEV, N_GA, 1, A_DEV // 2, 2))(charge_slab_keys, charge_slab_turns).reshape((NMM, 1))
    return {"waves": waves, "ionic_field": ionic_field, "point_charge": point_charge, "charge_place": charge_place, "charge_slab": charge_slab}


width_cells = 1.5

def tables(length):
    indices = jnp.arange(length, dtype=jnp.int32)
    phases = indices[:, None] * indices[None, :] % length
    angles = phases.astype(jnp.float32) * (2.0 * jnp.pi / length)
    factor = 1.0 / jnp.sqrt(jnp.float32(length))
    return jnp.stack([jnp.cos(angles) * factor, jnp.sin(angles) * factor]).astype(jnp.bfloat16)

def combine(products, sign_flip):
    return jnp.stack([products[0, 0] - sign_flip * products[1, 1], sign_flip * products[0, 1] + products[1, 0]])

def product_f32(form, left_side, right_side):
    return jnp.einsum(form, left_side.astype(jnp.float32), right_side.astype(jnp.float32), precision=lax.Precision.HIGHEST)

def gaussian(distance):
    return jnp.exp(-distance * distance / (2.0 * width_cells * width_cells))

def frequency(indices, length):
    return jnp.where(indices < length // 2, indices, indices - length).astype(jnp.float32)

def charge_field(point_charge, charge_place, charge_slab):
    target = charge_slab[:, 0]
    cells_x = jnp.arange(NX, dtype=jnp.float32)
    cells_y = jnp.arange(NY, dtype=jnp.float32)
    plane_cells = jnp.arange(P_SIZE, dtype=jnp.float32)
    along_y = target.astype(jnp.float32) * SLAB + SLAB * charge_place[1]
    kernel_x = gaussian(cells_x[None, :] - NX * charge_place[0][:, None])
    inside = jnp.arange(NY, dtype=jnp.int32)[None, :] // SLAB == target[:, None]
    kernel_y = gaussian(cells_y[None, :] - along_y[:, None]) * inside.astype(jnp.float32)
    kernel_z = gaussian(plane_cells[None, :] - P_SIZE * charge_place[2][:, None])
    right_side = ((point_charge[:, None] * kernel_z)[:, :, None] * kernel_x[:, None, :]).reshape(NMM, P_SIZE * NX)
    return jnp.dot(kernel_y.T, right_side, precision=lax.Precision.HIGHEST, preferred_element_type=jnp.float32)

def reference(waves, ionic_field, point_charge, charge_place, charge_slab):
    potential = (ionic_field + charge_field(point_charge, charge_place, charge_slab)).reshape(NY, P_SIZE, NX)
    table_rows = tables(NX)
    table_cols = tables(NY)
    freq_x = frequency(jnp.arange(NX, dtype=jnp.int32), NX)
    freq_y = frequency(jnp.arange(NY, dtype=jnp.int32), NY)
    kinetic = 2.0 * (freq_x[:, None] * freq_x[:, None] / (NX * NX) + freq_y[None, :] * freq_y[None, :] / (NY * NY))

    def apply_band(single_band):
        waves_grid = single_band.reshape(2, P_SIZE, NX, NY)
        half_done = combine(product_f32('cpxy,tyk->ctpxk', waves_grid, table_cols), 1.0).astype(jnp.bfloat16)
        in_space = combine(product_f32('cpxy,txk->ctypk', half_done, table_rows), 1.0)
        weighted = (potential * in_space).astype(jnp.bfloat16)
        return_half = combine(product_f32('cypx,txk->ctpyk', weighted, table_rows), -1.0).astype(jnp.bfloat16)
        recip_part = combine(product_f32('cpyx,tyk->ctpxk', return_half, table_cols), -1.0)
        applied = (kinetic * waves_grid.astype(jnp.float32) + recip_part).astype(jnp.bfloat16)
        return applied.reshape(2, P_SIZE, NX * NY)
    applied_waves = jnp.moveaxis(lax.map(apply_band, jnp.moveaxis(waves, 1, 0)), 0, 1)
    products = product_f32('cnpg,dmpg->cdnm', waves, applied_waves)
    inverse_cells = 1.0 / (P_SIZE * NX * NY)
    subspace = jnp.stack([products[0, 0] + products[1, 1], products[0, 1] - products[1, 0]]) * inverse_cells
    return (applied_waves, subspace)
```

```python
import functools

import jax
import jax.numpy as jnp
from jax import lax
from jax.experimental import pallas as pl
from jax.experimental.pallas import tpu as pltpu
from jax.sharding import PartitionSpec as P

NX = 384
NY = 384
LANES = 128

width_cells = 1.5


def tables(length):
    indices = jnp.arange(length, dtype=jnp.int32)
    phases = indices[:, None] * indices[None, :] % length
    angles = phases.astype(jnp.float32) * (2.0 * jnp.pi / length)
    factor = 1.0 / jnp.sqrt(jnp.float32(length))
    return (
        (jnp.cos(angles) * factor).astype(jnp.bfloat16),
        (jnp.sin(angles) * factor).astype(jnp.bfloat16),
    )


def gaussian(distance):
    return jnp.exp(-distance * distance / (2.0 * width_cells * width_cells))


def frequency(indices, length):
    return jnp.where(indices < length // 2, indices, indices - length).astype(jnp.float32)


def dot(left, right):
    return jnp.dot(left, right, preferred_element_type=jnp.float32)


def lasting(microseconds):
    return pl.CostEstimate(
        flops=0, bytes_accessed=int(microseconds * 3.69e6), transcendentals=0
    )


def pack_body(place, *refs):
    halves = len(refs) - 1 - refs[-1].shape[0]
    sources, messages, held = refs[:halves], refs[halves:-1], refs[-1]
    groups, count, rows, _ = held.shape
    planes = groups // halves
    for h, source in enumerate(sources):
        for i in range(count):
            split = source[0, i].reshape(planes, rows, NY)
            for p in range(planes):
                held[p * halves + h, i] = split[p]
    for s, message in enumerate(messages):
        message[0] = held[lax.rem(place[0] + s, groups)]


def pack(waves, place, first, count, rows, groups):
    planes = waves.shape[2]
    halves = groups // planes
    own = waves.shape[1] // halves
    return pl.pallas_call(
        pack_body,
        grid=(2, count),
        in_specs=[pl.BlockSpec(memory_space=pltpu.SMEM)]
        + [
            pl.BlockSpec((1, 1, planes, rows * NY), functools.partial(block_at, h * own + first))
            for h in range(halves)
        ],
        out_specs=[pl.BlockSpec((1, 1, rows, NY), lambda c, n: (c, n, 0, 0))] * groups,
        out_shape=[jax.ShapeDtypeStruct((2, count, rows, NY), jnp.bfloat16)] * groups,
        scratch_shapes=[pltpu.VMEM((groups, 1, rows, NY), jnp.bfloat16)],
        compiler_params=pltpu.CompilerParams(vmem_limit_bytes=56 << 20),
        cost_estimate=lasting(1.0 * count),
        name="pack_planes",
    )(place, *[waves] * halves)


def block_at(base, c, n):
    return (c, base + n, 0, 0)


def mix_waves_body(w_ref, z_ref, mixed):
    _, bands, planes, width = w_ref.shape
    rows = width // NY
    per = 2 * bands
    for c in range(2):
        for n in range(bands):
            wide = w_ref[c, n].reshape(planes, rows, NY).astype(jnp.float32)
            for p in range(planes):
                at = pl.ds(p * rows * per + c * bands + n, rows, stride=per)
                for t in range(NY // LANES):
                    mixed[t, at, :] = wide[p, :, t * LANES : (t + 1) * LANES]
    for t in range(NY // LANES):
        z_ref[0, :, t * LANES : (t + 1) * LANES] = mixed[t].astype(jnp.bfloat16)


def mix_waves(waves, rows, shares):
    _, bands, planes, _ = waves.shape
    own = rows // shares
    depth = planes * own * 2 * bands
    return pl.pallas_call(
        mix_waves_body,
        grid=(shares,),
        in_specs=[pl.BlockSpec((2, bands, planes, own * NY), lambda d: (0, 0, 0, d))],
        out_specs=pl.BlockSpec((1, depth, NY), lambda d: (d, 0, 0)),
        out_shape=jax.ShapeDtypeStruct((shares, depth, NY), jnp.bfloat16),
        scratch_shapes=[pltpu.VMEM((NY // LANES, depth, LANES), jnp.float32)],
        compiler_params=pltpu.CompilerParams(vmem_limit_bytes=56 << 20),
        cost_estimate=lasting(8.0),
        name="mix_waves",
    )(waves)


def mix_space_body(*refs):
    sources, z_ref, mixed = refs[:-2], refs[-2], refs[-1]
    bands = sum(source.shape[0] for source in sources)
    rows = sources[0].shape[2]
    for c in range(2):
        row = c * bands
        for source in sources:
            for n in range(source.shape[0]):
                wide = source[n, c].astype(jnp.float32)
                for t in range(NY // LANES):
                    mixed[t, pl.ds(row, rows, stride=2 * bands), :] = wide[
                        :, t * LANES : (t + 1) * LANES
                    ]
                row += 1
    for t in range(NY // LANES):
        z_ref[:, :, t * LANES : (t + 1) * LANES] = (
            mixed[t].astype(jnp.bfloat16).reshape(z_ref.shape[:2] + (LANES,))
        )


def mix_space(sources, shares):
    bands = sum(source.shape[0] for source in sources)
    own = NX // shares
    depth = own * 2 * bands
    group = max(1, 48 // own)
    return pl.pallas_call(
        mix_space_body,
        grid=(shares // group,),
        in_specs=[
            pl.BlockSpec((source.shape[0], 2, group * own, NY), lambda d: (0, 0, d, 0))
            for source in sources
        ],
        out_specs=pl.BlockSpec((group, depth, NY), lambda d: (d, 0, 0)),
        out_shape=jax.ShapeDtypeStruct((shares, depth, NY), jnp.bfloat16),
        scratch_shapes=[pltpu.VMEM((NY // LANES, group * depth, LANES), jnp.float32)],
        compiler_params=pltpu.CompilerParams(vmem_limit_bytes=56 << 20),
        cost_estimate=lasting(8.0),
        name="mix_space",
    )(*sources)


def unpack_body(groups, place, *refs):
    messages, o_ref, held = refs[:groups], refs[-2], refs[-1]
    halves, planes, count, rows, _ = held.shape
    for s, message in enumerate(messages):
        source = lax.rem(place[0] + groups - s, groups)
        held[lax.rem(source, halves), source // halves] = message[0]
    half = pl.program_id(1)
    for i in range(count):
        o_ref[0, i] = held[half, :, i].reshape(planes, rows * NY)


def unpack(messages, place, base, first, bands, planes):
    groups = len(messages)
    _, count, rows, _ = messages[0].shape
    halves = groups // planes
    own = bands // halves
    in_specs = [pl.BlockSpec(memory_space=pltpu.SMEM)] + [
        pl.BlockSpec((1, 1, rows, NY), lambda c, h, n: (c, n, 0, 0))
    ] * groups
    operands = [place, *messages]
    aliases = {}
    if base is not None:
        in_specs.append(pl.BlockSpec(memory_space=pl.ANY))
        operands.append(base)
        aliases = {groups + 1: 0}
    return pl.pallas_call(
        functools.partial(unpack_body, groups),
        grid=(2, halves, count),
        in_specs=in_specs,
        out_specs=pl.BlockSpec(
            (1, 1, planes, rows * NY), lambda c, h, n: (c, h * own + first + n, 0, 0)
        ),
        out_shape=jax.ShapeDtypeStruct((2, bands, planes, rows * NY), jnp.bfloat16),
        scratch_shapes=[pltpu.VMEM((halves, planes, 1, rows, NY), jnp.bfloat16)],
        input_output_aliases=aliases,
        compiler_params=pltpu.CompilerParams(vmem_limit_bytes=56 << 20),
        cost_estimate=lasting(1.2 * count),
        name="unpack_planes",
    )(*operands)


def forward_body(groups, place, *refs):
    messages, (f_ref, b_ref, s_ref, held) = refs[:groups], refs[groups:]
    for s, message in enumerate(messages):
        held[lax.rem(place[0] + groups - s, groups)] = message[:, 0]
    parts = [held[:, c].reshape(NX, NY) for c in range(2)]
    first = dot(jnp.concatenate(parts, axis=1), f_ref[...]).astype(jnp.bfloat16)
    first = jnp.concatenate([first[:, :NY], first[:, NY:]], axis=0)
    in_space = dot(b_ref[...], first).astype(jnp.bfloat16)
    s_ref[0, 0] = in_space[:NX]
    s_ref[0, 1] = in_space[NX:]


def forward(messages, place, forth, back):
    groups = len(messages)
    _, bands, rows, _ = messages[0].shape
    square = pl.BlockSpec((2 * NX, 2 * NX), lambda n: (0, 0))
    return pl.pallas_call(
        functools.partial(forward_body, groups),
        grid=(bands,),
        in_specs=[pl.BlockSpec(memory_space=pltpu.SMEM)]
        + [pl.BlockSpec((2, 1, rows, NY), lambda n: (0, n, 0, 0))] * groups
        + [square, square],
        out_specs=pl.BlockSpec((1, 2, NX, NY), lambda n: (n, 0, 0, 0)),
        out_shape=jax.ShapeDtypeStruct((bands, 2, NX, NY), jnp.bfloat16),
        scratch_shapes=[pltpu.VMEM((groups, 2, rows, NY), jnp.bfloat16)],
        compiler_params=pltpu.CompilerParams(vmem_limit_bytes=56 << 20),
        cost_estimate=lasting(1.5 * bands + 1.0),
        name="forward",
    )(place, *messages, forth, back)


def inverse_body(groups, place, *refs):
    messages, (s_ref, v_ref, f_ref, b_ref) = refs[:groups], refs[groups : groups + 4]
    held = refs[-1]
    results = refs[-1 - groups : -1]
    rows = held.shape[2]
    freq_x = frequency(lax.broadcasted_iota(jnp.int32, (NX, 1), 0), NX)
    freq_y = frequency(lax.broadcasted_iota(jnp.int32, (1, NY), 1), NY)
    kinetic = 2.0 * (freq_x * freq_x / (NX * NX) + freq_y * freq_y / (NY * NY))
    for s, message in enumerate(messages):
        held[lax.rem(place[0] + groups - s, groups)] = message[:, 0]
    weighted = jnp.concatenate(
        [v_ref[...] * s_ref[0, c].astype(jnp.float32) for c in range(2)],
        axis=0,
    ).astype(jnp.bfloat16)
    back = dot(f_ref[...], weighted).astype(jnp.bfloat16)
    recip = dot(jnp.concatenate([back[:NX], back[NX:]], axis=1), b_ref[...])
    for c in range(2):
        wide = held[:, c].reshape(NX, NY).astype(jnp.float32)
        applied = kinetic * wide + recip[:, c * NY : (c + 1) * NY]
        held[:, c] = applied.astype(jnp.bfloat16).reshape(groups, rows, NY)
    for s, result in enumerate(results):
        result[:, 0] = held[lax.rem(place[0] + s, groups)]


def inverse(messages, place, in_space, potential, forth, back):
    groups = len(messages)
    shape = messages[0].shape
    _, bands, rows, _ = shape
    square = pl.BlockSpec((2 * NX, 2 * NX), lambda n: (0, 0))
    return pl.pallas_call(
        functools.partial(inverse_body, groups),
        grid=(bands,),
        in_specs=[pl.BlockSpec(memory_space=pltpu.SMEM)]
        + [pl.BlockSpec((2, 1, rows, NY), lambda n: (0, n, 0, 0))] * groups
        + [
            pl.BlockSpec((1, 2, NX, NY), lambda n: (n, 0, 0, 0)),
            pl.BlockSpec((NX, NY), lambda n: (0, 0)),
            square,
            square,
        ],
        out_specs=[pl.BlockSpec((2, 1, rows, NY), lambda n: (0, n, 0, 0))] * groups,
        out_shape=[jax.ShapeDtypeStruct(shape, jnp.bfloat16)] * groups,
        scratch_shapes=[pltpu.VMEM((groups, 2, rows, NY), jnp.bfloat16)],
        compiler_params=pltpu.CompilerParams(vmem_limit_bytes=56 << 20),
        cost_estimate=lasting(1.8 * bands + 1.0),
        name="inverse",
    )(place, *messages, in_space, potential, forth, back)


def overlap_body(scale, per, z_ref, w_ref, *refs):
    g_ref, total = refs[-2:]
    shares = z_ref.shape[0]
    if len(refs) == 3:
        total[...] = refs[0][...]
    else:
        total[...] = jnp.zeros_like(total)

    @pl.loop(0, w_ref.shape[0] // 2)
    def _(pair):
        plain, scaled = [], []
        for k in range(2):
            point = pair * 2 + k
            at = pl.multiple_of(point * per, per)
            rows = jnp.concatenate([z_ref[d, pl.ds(at, per), :] for d in range(shares)], axis=0)
            plain.append(rows)
            scaled.append(
                (rows.astype(jnp.float32) * w_ref[pl.ds(point, 1), :]).astype(jnp.bfloat16)
            )
        total[...] += lax.dot_general(
            jnp.concatenate(plain, axis=1),
            jnp.concatenate(scaled, axis=1),
            (((1,), (1,)), ((), ())),
            preferred_element_type=jnp.float32,
        )

    if len(refs) == 2:
        g_ref[...] = total[...]
        return
    half = per // 2

    def picked(rows, c):
        return jnp.concatenate(
            [rows[d * per + c * half : d * per + (c + 1) * half] for d in range(shares)], axis=0
        )

    grams = total[...]
    parts = [[picked(picked(grams, c).T, d) for d in range(2)] for c in range(2)]
    g_ref[0] = (parts[0][0] + parts[1][1]).T * scale
    g_ref[1] = (parts[0][1] - parts[1][0]).T * scale


def overlap(pieces, weights, per, scale, before=None):
    shares = pieces.shape[0]
    size = shares * per
    whole = pl.BlockSpec(memory_space=pltpu.VMEM)
    last = before is not None
    shape = (2, size // 2, size // 2) if last else (size, size)
    operands = [pieces, weights] + ([before] if last else [])
    return pl.pallas_call(
        functools.partial(overlap_body, scale, per),
        in_specs=[whole] * len(operands),
        out_specs=whole,
        out_shape=jax.ShapeDtypeStruct(shape, jnp.float32),
        scratch_shapes=[pltpu.VMEM((size, size), jnp.float32)],
        compiler_params=pltpu.CompilerParams(vmem_limit_bytes=56 << 20),
        cost_estimate=lasting(8.0),
        name="overlap",
    )(*operands)


def shifted(messages):
    groups = len(messages)
    return [
        lax.ppermute(message, "ga", [(i, (i + s) % groups) for i in range(groups)]) if s else message
        for s, message in enumerate(messages)
    ]


def split(wide):
    high = wide.astype(jnp.bfloat16)
    return high, (wide - high.astype(jnp.float32)).astype(jnp.bfloat16)


def charges_body(planes, slab_rows, place, c_ref, i_ref, o_ref):
    share = o_ref.shape[0]
    first = place[0].astype(jnp.float32)
    plane = place[1].astype(jnp.float32)
    own_x = lax.broadcasted_iota(jnp.int32, (share, 1), 0).astype(jnp.float32) + first
    cells_y = lax.broadcasted_iota(jnp.int32, (NY, 1), 0)
    slab_y = (cells_y // slab_rows).astype(jnp.float32)
    cells_y = cells_y.astype(jnp.float32)
    o_ref[...] = i_ref[...]

    @pl.loop(0, c_ref.shape[0])
    def _(device):
        along_u, along_v, along_w, amount, slab = [c_ref[device, k : k + 1, :] for k in range(5)]
        kernel_x = gaussian(own_x - NX * along_u) * (amount * gaussian(plane - planes * along_w))
        kernel_y = gaussian(cells_y - (slab * slab_rows + slab_rows * along_v))
        kernel_y = jnp.where(slab_y == slab, kernel_y, 0.0)
        (x_high, x_low), (y_high, y_low) = split(kernel_x), split(kernel_y)
        total = o_ref[...]
        for left, right in ((x_high, y_low), (x_low, y_high), (x_high, y_high)):
            total = total + lax.dot_general(
                left, right, (((1,), (1,)), ((), ())), preferred_element_type=jnp.float32
            )
        o_ref[...] = total


def potential_message(ionic_field, point_charge, charge_place, charge_slab, planes, halves):
    ga_count = lax.axis_size("ga")
    band_groups = lax.axis_size("band")
    devices = band_groups * ga_count
    slab_rows = NY // ga_count
    share = NX // band_groups
    piece = share * slab_rows // band_groups
    atoms = point_charge.shape[0]
    spare = -(-piece // atoms)
    band_at = lax.axis_index("band")
    charges = jnp.concatenate(
        [charge_place, point_charge[None], charge_slab[:, 0][None].astype(jnp.float32)], axis=0
    )
    ionic = ionic_field.T.reshape(planes, band_groups, band_groups, piece)
    ionic = lax.dynamic_index_in_dim(ionic, band_at, 2, keepdims=False)
    ionic = jnp.broadcast_to(
        ionic.transpose(1, 0, 2)[:, :, None], (band_groups, planes, halves, piece)
    )
    ionic = jnp.pad(ionic.reshape(devices, piece), ((0, 0), (0, spare * atoms - piece)))
    return jnp.concatenate(
        [
            jnp.broadcast_to(charges[None], (devices, 5, atoms)),
            ionic.reshape(devices, spare, atoms),
        ],
        axis=1,
    )


def own_share(message, planes, halves):
    ga_count = lax.axis_size("ga")
    band_groups = lax.axis_size("band")
    slab_rows = NY // ga_count
    share = NX // band_groups
    piece = share * slab_rows // band_groups
    atoms = message.shape[2]
    spare = message.shape[1] - 5
    band_at = lax.axis_index("band")
    ionic = message[:, 5:].reshape(band_groups, ga_count, spare * atoms)[:, :, :piece]
    ionic = ionic.transpose(1, 0, 2).reshape(ga_count, share, slab_rows)
    ionic = ionic.transpose(1, 0, 2).reshape(share, NY)
    place = jnp.stack([band_at * share, lax.axis_index("ga") // halves]).astype(jnp.int32)
    return pl.pallas_call(
        functools.partial(charges_body, planes, slab_rows),
        in_specs=[
            pl.BlockSpec(memory_space=pltpu.SMEM),
            pl.BlockSpec(memory_space=pltpu.VMEM),
            pl.BlockSpec(memory_space=pltpu.VMEM),
        ],
        out_specs=pl.BlockSpec(memory_space=pltpu.VMEM),
        out_shape=jax.ShapeDtypeStruct((share, NY), jnp.float32),
        compiler_params=pltpu.CompilerParams(vmem_limit_bytes=56 << 20),
        cost_estimate=lasting(12.0),
        name="charge_potential",
    )(place, message, ionic)


def shards(waves, ionic_field, point_charge, charge_place, charge_slab):
    ga_count = lax.axis_size("ga")
    band_groups = lax.axis_size("band")
    bands = waves.shape[1]
    planes = waves.shape[2]
    rows = NX // ga_count
    halves = ga_count // planes
    own_bands = bands // halves
    chunks = [(0, 2), (2, own_bands - 3), (own_bands - 1, 1)]
    per = 2 * bands
    pairs = [[p * halves + h for h in range(halves)] for p in range(planes)]
    ga_at, band_at = lax.axis_index("ga"), lax.axis_index("band")
    place = ga_at.astype(jnp.int32)[None]

    packed = [pack(waves, place, first, count, rows, ga_count) for first, count in chunks]
    message = potential_message(
        ionic_field, point_charge, charge_place, charge_slab, planes, halves
    )
    cosine, sine = tables(NX)
    forth = jnp.concatenate(
        [jnp.concatenate([cosine, sine], axis=1), jnp.concatenate([-sine, cosine], axis=1)], axis=0
    )
    back = jnp.concatenate(
        [jnp.concatenate([cosine, -sine], axis=1), jnp.concatenate([sine, cosine], axis=1)], axis=0
    )

    arrived = [shifted(packed[0])]
    message = lax.all_to_all(message, ("band", "ga"), 0, 0, tiled=True)
    mixed = mix_waves(waves, rows, band_groups)
    arrived[0], message, packed[1], mixed = lax.optimization_barrier(
        (arrived[0], message, packed[1], mixed)
    )

    arrived.append(shifted(packed[1]))
    met_waves = lax.all_to_all(mixed, "band", 0, 0, tiled=True)
    own_potential = own_share(message, planes, halves)
    copies = jnp.broadcast_to(own_potential[None], (band_groups,) + own_potential.shape)
    in_space = [forward(arrived[0], place, forth, back)]
    arrived[1], met_waves, packed[2], copies, in_space[0], forth, back = (
        lax.optimization_barrier(
            (arrived[1], met_waves, packed[2], copies, in_space[0], forth, back)
        )
    )

    arrived.append(shifted(packed[2]))
    potential = lax.all_to_all(copies, "band", 0, 0, tiled=True).reshape(NX, NY)
    in_space.append(forward(arrived[1], place, forth, back))
    applied = []
    for j in range(2):
        result = inverse(arrived[j], place, in_space[j], potential, forth, back)
        result, place = lax.optimization_barrier((result, place))
        applied.append(result)
    returned = [shifted(result) for result in applied]
    in_space.append(forward(arrived[2], place, forth, back))
    mixed = mix_space(in_space, band_groups * halves)
    mixed = mixed.reshape(band_groups, halves, -1, NY)
    if halves > 1:
        mixed = lax.all_to_all(mixed, "ga", 1, 1, axis_index_groups=pairs, tiled=True)
    met_space = lax.all_to_all(mixed, "band", 0, 0, tiled=True)
    if halves > 1:
        met_space = met_space.reshape(band_groups, halves, -1, 2, own_bands, NY)
        met_space = met_space.transpose(0, 2, 3, 1, 4, 5)
    met_space = met_space.reshape(band_groups, -1, NY)
    space_weights = own_potential
    if halves > 1:
        space_weights = lax.dynamic_slice_in_dim(
            own_potential, ga_at % halves * (NX // band_groups // halves),
            NX // band_groups // halves, 0,
        )

    share = rows // band_groups
    own_x = ga_at * rows + band_at * share + jnp.arange(share, dtype=jnp.int32)
    freq_x, freq_y = frequency(own_x, NX), frequency(jnp.arange(NY, dtype=jnp.int32), NY)
    kinetic = 2.0 * (
        freq_x[:, None] * freq_x[:, None] / (NX * NX)
        + freq_y[None, :] * freq_y[None, :] / (NY * NY)
    )
    kinetic = jnp.broadcast_to(kinetic[None], (planes, share, NY)).reshape(planes * share, NY)

    scale = 1.0 / (planes * NX * NY)
    grams = overlap(met_waves, kinetic, per, scale)
    grams, place = lax.optimization_barrier((grams, place))
    returned.append(shifted(inverse(arrived[2], place, in_space[2], potential, forth, back)))
    full_matrix = overlap(met_space, space_weights, per, scale, grams)
    all_bands = bands * band_groups
    col_width = all_bands // ga_count
    blocks = full_matrix.reshape(2, band_groups, bands, ga_count, col_width)
    blocks = blocks.transpose(1, 3, 0, 2, 4).reshape(
        band_groups * ga_count, 2, bands, col_width
    )
    subspace = lax.all_to_all(blocks, ("band", "ga"), 0, 0, tiled=True).sum(0)

    applied_waves = None
    for j, (first, _) in enumerate(chunks):
        if j == 2:
            place, subspace = lax.optimization_barrier((place, subspace))
        applied_waves = unpack(returned[j], place, applied_waves, first, bands, planes)
    return (applied_waves, subspace)


def solution(mesh):
    placed = (
        P(None, "band", None, "ga"),
        P("ga", None),
        P(("band", "ga")),
        P(None, ("band", "ga")),
        P(("band", "ga"), None),
    )
    return jax.shard_map(
        shards,
        mesh=mesh,
        in_specs=placed,
        out_specs=(P(None, "band", None, "ga"), P(None, "band", "ga")),
        check_vma=False,
    )
```

```python
import functools

import jax
import jax.numpy as jnp
from jax import lax
from jax.experimental import pallas as pl
from jax.experimental.pallas import tpu as pltpu
from jax.sharding import PartitionSpec as P

NX = 384
NY = 384
LANES = 128
STEP = 2

width_cells = 1.5


def tables(indices):
    length = indices.shape[0]
    phases = indices[:, None] * indices[None, :] % length
    angles = phases.astype(jnp.float32) * (2.0 * jnp.pi / length)
    factor = 1.0 / jnp.sqrt(jnp.float32(length))
    return (
        (jnp.cos(angles) * factor).astype(jnp.bfloat16),
        (jnp.sin(angles) * factor).astype(jnp.bfloat16),
    )


def gaussian(distance):
    return jnp.exp(-distance * distance / (2.0 * width_cells * width_cells))


def frequency(indices, length):
    return jnp.where(indices < length // 2, indices, indices - length).astype(jnp.float32)


def dot(left, right):
    return jnp.dot(left, right, preferred_element_type=jnp.float32)


def lasting(microseconds):
    return pl.CostEstimate(
        flops=0, bytes_accessed=int(microseconds * 3.69e6), transcendentals=0
    )


def pack_body(place, *refs):
    halves = len(refs) - 1 - refs[-1].shape[0]
    sources, messages, held = refs[:halves], refs[halves:-1], refs[-1]
    groups, count, rows, _ = held.shape
    planes = groups // halves
    for h, source in enumerate(sources):
        for i in range(count):
            split = source[0, i].reshape(planes, rows, NY)
            for p in range(planes):
                held[p * halves + h, i] = split[p]
    for s, message in enumerate(messages):
        message[0] = held[lax.rem(place[0] + s, groups)]


def pack(waves, place, first, count, rows, groups):
    planes = waves.shape[2]
    halves = groups // planes
    own = waves.shape[1] // halves
    return pl.pallas_call(
        pack_body,
        grid=(2, count // STEP),
        in_specs=[pl.BlockSpec(memory_space=pltpu.SMEM)]
        + [
            pl.BlockSpec(
                (1, STEP, planes, rows * NY),
                functools.partial(block_at, (h * own + first) // STEP),
            )
            for h in range(halves)
        ],
        out_specs=[pl.BlockSpec((1, STEP, rows, NY), lambda c, n: (c, n, 0, 0))] * groups,
        out_shape=[jax.ShapeDtypeStruct((2, count, rows, NY), jnp.bfloat16)] * groups,
        scratch_shapes=[pltpu.VMEM((groups, STEP, rows, NY), jnp.bfloat16)],
        compiler_params=pltpu.CompilerParams(vmem_limit_bytes=56 << 20),
        cost_estimate=lasting(0.01),
        name="pack_planes",
    )(place, *[waves] * halves)


def block_at(base, c, n):
    return (c, base + n, 0, 0)


def mix_waves_body(w_ref, z_ref, mixed):
    _, bands, planes, width = w_ref.shape
    rows = width // NY
    per = 2 * bands
    for c in range(2):
        for n in range(bands):
            wide = w_ref[c, n].reshape(planes, rows, NY).astype(jnp.float32)
            for p in range(planes):
                at = pl.ds(p * rows * per + c * bands + n, rows, stride=per)
                for t in range(NY // LANES):
                    mixed[t, at, :] = wide[p, :, t * LANES : (t + 1) * LANES]
    for t in range(NY // LANES):
        z_ref[0, :, t * LANES : (t + 1) * LANES] = mixed[t].astype(jnp.bfloat16)


def mix_waves(waves, rows, shares):
    _, bands, planes, _ = waves.shape
    own = rows // shares
    depth = planes * own * 2 * bands
    return pl.pallas_call(
        mix_waves_body,
        grid=(shares,),
        in_specs=[pl.BlockSpec((2, bands, planes, own * NY), lambda d: (0, 0, 0, d))],
        out_specs=pl.BlockSpec((1, depth, NY), lambda d: (d, 0, 0)),
        out_shape=jax.ShapeDtypeStruct((shares, depth, NY), jnp.bfloat16),
        scratch_shapes=[pltpu.VMEM((NY // LANES, depth, LANES), jnp.float32)],
        compiler_params=pltpu.CompilerParams(vmem_limit_bytes=56 << 20),
        cost_estimate=lasting(0.01),
        name="mix_waves",
    )(waves)


def mix_space_body(*refs):
    sources, z_ref, mixed = refs[:-2], refs[-2], refs[-1]
    bands = sum(source.shape[0] for source in sources)
    rows = sources[0].shape[2]
    for c in range(2):
        row = c * bands
        for source in sources:
            for n in range(source.shape[0]):
                wide = source[n, c].astype(jnp.float32)
                for t in range(NY // LANES):
                    mixed[t, pl.ds(row, rows, stride=2 * bands), :] = wide[
                        :, t * LANES : (t + 1) * LANES
                    ]
                row += 1
    for t in range(NY // LANES):
        z_ref[:, :, t * LANES : (t + 1) * LANES] = (
            mixed[t].astype(jnp.bfloat16).reshape(z_ref.shape[:2] + (LANES,))
        )


def mix_space(sources, shares):
    bands = sum(source.shape[0] for source in sources)
    own = NX // shares
    depth = own * 2 * bands
    group = max(1, 48 // own)
    return pl.pallas_call(
        mix_space_body,
        grid=(shares // group,),
        in_specs=[
            pl.BlockSpec((source.shape[0], 2, group * own, NY), lambda d: (0, 0, d, 0))
            for source in sources
        ],
        out_specs=pl.BlockSpec((group, depth, NY), lambda d: (d, 0, 0)),
        out_shape=jax.ShapeDtypeStruct((shares, depth, NY), jnp.bfloat16),
        scratch_shapes=[pltpu.VMEM((NY // LANES, group * depth, LANES), jnp.float32)],
        compiler_params=pltpu.CompilerParams(vmem_limit_bytes=56 << 20),
        cost_estimate=lasting(0.01),
        name="mix_space",
    )(*sources)


def unpack_body(groups, place, *refs):
    messages, o_ref, held = refs[:groups], refs[-2], refs[-1]
    halves, planes, count, rows, _ = held.shape
    for s, message in enumerate(messages):
        source = lax.rem(place[0] + groups - s, groups)
        held[lax.rem(source, halves), source // halves] = message[0]
    half = pl.program_id(1)
    for i in range(count):
        o_ref[0, i] = held[half, :, i].reshape(planes, rows * NY)


def unpack(messages, place, base, first, bands, planes):
    groups = len(messages)
    _, count, rows, _ = messages[0].shape
    halves = groups // planes
    own = bands // halves
    in_specs = [pl.BlockSpec(memory_space=pltpu.SMEM)] + [
        pl.BlockSpec((1, 1, rows, NY), lambda c, h, n: (c, n, 0, 0))
    ] * groups
    operands = [place, *messages]
    aliases = {}
    if base is not None:
        in_specs.append(pl.BlockSpec(memory_space=pl.ANY))
        operands.append(base)
        aliases = {groups + 1: 0}
    return pl.pallas_call(
        functools.partial(unpack_body, groups),
        grid=(2, halves, count),
        in_specs=in_specs,
        out_specs=pl.BlockSpec(
            (1, 1, planes, rows * NY), lambda c, h, n: (c, h * own + first + n, 0, 0)
        ),
        out_shape=jax.ShapeDtypeStruct((2, bands, planes, rows * NY), jnp.bfloat16),
        scratch_shapes=[pltpu.VMEM((halves, planes, 1, rows, NY), jnp.bfloat16)],
        input_output_aliases=aliases,
        compiler_params=pltpu.CompilerParams(vmem_limit_bytes=56 << 20),
        cost_estimate=lasting(1.2 * count),
        name="unpack_planes",
    )(*operands)


def forward_body(groups, place, *refs):
    messages, (f_ref, b_ref, s_ref, held) = refs[:groups], refs[groups:]
    for s, message in enumerate(messages):
        held[lax.rem(place[0] + groups - s, groups)] = message[:, 0]
    parts = [held[:, c].reshape(NX, NY) for c in range(2)]
    first = dot(jnp.concatenate(parts, axis=1), f_ref[...]).astype(jnp.bfloat16)
    first = jnp.concatenate([first[:, :NY], first[:, NY:]], axis=0)
    in_space = dot(b_ref[...], first).astype(jnp.bfloat16)
    s_ref[0, 0] = in_space[:NX]
    s_ref[0, 1] = in_space[NX:]


def forward(messages, place, forth, back):
    groups = len(messages)
    _, bands, rows, _ = messages[0].shape
    square = pl.BlockSpec((2 * NX, 2 * NX), lambda n: (0, 0))
    return pl.pallas_call(
        functools.partial(forward_body, groups),
        grid=(bands,),
        in_specs=[pl.BlockSpec(memory_space=pltpu.SMEM)]
        + [pl.BlockSpec((2, 1, rows, NY), lambda n: (0, n, 0, 0))] * groups
        + [square, square],
        out_specs=pl.BlockSpec((1, 2, NX, NY), lambda n: (n, 0, 0, 0)),
        out_shape=jax.ShapeDtypeStruct((bands, 2, NX, NY), jnp.bfloat16),
        scratch_shapes=[pltpu.VMEM((groups, 2, rows, NY), jnp.bfloat16)],
        compiler_params=pltpu.CompilerParams(vmem_limit_bytes=56 << 20),
        cost_estimate=lasting(0.01),
        name="forward",
    )(place, *messages, forth, back)


def inverse_body(groups, place, *refs):
    messages, (s_ref, v_ref, f_ref, b_ref) = refs[:groups], refs[groups : groups + 4]
    held = refs[-1]
    results = refs[-1 - groups : -1]
    rows = held.shape[2]
    freq_x = frequency(lax.broadcasted_iota(jnp.int32, (NX, 1), 0), NX)
    freq_y = frequency(lax.broadcasted_iota(jnp.int32, (1, NY), 1), NY)
    kinetic = 2.0 * (freq_x * freq_x / (NX * NX) + freq_y * freq_y / (NY * NY))
    for s, message in enumerate(messages):
        held[lax.rem(place[0] + groups - s, groups)] = message[:, 0]
    weighted = jnp.concatenate(
        [v_ref[...] * s_ref[0, c].astype(jnp.float32) for c in range(2)],
        axis=0,
    ).astype(jnp.bfloat16)
    back = dot(f_ref[...], weighted).astype(jnp.bfloat16)
    recip = dot(jnp.concatenate([back[:NX], back[NX:]], axis=1), b_ref[...])
    for c in range(2):
        wide = held[:, c].reshape(NX, NY).astype(jnp.float32)
        applied = kinetic * wide + recip[:, c * NY : (c + 1) * NY]
        held[:, c] = applied.astype(jnp.bfloat16).reshape(groups, rows, NY)
    for s, result in enumerate(results):
        result[:, 0] = held[lax.rem(place[0] + s, groups)]


def inverse(messages, base, bands, place, in_space, potential, forth, back):
    groups = len(messages)
    rows = messages[0].shape[2]
    shape = (2, bands, rows, NY)
    square = pl.BlockSpec((2 * NX, 2 * NX), lambda n: (0, 0))
    return pl.pallas_call(
        functools.partial(inverse_body, groups),
        grid=(bands,),
        in_specs=[pl.BlockSpec(memory_space=pltpu.SMEM)]
        + [pl.BlockSpec((2, 1, rows, NY), lambda n: (0, base + n, 0, 0))] * groups
        + [
            pl.BlockSpec((1, 2, NX, NY), lambda n: (base + n, 0, 0, 0)),
            pl.BlockSpec((NX, NY), lambda n: (0, 0)),
            square,
            square,
        ],
        out_specs=[pl.BlockSpec((2, 1, rows, NY), lambda n: (0, n, 0, 0))] * groups,
        out_shape=[jax.ShapeDtypeStruct(shape, jnp.bfloat16)] * groups,
        scratch_shapes=[pltpu.VMEM((groups, 2, rows, NY), jnp.bfloat16)],
        compiler_params=pltpu.CompilerParams(vmem_limit_bytes=56 << 20),
        cost_estimate=lasting(0.01),
        name="inverse",
    )(place, *messages, in_space, potential, forth, back)


def overlap_body(scale, per, z_ref, w_ref, *refs):
    g_ref, total = refs[-2:]
    shares = z_ref.shape[0]
    if len(refs) == 3:
        total[...] = refs[0][...]
    else:
        total[...] = jnp.zeros_like(total)

    @pl.loop(0, w_ref.shape[0] // 2)
    def _(pair):
        plain, scaled = [], []
        for k in range(2):
            point = pair * 2 + k
            at = pl.multiple_of(point * per, per)
            rows = jnp.concatenate([z_ref[d, pl.ds(at, per), :] for d in range(shares)], axis=0)
            plain.append(rows)
            scaled.append(
                (rows.astype(jnp.float32) * w_ref[pl.ds(point, 1), :]).astype(jnp.bfloat16)
            )
        total[...] += lax.dot_general(
            jnp.concatenate(plain, axis=1),
            jnp.concatenate(scaled, axis=1),
            (((1,), (1,)), ((), ())),
            preferred_element_type=jnp.float32,
        )

    if len(refs) == 2:
        g_ref[...] = total[...]
        return
    half = per // 2

    def picked(rows, c):
        return jnp.concatenate(
            [rows[d * per + c * half : d * per + (c + 1) * half] for d in range(shares)], axis=0
        )

    grams = total[...]
    parts = [[picked(picked(grams, c).T, d) for d in range(2)] for c in range(2)]
    g_ref[0] = (parts[0][0] + parts[1][1]).T * scale
    g_ref[1] = (parts[0][1] - parts[1][0]).T * scale


def overlap(pieces, weights, per, scale, before=None):
    shares = pieces.shape[0]
    size = shares * per
    whole = pl.BlockSpec(memory_space=pltpu.VMEM)
    last = before is not None
    shape = (2, size // 2, size // 2) if last else (size, size)
    operands = [pieces, weights] + ([before] if last else [])
    return pl.pallas_call(
        functools.partial(overlap_body, scale, per),
        in_specs=[whole] * len(operands),
        out_specs=whole,
        out_shape=jax.ShapeDtypeStruct(shape, jnp.float32),
        scratch_shapes=[pltpu.VMEM((size, size), jnp.float32)],
        compiler_params=pltpu.CompilerParams(vmem_limit_bytes=56 << 20),
        cost_estimate=lasting(8.0),
        name="overlap",
    )(*operands)


def shifted(messages):
    groups = len(messages)
    return [
        lax.ppermute(message, "ga", [(i, (i + s) % groups) for i in range(groups)]) if s else message
        for s, message in enumerate(messages)
    ]


def split(wide):
    high = wide.astype(jnp.bfloat16)
    return high, (wide - high.astype(jnp.float32)).astype(jnp.bfloat16)


def charges_body(planes, slab_rows, place, c_ref, i_ref, o_ref):
    share = o_ref.shape[0]
    first = place[0].astype(jnp.float32)
    plane = place[1].astype(jnp.float32)
    own_x = lax.broadcasted_iota(jnp.int32, (share, 1), 0).astype(jnp.float32) + first
    cells_y = lax.broadcasted_iota(jnp.int32, (NY, 1), 0)
    slab_y = (cells_y // slab_rows).astype(jnp.float32)
    cells_y = cells_y.astype(jnp.float32)
    o_ref[...] = i_ref[...]

    @pl.loop(0, c_ref.shape[0])
    def _(device):
        along_u, along_v, along_w, amount, slab = [c_ref[device, k : k + 1, :] for k in range(5)]
        kernel_x = gaussian(own_x - NX * along_u) * (amount * gaussian(plane - planes * along_w))
        kernel_y = gaussian(cells_y - (slab * slab_rows + slab_rows * along_v))
        kernel_y = jnp.where(slab_y == slab, kernel_y, 0.0)
        (x_high, x_low), (y_high, y_low) = split(kernel_x), split(kernel_y)
        total = o_ref[...]
        for left, right in ((x_high, y_low), (x_low, y_high), (x_high, y_high)):
            total = total + lax.dot_general(
                left, right, (((1,), (1,)), ((), ())), preferred_element_type=jnp.float32
            )
        o_ref[...] = total


def potential_message(ionic_field, point_charge, charge_place, charge_slab, planes, halves):
    ga_count = lax.axis_size("ga")
    band_groups = lax.axis_size("band")
    devices = band_groups * ga_count
    slab_rows = NY // ga_count
    share = NX // band_groups
    piece = share * slab_rows // band_groups
    atoms = point_charge.shape[0]
    spare = -(-piece // atoms)
    band_at = lax.axis_index("band")
    charges = jnp.concatenate(
        [charge_place, point_charge[None], charge_slab[:, 0][None].astype(jnp.float32)], axis=0
    )
    ionic = ionic_field.T.reshape(planes, band_groups, band_groups, piece)
    ionic = lax.dynamic_index_in_dim(ionic, band_at, 2, keepdims=False)
    ionic = jnp.broadcast_to(
        ionic.transpose(1, 0, 2)[:, :, None], (band_groups, planes, halves, piece)
    )
    ionic = jnp.pad(ionic.reshape(devices, piece), ((0, 0), (0, spare * atoms - piece)))
    return jnp.concatenate(
        [
            jnp.broadcast_to(charges[None], (devices, 5, atoms)),
            ionic.reshape(devices, spare, atoms),
        ],
        axis=1,
    )


def own_share(message, planes, halves):
    ga_count = lax.axis_size("ga")
    band_groups = lax.axis_size("band")
    slab_rows = NY // ga_count
    share = NX // band_groups
    piece = share * slab_rows // band_groups
    atoms = message.shape[2]
    spare = message.shape[1] - 5
    band_at = lax.axis_index("band")
    ionic = message[:, 5:].reshape(band_groups, ga_count, spare * atoms)[:, :, :piece]
    ionic = ionic.transpose(1, 0, 2).reshape(ga_count, share, slab_rows)
    ionic = ionic.transpose(1, 0, 2).reshape(share, NY)
    place = jnp.stack([band_at * share, lax.axis_index("ga") // halves]).astype(jnp.int32)
    return pl.pallas_call(
        functools.partial(charges_body, planes, slab_rows),
        in_specs=[
            pl.BlockSpec(memory_space=pltpu.SMEM),
            pl.BlockSpec(memory_space=pltpu.VMEM),
            pl.BlockSpec(memory_space=pltpu.VMEM),
        ],
        out_specs=pl.BlockSpec(memory_space=pltpu.VMEM),
        out_shape=jax.ShapeDtypeStruct((share, NY), jnp.float32),
        compiler_params=pltpu.CompilerParams(vmem_limit_bytes=56 << 20),
        cost_estimate=lasting(0.01),
        name="charge_potential",
    )(place, message, ionic)


def shards(waves, ionic_field, point_charge, charge_place, charge_slab):
    ga_count = lax.axis_size("ga")
    band_groups = lax.axis_size("band")
    bands = waves.shape[1]
    planes = waves.shape[2]
    rows = NX // ga_count
    halves = ga_count // planes
    own_bands = bands // halves
    half = own_bands // 2
    chunks = [(0, half), (half, half)]
    per = 2 * bands
    pairs = [[p * halves + h for h in range(halves)] for p in range(planes)]
    ga_at, band_at = lax.axis_index("ga"), lax.axis_index("band")
    place = ga_at.astype(jnp.int32)[None]

    packed = [pack(waves, place, first, count, rows, ga_count) for first, count in chunks]
    message = potential_message(
        ionic_field, point_charge, charge_place, charge_slab, planes, halves
    )

    arrived = [shifted(packed[0])]
    message = lax.all_to_all(message, ("band", "ga"), 0, 0, tiled=True)
    own_potential = own_share(message, planes, halves)
    copies = jnp.broadcast_to(own_potential[None], (band_groups,) + own_potential.shape)
    potential = lax.all_to_all(copies, "band", 0, 0, tiled=True).reshape(NX, NY)
    mixed = mix_waves(waves, rows, band_groups)
    cells = jnp.arange(NX, dtype=jnp.int32)
    arrived[0], potential, packed[1], mixed, cells = lax.optimization_barrier(
        (arrived[0], potential, packed[1], mixed, cells)
    )

    arrived.append(shifted(packed[1]))
    met_waves = lax.all_to_all(mixed, "band", 0, 0, tiled=True)
    cosine, sine = tables(cells)
    forth = jnp.concatenate(
        [jnp.concatenate([cosine, sine], axis=1), jnp.concatenate([-sine, cosine], axis=1)], axis=0
    )
    back = jnp.concatenate(
        [jnp.concatenate([cosine, -sine], axis=1), jnp.concatenate([sine, cosine], axis=1)], axis=0
    )
    in_space = [forward(arrived[0], place, forth, back)]
    result = inverse(arrived[0], 0, half, place, in_space[0], potential, forth, back)
    arrived[1], met_waves, result = lax.optimization_barrier((arrived[1], met_waves, result))

    returned = [shifted(result)]
    in_space.append(forward(arrived[1], place, forth, back))
    mixed = mix_space(in_space, band_groups * halves)
    middle = ga_count // 2
    mixed, returned[0][middle] = lax.optimization_barrier((mixed, returned[0][middle]))
    mixed = mixed.reshape(band_groups, halves, -1, NY)
    if halves > 1:
        mixed = lax.all_to_all(mixed, "ga", 1, 1, axis_index_groups=pairs, tiled=True)
    met_space = lax.all_to_all(mixed, "band", 0, 0, tiled=True)
    if halves > 1:
        met_space = met_space.reshape(band_groups, halves, -1, 2, own_bands, NY)
        met_space = met_space.transpose(0, 2, 3, 1, 4, 5)
    met_space = met_space.reshape(band_groups, -1, NY)
    space_weights = own_potential
    if halves > 1:
        space_weights = lax.dynamic_slice_in_dim(
            own_potential, ga_at % halves * (NX // band_groups // halves),
            NX // band_groups // halves, 0,
        )

    share = rows // band_groups
    own_x = ga_at * rows + band_at * share + jnp.arange(share, dtype=jnp.int32)
    freq_x, freq_y = frequency(own_x, NX), frequency(jnp.arange(NY, dtype=jnp.int32), NY)
    kinetic = 2.0 * (
        freq_x[:, None] * freq_x[:, None] / (NX * NX)
        + freq_y[None, :] * freq_y[None, :] / (NY * NY)
    )
    kinetic = jnp.broadcast_to(kinetic[None], (planes, share, NY)).reshape(planes * share, NY)

    scale = 1.0 / (planes * NX * NY)
    grams = overlap(met_waves, kinetic, per, scale)
    spectrum = (in_space[1], potential, forth, back)
    returned.append(shifted(inverse(arrived[1], 0, half - 1, place, *spectrum)))
    grams, place = lax.optimization_barrier((grams, place))
    returned.append(shifted(inverse(arrived[1], half - 1, 1, place, *spectrum)))
    full_matrix = overlap(met_space, space_weights, per, scale, grams)
    all_bands = bands * band_groups
    col_width = all_bands // ga_count
    blocks = full_matrix.reshape(2, band_groups, bands, ga_count, col_width)
    blocks = blocks.transpose(1, 3, 0, 2, 4).reshape(
        band_groups * ga_count, 2, bands, col_width
    )
    subspace = lax.all_to_all(blocks, ("band", "ga"), 0, 0, tiled=True).sum(0)

    applied_waves = None
    for j, first in enumerate((0, half, own_bands - 1)):
        if j == 2:
            place, subspace = lax.optimization_barrier((place, subspace))
        applied_waves = unpack(returned[j], place, applied_waves, first, bands, planes)
    return (applied_waves, subspace)


def solution(mesh):
    placed = (
        P(None, "band", None, "ga"),
        P("ga", None),
        P(("band", "ga")),
        P(None, ("band", "ga")),
        P(("band", "ga"), None),
    )
    return jax.shard_map(
        shards,
        mesh=mesh,
        in_specs=placed,
        out_specs=(P(None, "band", None, "ga"), P(None, "band", "ga")),
        check_vma=False,
    )
```

```python
import functools

import jax
import jax.numpy as jnp
from jax import lax
from jax.experimental import pallas as pl
from jax.experimental.pallas import tpu as pltpu
from jax.sharding import PartitionSpec as P

NX = 384
NY = 384
LANES = 128
STEP = 2

width_cells = 1.5


def tables(indices):
    length = indices.shape[0]
    phases = indices[:, None] * indices[None, :] % length
    angles = phases.astype(jnp.float32) * (2.0 * jnp.pi / length)
    factor = 1.0 / jnp.sqrt(jnp.float32(length))
    return (
        (jnp.cos(angles) * factor).astype(jnp.bfloat16),
        (jnp.sin(angles) * factor).astype(jnp.bfloat16),
    )


def gaussian(distance):
    return jnp.exp(-distance * distance / (2.0 * width_cells * width_cells))


def frequency(indices, length):
    return jnp.where(indices < length // 2, indices, indices - length).astype(jnp.float32)


def dot(left, right):
    return jnp.dot(left, right, preferred_element_type=jnp.float32)


def lasting(microseconds):
    return pl.CostEstimate(
        flops=0, bytes_accessed=int(microseconds * 3.69e6), transcendentals=0
    )


def pack_body(place, *refs):
    halves = len(refs) - 1 - refs[-1].shape[0]
    sources, messages, held = refs[:halves], refs[halves:-1], refs[-1]
    groups, count, rows, _ = held.shape
    planes = groups // halves
    for h, source in enumerate(sources):
        for i in range(count):
            split = source[0, i].reshape(planes, rows, NY)
            for p in range(planes):
                held[p * halves + h, i] = split[p]
    for s, message in enumerate(messages):
        message[0] = held[lax.rem(place[0] + s, groups)]


def pack(waves, place, first, count, rows, groups):
    planes = waves.shape[2]
    halves = groups // planes
    own = waves.shape[1] // halves
    return pl.pallas_call(
        pack_body,
        grid=(2, count // STEP),
        in_specs=[pl.BlockSpec(memory_space=pltpu.SMEM)]
        + [
            pl.BlockSpec(
                (1, STEP, planes, rows * NY),
                functools.partial(block_at, (h * own + first) // STEP),
            )
            for h in range(halves)
        ],
        out_specs=[pl.BlockSpec((1, STEP, rows, NY), lambda c, n: (c, n, 0, 0))] * groups,
        out_shape=[jax.ShapeDtypeStruct((2, count, rows, NY), jnp.bfloat16)] * groups,
        scratch_shapes=[pltpu.VMEM((groups, STEP, rows, NY), jnp.bfloat16)],
        compiler_params=pltpu.CompilerParams(vmem_limit_bytes=56 << 20),
        cost_estimate=lasting(0.01),
        name="pack_planes",
    )(place, *[waves] * halves)


def block_at(base, c, n):
    return (c, base + n, 0, 0)


def mix_waves_body(w_ref, z_ref, mixed):
    _, bands, planes, width = w_ref.shape
    rows = width // NY
    per = 2 * bands
    for c in range(2):
        for n in range(bands):
            wide = w_ref[c, n].reshape(planes, rows, NY).astype(jnp.float32)
            for p in range(planes):
                at = pl.ds(p * rows * per + c * bands + n, rows, stride=per)
                for t in range(NY // LANES):
                    mixed[t, at, :] = wide[p, :, t * LANES : (t + 1) * LANES]
    for t in range(NY // LANES):
        z_ref[0, :, t * LANES : (t + 1) * LANES] = mixed[t].astype(jnp.bfloat16)


def mix_waves(waves, rows, shares):
    _, bands, planes, _ = waves.shape
    own = rows // shares
    depth = planes * own * 2 * bands
    return pl.pallas_call(
        mix_waves_body,
        grid=(shares,),
        in_specs=[pl.BlockSpec((2, bands, planes, own * NY), lambda d: (0, 0, 0, d))],
        out_specs=pl.BlockSpec((1, depth, NY), lambda d: (d, 0, 0)),
        out_shape=jax.ShapeDtypeStruct((shares, depth, NY), jnp.bfloat16),
        scratch_shapes=[pltpu.VMEM((NY // LANES, depth, LANES), jnp.float32)],
        compiler_params=pltpu.CompilerParams(vmem_limit_bytes=56 << 20),
        cost_estimate=lasting(0.01),
        name="mix_waves",
    )(waves)


def mix_space_body(s_ref, *refs):
    z_ref, mixed = refs[-2:]
    bands, _, rows, _ = s_ref.shape
    for c in range(2):
        for n in range(bands):
            wide = s_ref[n, c].astype(jnp.float32)
            for t in range(NY // LANES):
                mixed[t, pl.ds(c * bands + n, rows, stride=2 * bands), :] = wide[
                    :, t * LANES : (t + 1) * LANES
                ]
    for t in range(NY // LANES):
        z_ref[:, 0, :, t * LANES : (t + 1) * LANES] = (
            mixed[t].astype(jnp.bfloat16).reshape(z_ref.shape[0], -1, LANES)
        )


def mix_space(in_space, part, base, shares):
    bands = in_space.shape[0]
    own = NX // shares
    depth = own * 2 * bands
    group = max(1, 48 // own)
    in_specs = [pl.BlockSpec((bands, 2, group * own, NY), lambda d: (0, 0, d, 0))]
    operands = [in_space]
    aliases = {}
    if base is not None:
        in_specs.append(pl.BlockSpec(memory_space=pl.ANY))
        operands.append(base)
        aliases = {1: 0}
    return pl.pallas_call(
        mix_space_body,
        grid=(shares // group,),
        in_specs=in_specs,
        out_specs=pl.BlockSpec((group, 1, depth, NY), lambda d: (d, part, 0, 0)),
        out_shape=jax.ShapeDtypeStruct((shares, 2, depth, NY), jnp.bfloat16),
        scratch_shapes=[pltpu.VMEM((NY // LANES, group * depth, LANES), jnp.float32)],
        input_output_aliases=aliases,
        compiler_params=pltpu.CompilerParams(vmem_limit_bytes=56 << 20),
        cost_estimate=lasting(0.01),
        name="mix_space",
    )(*operands)


def unpack_body(groups, place, *refs):
    messages, o_ref, held = refs[:groups], refs[-2], refs[-1]
    halves, planes, count, rows, _ = held.shape
    for s, message in enumerate(messages):
        source = lax.rem(place[0] + groups - s, groups)
        held[lax.rem(source, halves), source // halves] = message[0]
    half = pl.program_id(1)
    for i in range(count):
        o_ref[0, i] = held[half, :, i].reshape(planes, rows * NY)


def unpack(messages, place, base, first, bands, planes):
    groups = len(messages)
    _, count, rows, _ = messages[0].shape
    halves = groups // planes
    own = bands // halves
    in_specs = [pl.BlockSpec(memory_space=pltpu.SMEM)] + [
        pl.BlockSpec((1, STEP, rows, NY), lambda c, h, n: (c, n, 0, 0))
    ] * groups
    operands = [place, *messages]
    aliases = {}
    if base is not None:
        in_specs.append(pl.BlockSpec(memory_space=pl.ANY))
        operands.append(base)
        aliases = {groups + 1: 0}
    return pl.pallas_call(
        functools.partial(unpack_body, groups),
        grid=(2, halves, count // STEP),
        in_specs=in_specs,
        out_specs=pl.BlockSpec(
            (1, STEP, planes, rows * NY), lambda c, h, n: (c, (h * own + first) // STEP + n, 0, 0)
        ),
        out_shape=jax.ShapeDtypeStruct((2, bands, planes, rows * NY), jnp.bfloat16),
        scratch_shapes=[pltpu.VMEM((halves, planes, STEP, rows, NY), jnp.bfloat16)],
        input_output_aliases=aliases,
        compiler_params=pltpu.CompilerParams(vmem_limit_bytes=56 << 20),
        cost_estimate=lasting(1.2 * count),
        name="unpack_planes",
    )(*operands)


def forward_body(groups, place, *refs):
    messages, (f_ref, b_ref, s_ref, held) = refs[:groups], refs[groups:]
    for s, message in enumerate(messages):
        held[lax.rem(place[0] + groups - s, groups)] = message[...]
    for i in range(STEP):
        parts = [held[:, c, i].reshape(NX, NY) for c in range(2)]
        first = dot(jnp.concatenate(parts, axis=1), f_ref[...]).astype(jnp.bfloat16)
        first = jnp.concatenate([first[:, :NY], first[:, NY:]], axis=0)
        in_space = dot(b_ref[...], first).astype(jnp.bfloat16)
        s_ref[i, 0] = in_space[:NX]
        s_ref[i, 1] = in_space[NX:]


def forward(messages, place, forth, back):
    groups = len(messages)
    _, bands, rows, _ = messages[0].shape
    square = pl.BlockSpec((2 * NX, 2 * NX), lambda n: (0, 0))
    return pl.pallas_call(
        functools.partial(forward_body, groups),
        grid=(bands // STEP,),
        in_specs=[pl.BlockSpec(memory_space=pltpu.SMEM)]
        + [pl.BlockSpec((2, STEP, rows, NY), lambda n: (0, n, 0, 0))] * groups
        + [square, square],
        out_specs=pl.BlockSpec((STEP, 2, NX, NY), lambda n: (n, 0, 0, 0)),
        out_shape=jax.ShapeDtypeStruct((bands, 2, NX, NY), jnp.bfloat16),
        scratch_shapes=[pltpu.VMEM((groups, 2, STEP, rows, NY), jnp.bfloat16)],
        compiler_params=pltpu.CompilerParams(vmem_limit_bytes=56 << 20),
        cost_estimate=lasting(0.01),
        name="forward",
    )(place, *messages, forth, back)


def inverse_body(groups, place, *refs):
    messages, (s_ref, v_ref, f_ref, b_ref) = refs[:groups], refs[groups : groups + 4]
    held = refs[-1]
    results = refs[-1 - groups : -1]
    rows = held.shape[3]
    freq_x = frequency(lax.broadcasted_iota(jnp.int32, (NX, 1), 0), NX)
    freq_y = frequency(lax.broadcasted_iota(jnp.int32, (1, NY), 1), NY)
    kinetic = 2.0 * (freq_x * freq_x / (NX * NX) + freq_y * freq_y / (NY * NY))
    for s, message in enumerate(messages):
        held[lax.rem(place[0] + groups - s, groups)] = message[...]
    for i in range(STEP):
        weighted = jnp.concatenate(
            [v_ref[...] * s_ref[i, c].astype(jnp.float32) for c in range(2)], axis=0
        ).astype(jnp.bfloat16)
        back = dot(f_ref[...], weighted).astype(jnp.bfloat16)
        recip = dot(jnp.concatenate([back[:NX], back[NX:]], axis=1), b_ref[...])
        for c in range(2):
            wide = held[:, c, i].reshape(NX, NY).astype(jnp.float32)
            applied = kinetic * wide + recip[:, c * NY : (c + 1) * NY]
            held[:, c, i] = applied.astype(jnp.bfloat16).reshape(groups, rows, NY)
    for s, result in enumerate(results):
        result[...] = held[lax.rem(place[0] + s, groups)]


def inverse(messages, base, bands, place, in_space, potential, forth, back):
    groups = len(messages)
    rows = messages[0].shape[2]
    shape = (2, bands, rows, NY)
    square = pl.BlockSpec((2 * NX, 2 * NX), lambda n: (0, 0))
    return pl.pallas_call(
        functools.partial(inverse_body, groups),
        grid=(bands // STEP,),
        in_specs=[pl.BlockSpec(memory_space=pltpu.SMEM)]
        + [pl.BlockSpec((2, STEP, rows, NY), lambda n: (0, base // STEP + n, 0, 0))] * groups
        + [
            pl.BlockSpec((STEP, 2, NX, NY), lambda n: (base // STEP + n, 0, 0, 0)),
            pl.BlockSpec((NX, NY), lambda n: (0, 0)),
            square,
            square,
        ],
        out_specs=[pl.BlockSpec((2, STEP, rows, NY), lambda n: (0, n, 0, 0))] * groups,
        out_shape=[jax.ShapeDtypeStruct(shape, jnp.bfloat16)] * groups,
        scratch_shapes=[pltpu.VMEM((groups, 2, STEP, rows, NY), jnp.bfloat16)],
        compiler_params=pltpu.CompilerParams(vmem_limit_bytes=56 << 20),
        cost_estimate=lasting(0.01),
        name="inverse",
    )(place, *messages, in_space, potential, forth, back)


def overlap_body(scale, per, z_ref, w_ref, *refs):
    o_ref, total = refs[-2:]
    shares, parts, _, _ = z_ref.shape
    bands = per // 2
    total[...] = jnp.zeros_like(total)
    pieces = [(d, h) for d in range(shares) for h in range(parts)]

    @pl.loop(0, w_ref.shape[0] // 2)
    def _(pair):
        plain, scaled = [], []
        at = pl.multiple_of(pair * 2 * per, 2 * per)
        both = [z_ref[d, h, pl.ds(at, 2 * per), :].astype(jnp.float32) for d, h in pieces]
        for k in range(2):
            wide = jnp.concatenate([rows[k * per : (k + 1) * per] for rows in both], axis=0)
            plain.append(wide.astype(jnp.bfloat16))
            scaled.append((wide * w_ref[pl.ds(pair * 2 + k, 1), :]).astype(jnp.bfloat16))
        total[...] += lax.dot_general(
            jnp.concatenate(plain, axis=1),
            jnp.concatenate(scaled, axis=1),
            (((1,), (1,)), ((), ())),
            preferred_element_type=jnp.float32,
        )

    size = total.shape[0]
    half = size // 2
    to = lax.broadcasted_iota(jnp.int32, (size, size), 0)
    at = lax.broadcasted_iota(jnp.int32, (size, size), 1)
    order = at % per // bands * half + at // per * bands + at % bands
    chosen = (to == order).astype(jnp.float32)
    grams = jnp.dot(
        chosen, total[...], precision=lax.Precision.HIGHEST, preferred_element_type=jnp.float32
    )
    grams = lax.dot_general(
        grams,
        chosen,
        (((1,), (1,)), ((), ())),
        precision=lax.Precision.HIGHEST,
        preferred_element_type=jnp.float32,
    )
    real = (grams[:half, :half] + grams[half:, half:]) * scale
    imaginary = (grams[:half, half:] - grams[half:, :half]) * scale
    if len(refs) == 3:
        real, imaginary = real + refs[0][0], imaginary + refs[0][1]
    o_ref[0] = real
    o_ref[1] = imaginary


def overlap(pieces, weights, per, scale, before=None):
    shares, parts, _, _ = pieces.shape
    size = shares * parts * per
    whole = pl.BlockSpec(memory_space=pltpu.VMEM)
    operands = [pieces, weights] + ([] if before is None else [before])
    return pl.pallas_call(
        functools.partial(overlap_body, scale, per),
        in_specs=[whole] * len(operands),
        out_specs=whole,
        out_shape=jax.ShapeDtypeStruct((2, size // 2, size // 2), jnp.float32),
        scratch_shapes=[pltpu.VMEM((size, size), jnp.float32)],
        compiler_params=pltpu.CompilerParams(vmem_limit_bytes=56 << 20),
        cost_estimate=lasting(8.0),
        name="overlap",
    )(*operands)


def shifted(messages):
    groups = len(messages)
    return [
        lax.ppermute(message, "ga", [(i, (i + s) % groups) for i in range(groups)]) if s else message
        for s, message in enumerate(messages)
    ]


def split(wide):
    high = wide.astype(jnp.bfloat16)
    return high, (wide - high.astype(jnp.float32)).astype(jnp.bfloat16)


def charges_body(planes, slab_rows, place, c_ref, i_ref, o_ref):
    share = o_ref.shape[0]
    first = place[0].astype(jnp.float32)
    plane = place[1].astype(jnp.float32)
    own_x = lax.broadcasted_iota(jnp.int32, (share, 1), 0).astype(jnp.float32) + first
    cells_y = lax.broadcasted_iota(jnp.int32, (NY, 1), 0)
    slab_y = (cells_y // slab_rows).astype(jnp.float32)
    cells_y = cells_y.astype(jnp.float32)
    o_ref[...] = i_ref[...]

    @pl.loop(0, c_ref.shape[0])
    def _(device):
        along_u, along_v, along_w, amount, slab = [c_ref[device, k : k + 1, :] for k in range(5)]
        kernel_x = gaussian(own_x - NX * along_u) * (amount * gaussian(plane - planes * along_w))
        kernel_y = gaussian(cells_y - (slab * slab_rows + slab_rows * along_v))
        kernel_y = jnp.where(slab_y == slab, kernel_y, 0.0)
        (x_high, x_low), (y_high, y_low) = split(kernel_x), split(kernel_y)
        total = o_ref[...]
        for left, right in ((x_high, y_low), (x_low, y_high), (x_high, y_high)):
            total = total + lax.dot_general(
                left, right, (((1,), (1,)), ((), ())), preferred_element_type=jnp.float32
            )
        o_ref[...] = total


def potential_message(ionic_field, point_charge, charge_place, charge_slab, planes, halves):
    ga_count = lax.axis_size("ga")
    band_groups = lax.axis_size("band")
    devices = band_groups * ga_count
    slab_rows = NY // ga_count
    share = NX // band_groups
    piece = share * slab_rows // band_groups
    atoms = point_charge.shape[0]
    spare = -(-piece // atoms)
    band_at = lax.axis_index("band")
    charges = jnp.concatenate(
        [charge_place, point_charge[None], charge_slab[:, 0][None].astype(jnp.float32)], axis=0
    )
    ionic = ionic_field.T.reshape(planes, band_groups, band_groups, piece)
    ionic = lax.dynamic_index_in_dim(ionic, band_at, 2, keepdims=False)
    ionic = jnp.broadcast_to(
        ionic.transpose(1, 0, 2)[:, :, None], (band_groups, planes, halves, piece)
    )
    ionic = jnp.pad(ionic.reshape(devices, piece), ((0, 0), (0, spare * atoms - piece)))
    return jnp.concatenate(
        [
            jnp.broadcast_to(charges[None], (devices, 5, atoms)),
            ionic.reshape(devices, spare, atoms),
        ],
        axis=1,
    )


def own_share(message, planes, halves):
    ga_count = lax.axis_size("ga")
    band_groups = lax.axis_size("band")
    slab_rows = NY // ga_count
    share = NX // band_groups
    piece = share * slab_rows // band_groups
    atoms = message.shape[2]
    spare = message.shape[1] - 5
    band_at = lax.axis_index("band")
    ionic = message[:, 5:].reshape(band_groups, ga_count, spare * atoms)[:, :, :piece]
    ionic = ionic.transpose(1, 0, 2).reshape(ga_count, share, slab_rows)
    ionic = ionic.transpose(1, 0, 2).reshape(share, NY)
    place = jnp.stack([band_at * share, lax.axis_index("ga") // halves]).astype(jnp.int32)
    return pl.pallas_call(
        functools.partial(charges_body, planes, slab_rows),
        in_specs=[
            pl.BlockSpec(memory_space=pltpu.SMEM),
            pl.BlockSpec(memory_space=pltpu.VMEM),
            pl.BlockSpec(memory_space=pltpu.VMEM),
        ],
        out_specs=pl.BlockSpec(memory_space=pltpu.VMEM),
        out_shape=jax.ShapeDtypeStruct((share, NY), jnp.float32),
        compiler_params=pltpu.CompilerParams(vmem_limit_bytes=56 << 20),
        cost_estimate=lasting(0.01),
        name="charge_potential",
    )(place, message, ionic)


def shards(waves, ionic_field, point_charge, charge_place, charge_slab):
    ga_count = lax.axis_size("ga")
    band_groups = lax.axis_size("band")
    bands = waves.shape[1]
    planes = waves.shape[2]
    rows = NX // ga_count
    halves = ga_count // planes
    own_bands = bands // halves
    half = own_bands // 2
    chunks = [(0, half), (half, half)]
    per = 2 * bands
    pairs = [[p * halves + h for h in range(halves)] for p in range(planes)]
    ga_at, band_at = lax.axis_index("ga"), lax.axis_index("band")
    place = ga_at.astype(jnp.int32)[None]

    packed = [pack(waves, place, first, count, rows, ga_count) for first, count in chunks]
    message = potential_message(
        ionic_field, point_charge, charge_place, charge_slab, planes, halves
    )

    arrived = [shifted(packed[0])]
    message = lax.all_to_all(message, ("band", "ga"), 0, 0, tiled=True)
    own_potential = own_share(message, planes, halves)
    copies = jnp.broadcast_to(own_potential[None], (band_groups,) + own_potential.shape)
    potential = lax.all_to_all(copies, "band", 0, 0, tiled=True).reshape(NX, NY)
    mixed = mix_waves(waves, rows, band_groups)
    cells = jnp.arange(NX, dtype=jnp.int32)
    arrived[0], potential, packed[1], mixed, cells = lax.optimization_barrier(
        (arrived[0], potential, packed[1], mixed, cells)
    )

    arrived.append(shifted(packed[1]))
    met_waves = lax.all_to_all(mixed, "band", 0, 0, tiled=True)
    cosine, sine = tables(cells)
    forth = jnp.concatenate(
        [jnp.concatenate([cosine, sine], axis=1), jnp.concatenate([-sine, cosine], axis=1)], axis=0
    )
    back = jnp.concatenate(
        [jnp.concatenate([cosine, -sine], axis=1), jnp.concatenate([sine, cosine], axis=1)], axis=0
    )
    in_space = [forward(arrived[0], place, forth, back)]
    shares = band_groups * halves
    mixed = mix_space(in_space[0], 0, None, shares)
    result = inverse(arrived[0], 0, half, place, in_space[0], potential, forth, back)
    arrived[1], met_waves, result, mixed = lax.optimization_barrier(
        (arrived[1], met_waves, result, mixed)
    )

    returned = [shifted(result)]
    in_space.append(forward(arrived[1], place, forth, back))
    mixed = mix_space(in_space[1], 1, mixed, shares)
    mixed, returned[0][1] = lax.optimization_barrier((mixed, returned[0][1]))
    if halves > 1:
        mixed = mixed.reshape(band_groups, halves, -1, NY)
        mixed = lax.all_to_all(mixed, "ga", 1, 1, axis_index_groups=pairs, tiled=True)
    met_space = lax.all_to_all(mixed, "band", 0, 0, tiled=True)
    if halves > 1:
        met_space = met_space.reshape(band_groups, halves, 2, -1, 2, half, NY)
        met_space = met_space.transpose(0, 3, 4, 1, 2, 5, 6)
        met_space = met_space.reshape(band_groups, 1, -1, NY)
    space_weights = own_potential
    if halves > 1:
        space_weights = lax.dynamic_slice_in_dim(
            own_potential, ga_at % halves * (NX // band_groups // halves),
            NX // band_groups // halves, 0,
        )

    share = rows // band_groups
    own_x = ga_at * rows + band_at * share + jnp.arange(share, dtype=jnp.int32)
    freq_x, freq_y = frequency(own_x, NX), frequency(jnp.arange(NY, dtype=jnp.int32), NY)
    kinetic = 2.0 * (
        freq_x[:, None] * freq_x[:, None] / (NX * NX)
        + freq_y[None, :] * freq_y[None, :] / (NY * NY)
    )
    kinetic = jnp.broadcast_to(kinetic[None], (planes, share, NY)).reshape(planes * share, NY)

    scale = 1.0 / (planes * NX * NY)
    applied_waves = unpack(returned[0], place, None, 0, bands, planes)
    grams = overlap(met_waves[:, None], kinetic, per, scale)
    spectrum = (in_space[1], potential, forth, back)
    firsts = list(range(0, half, STEP))
    for first in firsts:
        if first == firsts[-1]:
            grams, place = lax.optimization_barrier((grams, place))
        returned.append(shifted(inverse(arrived[1], first, STEP, place, *spectrum)))
    grams, applied_waves = lax.optimization_barrier((grams, applied_waves))
    full_matrix = overlap(
        met_space, space_weights, per // met_space.shape[1], scale, grams
    )
    all_bands = bands * band_groups
    col_width = all_bands // ga_count
    blocks = full_matrix.reshape(2, band_groups, bands, ga_count, col_width)
    blocks = blocks.transpose(1, 3, 0, 2, 4).reshape(
        band_groups * ga_count, 2, bands, col_width
    )
    subspace = lax.all_to_all(blocks, ("band", "ga"), 0, 0, tiled=True).sum(0)

    for j, first in enumerate(firsts):
        if first == firsts[-1]:
            place, subspace = lax.optimization_barrier((place, subspace))
        applied_waves = unpack(returned[j + 1], place, applied_waves, half + first, bands, planes)
    return (applied_waves, subspace)


def solution(mesh):
    placed = (
        P(None, "band", None, "ga"),
        P("ga", None),
        P(("band", "ga")),
        P(None, ("band", "ga")),
        P(("band", "ga"), None),
    )
    return jax.shard_map(
        shards,
        mesh=mesh,
        in_specs=placed,
        out_specs=(P(None, "band", None, "ga"), P(None, "band", "ga")),
        check_vma=False,
    )
```

```python
import functools

import jax
import jax.numpy as jnp
from jax import lax
from jax.experimental import pallas as pl
from jax.experimental.pallas import tpu as pltpu
from jax.sharding import PartitionSpec as P

NX = 384
NY = 384
LANES = 128
STEP = 2
UNIT = 48

width_cells = 1.5


def tables(indices):
    length = indices.shape[0]
    phases = indices[:, None] * indices[None, :] % length
    angles = phases.astype(jnp.float32) * (2.0 * jnp.pi / length)
    factor = 1.0 / jnp.sqrt(jnp.float32(length))
    return (
        (jnp.cos(angles) * factor).astype(jnp.bfloat16),
        (jnp.sin(angles) * factor).astype(jnp.bfloat16),
    )


def gaussian(distance):
    return jnp.exp(-distance * distance / (2.0 * width_cells * width_cells))


def frequency(indices, length):
    return jnp.where(indices < length // 2, indices, indices - length).astype(jnp.float32)


def dot(left, right):
    return jnp.dot(left, right, preferred_element_type=jnp.float32)


def lasting(microseconds):
    return pl.CostEstimate(
        flops=0, bytes_accessed=int(microseconds * 3.69e6), transcendentals=0
    )


def pack_body(place, *refs):
    halves = len(refs) - 1 - refs[-1].shape[0]
    sources, messages, held = refs[:halves], refs[halves:-1], refs[-1]
    groups, count, rows, _ = held.shape
    planes = groups // halves
    for h, source in enumerate(sources):
        for i in range(count):
            split = source[0, i].reshape(planes, rows, NY)
            for p in range(planes):
                held[p * halves + h, i] = split[p]
    for s, message in enumerate(messages):
        message[0] = held[lax.rem(place[0] + s, groups)]


def pack(waves, place, first, count, rows, groups):
    planes = waves.shape[2]
    halves = groups // planes
    own = waves.shape[1] // halves
    return pl.pallas_call(
        pack_body,
        grid=(2, count // STEP),
        in_specs=[pl.BlockSpec(memory_space=pltpu.SMEM)]
        + [
            pl.BlockSpec(
                (1, STEP, planes, rows * NY),
                functools.partial(block_at, (h * own + first) // STEP),
            )
            for h in range(halves)
        ],
        out_specs=[pl.BlockSpec((1, STEP, rows, NY), lambda c, n: (c, n, 0, 0))] * groups,
        out_shape=[jax.ShapeDtypeStruct((2, count, rows, NY), jnp.bfloat16)] * groups,
        scratch_shapes=[pltpu.VMEM((groups, STEP, rows, NY), jnp.bfloat16)],
        compiler_params=pltpu.CompilerParams(vmem_limit_bytes=56 << 20),
        cost_estimate=lasting(0.01),
        name="pack_planes",
    )(place, *[waves] * halves)


def block_at(base, c, n):
    return (c, base + n, 0, 0)


def mix_waves_body(w_ref, z_ref, mixed):
    _, bands, planes, width = w_ref.shape
    rows = width // NY
    per = 2 * bands
    for c in range(2):
        for n in range(bands):
            wide = w_ref[c, n].reshape(planes, rows, NY).astype(jnp.float32)
            for p in range(planes):
                at = pl.ds(p * rows * per + c * bands + n, rows, stride=per)
                for t in range(NY // LANES):
                    mixed[t, at, :] = wide[p, :, t * LANES : (t + 1) * LANES]
    for t in range(NY // LANES):
        z_ref[0, :, t * LANES : (t + 1) * LANES] = mixed[t].astype(jnp.bfloat16)


def mix_waves(waves, rows, shares):
    _, bands, planes, _ = waves.shape
    own = rows // shares
    depth = planes * own * 2 * bands
    return pl.pallas_call(
        mix_waves_body,
        grid=(shares,),
        in_specs=[pl.BlockSpec((2, bands, planes, own * NY), lambda d: (0, 0, 0, d))],
        out_specs=pl.BlockSpec((1, depth, NY), lambda d: (d, 0, 0)),
        out_shape=jax.ShapeDtypeStruct((shares, depth, NY), jnp.bfloat16),
        scratch_shapes=[pltpu.VMEM((NY // LANES, depth, LANES), jnp.float32)],
        compiler_params=pltpu.CompilerParams(vmem_limit_bytes=56 << 20),
        cost_estimate=lasting(0.01),
        name="mix_waves",
    )(waves)


def mix_space_body(s_ref, *refs):
    z_ref = refs[-1]
    bands, _, rows, _ = s_ref.shape
    size = 2 * bands * UNIT
    to = lax.broadcasted_iota(jnp.int32, (size, size), 0)
    at = lax.broadcasted_iota(jnp.int32, (size, size), 1)
    band, part, row = at // (2 * UNIT), at // UNIT % 2, at % UNIT
    chosen = (to == row * 2 * bands + part * bands + band).astype(jnp.bfloat16)
    shares, _, depth, _ = z_ref.shape
    each = shares * UNIT // rows
    for unit in range(rows // UNIT):
        cut = slice(unit * UNIT, (unit + 1) * UNIT)
        stacked = jnp.concatenate(
            [s_ref[n, c, cut] for n in range(bands) for c in range(2)], axis=0
        )
        mixed = dot(chosen, stacked).astype(jnp.bfloat16)
        z_ref[unit * each : (unit + 1) * each, 0] = mixed.reshape(each, depth, NY)


def mix_space(in_space, part, base, shares):
    bands = in_space.shape[0]
    own = NX // shares
    depth = own * 2 * bands
    rows = 2 * UNIT
    in_specs = [pl.BlockSpec((bands, 2, rows, NY), lambda d: (0, 0, d, 0))]
    operands = [in_space]
    aliases = {}
    if base is not None:
        in_specs.append(pl.BlockSpec(memory_space=pl.ANY))
        operands.append(base)
        aliases = {1: 0}
    return pl.pallas_call(
        mix_space_body,
        grid=(NX // rows,),
        in_specs=in_specs,
        out_specs=pl.BlockSpec((rows // own, 1, depth, NY), lambda d: (d, part, 0, 0)),
        out_shape=jax.ShapeDtypeStruct((shares, 2, depth, NY), jnp.bfloat16),
        input_output_aliases=aliases,
        compiler_params=pltpu.CompilerParams(vmem_limit_bytes=56 << 20),
        cost_estimate=lasting(0.01),
        name="mix_space",
    )(*operands)


def unpack_body(groups, place, *refs):
    messages, o_ref, held = refs[:groups], refs[-2], refs[-1]
    halves, planes, count, rows, _ = held.shape
    for s, message in enumerate(messages):
        source = lax.rem(place[0] + groups - s, groups)
        held[lax.rem(source, halves), source // halves] = message[0]
    half = pl.program_id(1)
    for i in range(count):
        o_ref[0, i] = held[half, :, i].reshape(planes, rows * NY)


def unpack(messages, place, base, first, bands, planes):
    groups = len(messages)
    _, count, rows, _ = messages[0].shape
    halves = groups // planes
    own = bands // halves
    in_specs = [pl.BlockSpec(memory_space=pltpu.SMEM)] + [
        pl.BlockSpec((1, STEP, rows, NY), lambda c, h, n: (c, n, 0, 0))
    ] * groups
    operands = [place, *messages]
    aliases = {}
    if base is not None:
        in_specs.append(pl.BlockSpec(memory_space=pl.ANY))
        operands.append(base)
        aliases = {groups + 1: 0}
    return pl.pallas_call(
        functools.partial(unpack_body, groups),
        grid=(2, halves, count // STEP),
        in_specs=in_specs,
        out_specs=pl.BlockSpec(
            (1, STEP, planes, rows * NY), lambda c, h, n: (c, (h * own + first) // STEP + n, 0, 0)
        ),
        out_shape=jax.ShapeDtypeStruct((2, bands, planes, rows * NY), jnp.bfloat16),
        scratch_shapes=[pltpu.VMEM((halves, planes, STEP, rows, NY), jnp.bfloat16)],
        input_output_aliases=aliases,
        compiler_params=pltpu.CompilerParams(vmem_limit_bytes=56 << 20),
        cost_estimate=lasting(1.2 * count),
        name="unpack_planes",
    )(*operands)


def forward_body(groups, place, *refs):
    messages, (f_ref, b_ref, s_ref, held) = refs[:groups], refs[groups:]
    for s, message in enumerate(messages):
        held[lax.rem(place[0] + groups - s, groups)] = message[...]
    for i in range(STEP):
        parts = [held[:, c, i].reshape(NX, NY) for c in range(2)]
        first = dot(jnp.concatenate(parts, axis=1), f_ref[...]).astype(jnp.bfloat16)
        first = jnp.concatenate([first[:, :NY], first[:, NY:]], axis=0)
        in_space = dot(b_ref[...], first).astype(jnp.bfloat16)
        s_ref[i, 0] = in_space[:NX]
        s_ref[i, 1] = in_space[NX:]


def forward(messages, place, forth, back):
    groups = len(messages)
    _, bands, rows, _ = messages[0].shape
    square = pl.BlockSpec((2 * NX, 2 * NX), lambda n: (0, 0))
    return pl.pallas_call(
        functools.partial(forward_body, groups),
        grid=(bands // STEP,),
        in_specs=[pl.BlockSpec(memory_space=pltpu.SMEM)]
        + [pl.BlockSpec((2, STEP, rows, NY), lambda n: (0, n, 0, 0))] * groups
        + [square, square],
        out_specs=pl.BlockSpec((STEP, 2, NX, NY), lambda n: (n, 0, 0, 0)),
        out_shape=jax.ShapeDtypeStruct((bands, 2, NX, NY), jnp.bfloat16),
        scratch_shapes=[pltpu.VMEM((groups, 2, STEP, rows, NY), jnp.bfloat16)],
        compiler_params=pltpu.CompilerParams(vmem_limit_bytes=56 << 20),
        cost_estimate=lasting(0.01),
        name="forward",
    )(place, *messages, forth, back)


def inverse_body(groups, place, *refs):
    messages, (s_ref, v_ref, f_ref, b_ref) = refs[:groups], refs[groups : groups + 4]
    held = refs[-1]
    results = refs[-1 - groups : -1]
    rows = held.shape[3]
    freq_x = frequency(lax.broadcasted_iota(jnp.int32, (NX, 1), 0), NX)
    freq_y = frequency(lax.broadcasted_iota(jnp.int32, (1, NY), 1), NY)
    kinetic = 2.0 * (freq_x * freq_x / (NX * NX) + freq_y * freq_y / (NY * NY))
    for s, message in enumerate(messages):
        held[lax.rem(place[0] + groups - s, groups)] = message[...]
    for i in range(STEP):
        weighted = jnp.concatenate(
            [v_ref[...] * s_ref[i, c].astype(jnp.float32) for c in range(2)], axis=0
        ).astype(jnp.bfloat16)
        back = dot(f_ref[...], weighted).astype(jnp.bfloat16)
        recip = dot(jnp.concatenate([back[:NX], back[NX:]], axis=1), b_ref[...])
        for c in range(2):
            wide = held[:, c, i].reshape(NX, NY).astype(jnp.float32)
            applied = kinetic * wide + recip[:, c * NY : (c + 1) * NY]
            held[:, c, i] = applied.astype(jnp.bfloat16).reshape(groups, rows, NY)
    for s, result in enumerate(results):
        result[...] = held[lax.rem(place[0] + s, groups)]


def inverse(messages, base, bands, place, in_space, potential, forth, back):
    groups = len(messages)
    rows = messages[0].shape[2]
    shape = (2, bands, rows, NY)
    square = pl.BlockSpec((2 * NX, 2 * NX), lambda n: (0, 0))
    return pl.pallas_call(
        functools.partial(inverse_body, groups),
        grid=(bands // STEP,),
        in_specs=[pl.BlockSpec(memory_space=pltpu.SMEM)]
        + [pl.BlockSpec((2, STEP, rows, NY), lambda n: (0, base // STEP + n, 0, 0))] * groups
        + [
            pl.BlockSpec((STEP, 2, NX, NY), lambda n: (base // STEP + n, 0, 0, 0)),
            pl.BlockSpec((NX, NY), lambda n: (0, 0)),
            square,
            square,
        ],
        out_specs=[pl.BlockSpec((2, STEP, rows, NY), lambda n: (0, n, 0, 0))] * groups,
        out_shape=[jax.ShapeDtypeStruct(shape, jnp.bfloat16)] * groups,
        scratch_shapes=[pltpu.VMEM((groups, 2, STEP, rows, NY), jnp.bfloat16)],
        compiler_params=pltpu.CompilerParams(vmem_limit_bytes=56 << 20),
        cost_estimate=lasting(0.01),
        name="inverse",
    )(place, *messages, in_space, potential, forth, back)


def overlap_body(scale, per, z_ref, w_ref, *refs):
    o_ref, total = refs[-2:]
    shares, parts, _, _ = z_ref.shape
    bands = per // 2
    total[...] = jnp.zeros_like(total)
    pieces = [(d, h) for d in range(shares) for h in range(parts)]

    @pl.loop(0, w_ref.shape[0] // 2)
    def _(pair):
        plain, scaled = [], []
        at = pl.multiple_of(pair * 2 * per, 2 * per)
        both = [z_ref[d, h, pl.ds(at, 2 * per), :].astype(jnp.float32) for d, h in pieces]
        for k in range(2):
            wide = jnp.concatenate([rows[k * per : (k + 1) * per] for rows in both], axis=0)
            plain.append(wide.astype(jnp.bfloat16))
            scaled.append((wide * w_ref[pl.ds(pair * 2 + k, 1), :]).astype(jnp.bfloat16))
        total[...] += lax.dot_general(
            jnp.concatenate(plain, axis=1),
            jnp.concatenate(scaled, axis=1),
            (((1,), (1,)), ((), ())),
            preferred_element_type=jnp.float32,
        )

    size = total.shape[0]
    half = size // 2
    to = lax.broadcasted_iota(jnp.int32, (size, size), 0)
    at = lax.broadcasted_iota(jnp.int32, (size, size), 1)
    order = at % per // bands * half + at // per * bands + at % bands
    chosen = (to == order).astype(jnp.float32)
    grams = jnp.dot(
        chosen, total[...], precision=lax.Precision.HIGHEST, preferred_element_type=jnp.float32
    )
    grams = lax.dot_general(
        grams,
        chosen,
        (((1,), (1,)), ((), ())),
        precision=lax.Precision.HIGHEST,
        preferred_element_type=jnp.float32,
    )
    real = (grams[:half, :half] + grams[half:, half:]) * scale
    imaginary = (grams[:half, half:] - grams[half:, :half]) * scale
    if len(refs) == 3:
        real, imaginary = real + refs[0][0], imaginary + refs[0][1]
    o_ref[0] = real
    o_ref[1] = imaginary


def overlap(pieces, weights, per, scale, before=None):
    shares, parts, _, _ = pieces.shape
    size = shares * parts * per
    whole = pl.BlockSpec(memory_space=pltpu.VMEM)
    operands = [pieces, weights] + ([] if before is None else [before])
    return pl.pallas_call(
        functools.partial(overlap_body, scale, per),
        in_specs=[whole] * len(operands),
        out_specs=whole,
        out_shape=jax.ShapeDtypeStruct((2, size // 2, size // 2), jnp.float32),
        scratch_shapes=[pltpu.VMEM((size, size), jnp.float32)],
        compiler_params=pltpu.CompilerParams(vmem_limit_bytes=56 << 20),
        cost_estimate=lasting(8.0),
        name="overlap",
    )(*operands)


def shifted(messages):
    groups = len(messages)
    return [
        lax.ppermute(message, "ga", [(i, (i + s) % groups) for i in range(groups)]) if s else message
        for s, message in enumerate(messages)
    ]


def split(wide):
    high = wide.astype(jnp.bfloat16)
    return high, (wide - high.astype(jnp.float32)).astype(jnp.bfloat16)


def charges_body(planes, slab_rows, place, c_ref, i_ref, o_ref, total):
    first = place[0].astype(jnp.float32)
    plane = place[1].astype(jnp.float32)
    own_x = lax.broadcasted_iota(jnp.int32, (LANES, 1), 0).astype(jnp.float32) + first
    cells_y = lax.broadcasted_iota(jnp.int32, (NY, 1), 0)
    slab_y = (cells_y // slab_rows).astype(jnp.float32)
    cells_y = cells_y.astype(jnp.float32)
    total[...] = jnp.zeros_like(total)

    @pl.loop(0, c_ref.shape[0] // 2)
    def _(pair):
        lefts, rights = [], []
        for k in range(2):
            along_u, along_v, along_w, amount, slab = [
                c_ref[pair * 2 + k, row : row + 1, :] for row in range(5)
            ]
            weight = amount * gaussian(plane - planes * along_w)
            x_high, x_low = split(gaussian(own_x - NX * along_u) * weight)
            kernel_y = gaussian(cells_y - (slab * slab_rows + slab_rows * along_v))
            y_high, y_low = split(jnp.where(slab_y == slab, kernel_y, 0.0))
            lefts += [y_low, y_high, y_high]
            rights += [x_high, x_low, x_high]
        total[...] += lax.dot_general(
            jnp.concatenate(lefts, axis=1),
            jnp.concatenate(rights, axis=1),
            (((1,), (1,)), ((), ())),
            preferred_element_type=jnp.float32,
        )

    o_ref[...] = i_ref[...] + total[...].T[: o_ref.shape[0]]


def potential_message(ionic_field, point_charge, charge_place, charge_slab, planes, halves):
    ga_count = lax.axis_size("ga")
    band_groups = lax.axis_size("band")
    devices = band_groups * ga_count
    slab_rows = NY // ga_count
    share = NX // band_groups
    piece = share * slab_rows // band_groups
    atoms = point_charge.shape[0]
    spare = -(-piece // atoms)
    band_at = lax.axis_index("band")
    charges = jnp.concatenate(
        [charge_place, point_charge[None], charge_slab[:, 0][None].astype(jnp.float32)], axis=0
    )
    ionic = ionic_field.T.reshape(planes, band_groups, band_groups, piece)
    ionic = lax.dynamic_index_in_dim(ionic, band_at, 2, keepdims=False)
    ionic = jnp.broadcast_to(
        ionic.transpose(1, 0, 2)[:, :, None], (band_groups, planes, halves, piece)
    )
    ionic = jnp.pad(ionic.reshape(devices, piece), ((0, 0), (0, spare * atoms - piece)))
    return jnp.concatenate(
        [
            jnp.broadcast_to(charges[None], (devices, 5, atoms)),
            ionic.reshape(devices, spare, atoms),
        ],
        axis=1,
    )


def own_share(message, planes, halves):
    ga_count = lax.axis_size("ga")
    band_groups = lax.axis_size("band")
    slab_rows = NY // ga_count
    share = NX // band_groups
    piece = share * slab_rows // band_groups
    atoms = message.shape[2]
    spare = message.shape[1] - 5
    band_at = lax.axis_index("band")
    ionic = message[:, 5:].reshape(band_groups, ga_count, spare * atoms)[:, :, :piece]
    ionic = ionic.transpose(1, 0, 2).reshape(ga_count, share, slab_rows)
    ionic = ionic.transpose(1, 0, 2).reshape(share, NY)
    place = jnp.stack([band_at * share, lax.axis_index("ga") // halves]).astype(jnp.int32)
    return pl.pallas_call(
        functools.partial(charges_body, planes, slab_rows),
        in_specs=[
            pl.BlockSpec(memory_space=pltpu.SMEM),
            pl.BlockSpec(memory_space=pltpu.VMEM),
            pl.BlockSpec(memory_space=pltpu.VMEM),
        ],
        out_specs=pl.BlockSpec(memory_space=pltpu.VMEM),
        out_shape=jax.ShapeDtypeStruct((share, NY), jnp.float32),
        scratch_shapes=[pltpu.VMEM((NY, LANES), jnp.float32)],
        compiler_params=pltpu.CompilerParams(vmem_limit_bytes=56 << 20),
        cost_estimate=lasting(0.01),
        name="charge_potential",
    )(place, message, ionic)


def shards(waves, ionic_field, point_charge, charge_place, charge_slab):
    ga_count = lax.axis_size("ga")
    band_groups = lax.axis_size("band")
    bands = waves.shape[1]
    planes = waves.shape[2]
    rows = NX // ga_count
    halves = ga_count // planes
    own_bands = bands // halves
    half = own_bands // 2
    chunks = [(0, half), (half, half)]
    per = 2 * bands
    pairs = [[p * halves + h for h in range(halves)] for p in range(planes)]
    ga_at, band_at = lax.axis_index("ga"), lax.axis_index("band")
    place = ga_at.astype(jnp.int32)[None]

    packed = [pack(waves, place, first, count, rows, ga_count) for first, count in chunks]
    message = potential_message(
        ionic_field, point_charge, charge_place, charge_slab, planes, halves
    )

    arrived = [shifted(packed[0])]
    message = lax.all_to_all(message, ("band", "ga"), 0, 0, tiled=True)
    mixed = mix_waves(waves, rows, band_groups)
    message, packed[1], mixed = lax.optimization_barrier((message, packed[1], mixed))
    own_potential = own_share(message, planes, halves)
    copies = jnp.broadcast_to(own_potential[None], (band_groups,) + own_potential.shape)
    potential = lax.all_to_all(copies, "band", 0, 0, tiled=True).reshape(NX, NY)
    cells = jnp.arange(NX, dtype=jnp.int32)
    arrived[0], potential, packed[1], mixed, cells = lax.optimization_barrier(
        (arrived[0], potential, packed[1], mixed, cells)
    )

    arrived.append(shifted(packed[1]))
    met_waves = lax.all_to_all(mixed, "band", 0, 0, tiled=True)
    cosine, sine = tables(cells)
    forth = jnp.concatenate(
        [jnp.concatenate([cosine, sine], axis=1), jnp.concatenate([-sine, cosine], axis=1)], axis=0
    )
    back = jnp.concatenate(
        [jnp.concatenate([cosine, -sine], axis=1), jnp.concatenate([sine, cosine], axis=1)], axis=0
    )
    in_space = [forward(arrived[0], place, forth, back)]
    shares = band_groups * halves
    mixed = mix_space(in_space[0], 0, None, shares)
    result = inverse(arrived[0], 0, half, place, in_space[0], potential, forth, back)
    arrived[1], met_waves, result, mixed = lax.optimization_barrier(
        (arrived[1], met_waves, result, mixed)
    )

    returned = [shifted(result)]
    in_space.append(forward(arrived[1], place, forth, back))
    mixed = mix_space(in_space[1], 1, mixed, shares)
    mixed, returned[0][1] = lax.optimization_barrier((mixed, returned[0][1]))
    if halves > 1:
        mixed = mixed.reshape(band_groups, halves, -1, NY)
        mixed = lax.all_to_all(mixed, "ga", 1, 1, axis_index_groups=pairs, tiled=True)
    met_space = lax.all_to_all(mixed, "band", 0, 0, tiled=True)
    if halves > 1:
        met_space = met_space.reshape(band_groups, halves, 2, -1, 2, half, NY)
        met_space = met_space.transpose(0, 3, 4, 1, 2, 5, 6)
        met_space = met_space.reshape(band_groups, 1, -1, NY)
    space_weights = own_potential
    if halves > 1:
        space_weights = lax.dynamic_slice_in_dim(
            own_potential, ga_at % halves * (NX // band_groups // halves),
            NX // band_groups // halves, 0,
        )

    share = rows // band_groups
    own_x = ga_at * rows + band_at * share + jnp.arange(share, dtype=jnp.int32)
    freq_x, freq_y = frequency(own_x, NX), frequency(jnp.arange(NY, dtype=jnp.int32), NY)
    kinetic = 2.0 * (
        freq_x[:, None] * freq_x[:, None] / (NX * NX)
        + freq_y[None, :] * freq_y[None, :] / (NY * NY)
    )
    kinetic = jnp.broadcast_to(kinetic[None], (planes, share, NY)).reshape(planes * share, NY)

    scale = 1.0 / (planes * NX * NY)
    spectrum = (in_space[1], potential, forth, back)
    place, returned[0][-1] = lax.optimization_barrier((place, returned[0][-1]))
    returned.append(shifted(inverse(arrived[1], 0, half, place, *spectrum)))
    grams = overlap(met_waves[:, None], kinetic, per, scale)
    applied_waves = unpack(returned[0], place, None, 0, bands, planes)
    full_matrix = overlap(
        met_space, space_weights, per // met_space.shape[1], scale, grams
    )
    all_bands = bands * band_groups
    col_width = all_bands // ga_count
    blocks = full_matrix.reshape(2, band_groups, bands, ga_count, col_width)
    blocks = blocks.transpose(1, 3, 0, 2, 4).reshape(
        band_groups * ga_count, 2, bands, col_width
    )
    subspace = lax.all_to_all(blocks, ("band", "ga"), 0, 0, tiled=True).sum(0)

    place, subspace = lax.optimization_barrier((place, subspace))
    applied_waves = unpack(returned[1], place, applied_waves, half, bands, planes)
    return (applied_waves, subspace)


def solution(mesh):
    placed = (
        P(None, "band", None, "ga"),
        P("ga", None),
        P(("band", "ga")),
        P(None, ("band", "ga")),
        P(("band", "ga"), None),
    )
    return jax.shard_map(
        shards,
        mesh=mesh,
        in_specs=placed,
        out_specs=(P(None, "band", None, "ga"), P(None, "band", "ga")),
        check_vma=False,
    )
```

```python
import functools

import jax
import jax.numpy as jnp
from jax import lax
from jax.experimental import pallas as pl
from jax.experimental.pallas import tpu as pltpu
from jax.sharding import PartitionSpec as P

NX = 384
NY = 384
LANES = 128
UNIT = 48

width_cells = 1.5


def tables(indices):
    length = indices.shape[0]
    phases = indices[:, None] * indices[None, :] % length
    angles = phases.astype(jnp.float32) * (2.0 * jnp.pi / length)
    factor = 1.0 / jnp.sqrt(jnp.float32(length))
    return (
        (jnp.cos(angles) * factor).astype(jnp.bfloat16),
        (jnp.sin(angles) * factor).astype(jnp.bfloat16),
    )


def gaussian(distance):
    return jnp.exp(-distance * distance / (2.0 * width_cells * width_cells))


def frequency(indices, length):
    return jnp.where(indices < length // 2, indices, indices - length).astype(jnp.float32)


def dot(left, right):
    return jnp.dot(left, right, preferred_element_type=jnp.float32)


def step_of(count):
    return 1 if count % 2 else 2


def lasting(microseconds):
    return pl.CostEstimate(
        flops=0, bytes_accessed=int(microseconds * 3.69e6), transcendentals=0
    )


def pack_body(place, *refs):
    halves = len(refs) - 1 - refs[-1].shape[0]
    sources, messages, held = refs[:halves], refs[halves:-1], refs[-1]
    groups, count, rows, _ = held.shape
    planes = groups // halves
    for h, source in enumerate(sources):
        for i in range(count):
            split = source[0, i].reshape(planes, rows, NY)
            for p in range(planes):
                held[p * halves + h, i] = split[p]
    for s, message in enumerate(messages):
        message[0] = held[place[0] ^ s]


def pack(waves, place, first, count, rows, groups):
    planes = waves.shape[2]
    halves = groups // planes
    own = waves.shape[1] // halves
    return pl.pallas_call(
        pack_body,
        grid=(2, 1),
        in_specs=[pl.BlockSpec(memory_space=pltpu.SMEM)]
        + [
            pl.BlockSpec(
                (1, count, planes, rows * NY),
                functools.partial(block_at, (h * own + first) // count),
            )
            for h in range(halves)
        ],
        out_specs=[pl.BlockSpec((1, count, rows, NY), lambda c, n: (c, n, 0, 0))] * groups,
        out_shape=[jax.ShapeDtypeStruct((2, count, rows, NY), jnp.bfloat16)] * groups,
        scratch_shapes=[pltpu.VMEM((groups, count, rows, NY), jnp.bfloat16)],
        compiler_params=pltpu.CompilerParams(vmem_limit_bytes=56 << 20),
        cost_estimate=lasting(0.01),
        name="pack_planes",
    )(place, *[waves] * halves)


def block_at(base, c, n):
    return (c, base + n, 0, 0)


def mix_waves_body(w_ref, z_ref, mixed):
    _, bands, planes, width = w_ref.shape
    rows = width // NY
    per = 2 * bands
    for c in range(2):
        for n in range(bands):
            wide = w_ref[c, n].reshape(planes, rows, NY).astype(jnp.float32)
            for p in range(planes):
                at = pl.ds(p * rows * per + c * bands + n, rows, stride=per)
                for t in range(NY // LANES):
                    mixed[t, at, :] = wide[p, :, t * LANES : (t + 1) * LANES]
    for t in range(NY // LANES):
        z_ref[0, :, t * LANES : (t + 1) * LANES] = mixed[t].astype(jnp.bfloat16)


def mix_waves(waves, rows, shares):
    _, bands, planes, _ = waves.shape
    own = rows // shares
    depth = planes * own * 2 * bands
    return pl.pallas_call(
        mix_waves_body,
        grid=(shares,),
        in_specs=[pl.BlockSpec((2, bands, planes, own * NY), lambda d: (0, 0, 0, d))],
        out_specs=pl.BlockSpec((1, depth, NY), lambda d: (d, 0, 0)),
        out_shape=jax.ShapeDtypeStruct((shares, depth, NY), jnp.bfloat16),
        scratch_shapes=[pltpu.VMEM((NY // LANES, depth, LANES), jnp.float32)],
        compiler_params=pltpu.CompilerParams(vmem_limit_bytes=56 << 20),
        cost_estimate=lasting(0.01),
        name="mix_waves",
    )(waves)


def mix_space_body(s_ref, *refs):
    z_ref = refs[-1]
    bands, _, rows, _ = s_ref.shape
    size = 2 * bands * UNIT
    to = lax.broadcasted_iota(jnp.int32, (size, size), 0)
    at = lax.broadcasted_iota(jnp.int32, (size, size), 1)
    band, part, row = at // (2 * UNIT), at // UNIT % 2, at % UNIT
    chosen = (to == row * 2 * bands + part * bands + band).astype(jnp.bfloat16)
    shares, _, depth, _ = z_ref.shape
    each = shares * UNIT // rows
    for unit in range(rows // UNIT):
        cut = slice(unit * UNIT, (unit + 1) * UNIT)
        stacked = jnp.concatenate(
            [s_ref[n, c, cut] for n in range(bands) for c in range(2)], axis=0
        )
        mixed = dot(chosen, stacked).astype(jnp.bfloat16)
        z_ref[unit * each : (unit + 1) * each, 0] = mixed.reshape(each, depth, NY)


def mix_space(in_space, part, base, shares):
    bands = in_space.shape[0]
    own = NX // shares
    depth = own * 2 * bands
    rows = 2 * UNIT
    in_specs = [pl.BlockSpec((bands, 2, rows, NY), lambda d: (0, 0, d, 0))]
    operands = [in_space]
    aliases = {}
    if base is not None:
        in_specs.append(pl.BlockSpec(memory_space=pl.ANY))
        operands.append(base)
        aliases = {1: 0}
    return pl.pallas_call(
        mix_space_body,
        grid=(NX // rows,),
        in_specs=in_specs,
        out_specs=pl.BlockSpec((rows // own, 1, depth, NY), lambda d: (d, part, 0, 0)),
        out_shape=jax.ShapeDtypeStruct((shares, 2, depth, NY), jnp.bfloat16),
        input_output_aliases=aliases,
        compiler_params=pltpu.CompilerParams(vmem_limit_bytes=56 << 20),
        cost_estimate=lasting(0.01),
        name="mix_space",
    )(*operands)


def unpack_body(groups, place, *refs):
    messages, o_ref, held = refs[:groups], refs[-2], refs[-1]
    halves, planes, count, rows, _ = held.shape
    for s, message in enumerate(messages):
        source = place[0] ^ s
        held[lax.rem(source, halves), source // halves] = message[0]
    half = pl.program_id(1)
    for i in range(count):
        o_ref[0, i] = held[half, :, i].reshape(planes, rows * NY)


def unpack(messages, place, base, first, bands, planes):
    groups = len(messages)
    _, count, rows, _ = messages[0].shape
    halves = groups // planes
    step = step_of(count)
    own = bands // halves
    in_specs = [pl.BlockSpec(memory_space=pltpu.SMEM)] + [
        pl.BlockSpec((1, step, rows, NY), lambda c, h, n: (c, n, 0, 0))
    ] * groups
    operands = [place, *messages]
    aliases = {}
    if base is not None:
        in_specs.append(pl.BlockSpec(memory_space=pl.ANY))
        operands.append(base)
        aliases = {groups + 1: 0}
    return pl.pallas_call(
        functools.partial(unpack_body, groups),
        grid=(2, halves, count // step),
        in_specs=in_specs,
        out_specs=pl.BlockSpec(
            (1, step, planes, rows * NY), lambda c, h, n: (c, (h * own + first) // step + n, 0, 0)
        ),
        out_shape=jax.ShapeDtypeStruct((2, bands, planes, rows * NY), jnp.bfloat16),
        scratch_shapes=[pltpu.VMEM((halves, planes, step, rows, NY), jnp.bfloat16)],
        input_output_aliases=aliases,
        compiler_params=pltpu.CompilerParams(vmem_limit_bytes=56 << 20),
        cost_estimate=lasting(1.2 * count),
        name="unpack_planes",
    )(*operands)


def forward_body(groups, place, *refs):
    messages, (f_ref, b_ref, s_ref, held) = refs[:groups], refs[groups:]
    for s, message in enumerate(messages):
        held[place[0] ^ s] = message[...]
    for i in range(held.shape[2]):
        parts = [held[:, c, i].reshape(NX, NY) for c in range(2)]
        first = dot(jnp.concatenate(parts, axis=1), f_ref[...]).astype(jnp.bfloat16)
        first = jnp.concatenate([first[:, :NY], first[:, NY:]], axis=0)
        in_space = dot(b_ref[...], first).astype(jnp.bfloat16)
        s_ref[i, 0] = in_space[:NX]
        s_ref[i, 1] = in_space[NX:]


def forward(messages, place, forth, back):
    groups = len(messages)
    _, bands, rows, _ = messages[0].shape
    step = step_of(bands)
    square = pl.BlockSpec((2 * NX, 2 * NX), lambda n: (0, 0))
    return pl.pallas_call(
        functools.partial(forward_body, groups),
        grid=(bands // step,),
        in_specs=[pl.BlockSpec(memory_space=pltpu.SMEM)]
        + [pl.BlockSpec((2, step, rows, NY), lambda n: (0, n, 0, 0))] * groups
        + [square, square],
        out_specs=pl.BlockSpec((step, 2, NX, NY), lambda n: (n, 0, 0, 0)),
        out_shape=jax.ShapeDtypeStruct((bands, 2, NX, NY), jnp.bfloat16),
        scratch_shapes=[pltpu.VMEM((groups, 2, step, rows, NY), jnp.bfloat16)],
        compiler_params=pltpu.CompilerParams(vmem_limit_bytes=56 << 20),
        cost_estimate=lasting(0.01),
        name="forward",
    )(place, *messages, forth, back)


def inverse_body(groups, place, *refs):
    messages, (s_ref, v_ref, f_ref, b_ref) = refs[:groups], refs[groups : groups + 4]
    held = refs[-1]
    results = refs[-1 - groups : -1]
    rows = held.shape[3]
    freq_x = frequency(lax.broadcasted_iota(jnp.int32, (NX, 1), 0), NX)
    freq_y = frequency(lax.broadcasted_iota(jnp.int32, (1, NY), 1), NY)
    kinetic = 2.0 * (freq_x * freq_x / (NX * NX) + freq_y * freq_y / (NY * NY))
    for s, message in enumerate(messages):
        held[place[0] ^ s] = message[...]
    for i in range(held.shape[2]):
        weighted = jnp.concatenate(
            [v_ref[...] * s_ref[i, c].astype(jnp.float32) for c in range(2)], axis=0
        ).astype(jnp.bfloat16)
        back = dot(f_ref[...], weighted).astype(jnp.bfloat16)
        recip = dot(jnp.concatenate([back[:NX], back[NX:]], axis=1), b_ref[...])
        for c in range(2):
            wide = held[:, c, i].reshape(NX, NY).astype(jnp.float32)
            applied = kinetic * wide + recip[:, c * NY : (c + 1) * NY]
            held[:, c, i] = applied.astype(jnp.bfloat16).reshape(groups, rows, NY)
    for s, result in enumerate(results):
        result[...] = held[place[0] ^ s]


def inverse(messages, base, bands, place, in_space, potential, forth, back):
    groups = len(messages)
    rows = messages[0].shape[2]
    shape = (2, bands, rows, NY)
    step = 1 if base % 2 else step_of(bands)
    square = pl.BlockSpec((2 * NX, 2 * NX), lambda n: (0, 0))
    return pl.pallas_call(
        functools.partial(inverse_body, groups),
        grid=(bands // step,),
        in_specs=[pl.BlockSpec(memory_space=pltpu.SMEM)]
        + [pl.BlockSpec((2, step, rows, NY), lambda n: (0, base // step + n, 0, 0))] * groups
        + [
            pl.BlockSpec((step, 2, NX, NY), lambda n: (base // step + n, 0, 0, 0)),
            pl.BlockSpec((NX, NY), lambda n: (0, 0)),
            square,
            square,
        ],
        out_specs=[pl.BlockSpec((2, step, rows, NY), lambda n: (0, n, 0, 0))] * groups,
        out_shape=[jax.ShapeDtypeStruct(shape, jnp.bfloat16)] * groups,
        scratch_shapes=[pltpu.VMEM((groups, 2, step, rows, NY), jnp.bfloat16)],
        compiler_params=pltpu.CompilerParams(vmem_limit_bytes=56 << 20),
        cost_estimate=lasting(0.01),
        name="inverse",
    )(place, *messages, in_space, potential, forth, back)


def overlap_body(scale, per, z_ref, w_ref, *refs):
    o_ref, total = refs[-2:]
    shares, parts, _, _ = z_ref.shape
    bands = per // 2
    total[...] = jnp.zeros_like(total)
    pieces = [(d, h) for d in range(shares) for h in range(parts)]

    @pl.loop(0, w_ref.shape[0] // 2)
    def _(pair):
        plain, scaled = [], []
        at = pl.multiple_of(pair * 2 * per, 2 * per)
        both = [z_ref[d, h, pl.ds(at, 2 * per), :].astype(jnp.float32) for d, h in pieces]
        for k in range(2):
            wide = jnp.concatenate([rows[k * per : (k + 1) * per] for rows in both], axis=0)
            plain.append(wide.astype(jnp.bfloat16))
            scaled.append((wide * w_ref[pl.ds(pair * 2 + k, 1), :]).astype(jnp.bfloat16))
        total[...] += lax.dot_general(
            jnp.concatenate(plain, axis=1),
            jnp.concatenate(scaled, axis=1),
            (((1,), (1,)), ((), ())),
            preferred_element_type=jnp.float32,
        )

    size = total.shape[0]
    half = size // 2
    to = lax.broadcasted_iota(jnp.int32, (size, size), 0)
    at = lax.broadcasted_iota(jnp.int32, (size, size), 1)
    order = at % per // bands * half + at // per * bands + at % bands
    chosen = (to == order).astype(jnp.float32)
    grams = jnp.dot(
        chosen, total[...], precision=lax.Precision.HIGHEST, preferred_element_type=jnp.float32
    )
    grams = lax.dot_general(
        grams,
        chosen,
        (((1,), (1,)), ((), ())),
        precision=lax.Precision.HIGHEST,
        preferred_element_type=jnp.float32,
    )
    real = (grams[:half, :half] + grams[half:, half:]) * scale
    imaginary = (grams[:half, half:] - grams[half:, :half]) * scale
    if len(refs) == 3:
        real, imaginary = real + refs[0][0], imaginary + refs[0][1]
    o_ref[0] = real
    o_ref[1] = imaginary


def overlap(pieces, weights, per, scale, before=None):
    shares, parts, _, _ = pieces.shape
    size = shares * parts * per
    whole = pl.BlockSpec(memory_space=pltpu.VMEM)
    operands = [pieces, weights] + ([] if before is None else [before])
    return pl.pallas_call(
        functools.partial(overlap_body, scale, per),
        in_specs=[whole] * len(operands),
        out_specs=whole,
        out_shape=jax.ShapeDtypeStruct((2, size // 2, size // 2), jnp.float32),
        scratch_shapes=[pltpu.VMEM((size, size), jnp.float32)],
        compiler_params=pltpu.CompilerParams(vmem_limit_bytes=56 << 20),
        cost_estimate=lasting(8.0),
        name="overlap",
    )(*operands)


def shifted(messages):
    groups = len(messages)
    return [
        lax.ppermute(message, "ga", [(i, i ^ s) for i in range(groups)]) if s else message
        for s, message in enumerate(messages)
    ]


def split(wide):
    high = wide.astype(jnp.bfloat16)
    return high, (wide - high.astype(jnp.float32)).astype(jnp.bfloat16)


def charges_body(planes, slab_rows, place, c_ref, i_ref, o_ref, total):
    first = place[0].astype(jnp.float32)
    plane = place[1].astype(jnp.float32)
    own_x = lax.broadcasted_iota(jnp.int32, (LANES, 1), 0).astype(jnp.float32) + first
    cells_y = lax.broadcasted_iota(jnp.int32, (NY, 1), 0)
    slab_y = (cells_y // slab_rows).astype(jnp.float32)
    cells_y = cells_y.astype(jnp.float32)
    total[...] = jnp.zeros_like(total)

    @pl.loop(0, c_ref.shape[0] // 2)
    def _(pair):
        lefts, rights = [], []
        for k in range(2):
            along_u, along_v, along_w, amount, slab = [
                c_ref[pair * 2 + k, row : row + 1, :] for row in range(5)
            ]
            weight = amount * gaussian(plane - planes * along_w)
            x_high, x_low = split(gaussian(own_x - NX * along_u) * weight)
            kernel_y = gaussian(cells_y - (slab * slab_rows + slab_rows * along_v))
            y_high, y_low = split(jnp.where(slab_y == slab, kernel_y, 0.0))
            lefts += [y_low, y_high, y_high]
            rights += [x_high, x_low, x_high]
        total[...] += lax.dot_general(
            jnp.concatenate(lefts, axis=1),
            jnp.concatenate(rights, axis=1),
            (((1,), (1,)), ((), ())),
            preferred_element_type=jnp.float32,
        )

    o_ref[...] = i_ref[...] + total[...].T[: o_ref.shape[0]]


def potential_message(ionic_field, point_charge, charge_place, charge_slab, planes, halves):
    ga_count = lax.axis_size("ga")
    band_groups = lax.axis_size("band")
    devices = band_groups * ga_count
    slab_rows = NY // ga_count
    share = NX // band_groups
    piece = share * slab_rows // band_groups
    atoms = point_charge.shape[0]
    spare = -(-piece // atoms)
    band_at = lax.axis_index("band")
    charges = jnp.concatenate(
        [charge_place, point_charge[None], charge_slab[:, 0][None].astype(jnp.float32)], axis=0
    )
    ionic = ionic_field.T.reshape(planes, band_groups, band_groups, piece)
    ionic = lax.dynamic_index_in_dim(ionic, band_at, 2, keepdims=False)
    ionic = jnp.broadcast_to(
        ionic.transpose(1, 0, 2)[:, :, None], (band_groups, planes, halves, piece)
    )
    ionic = jnp.pad(ionic.reshape(devices, piece), ((0, 0), (0, spare * atoms - piece)))
    return jnp.concatenate(
        [
            jnp.broadcast_to(charges[None], (devices, 5, atoms)),
            ionic.reshape(devices, spare, atoms),
        ],
        axis=1,
    )


def own_share(message, planes, halves):
    ga_count = lax.axis_size("ga")
    band_groups = lax.axis_size("band")
    slab_rows = NY // ga_count
    share = NX // band_groups
    piece = share * slab_rows // band_groups
    atoms = message.shape[2]
    spare = message.shape[1] - 5
    band_at = lax.axis_index("band")
    ionic = message[:, 5:].reshape(band_groups, ga_count, spare * atoms)[:, :, :piece]
    ionic = ionic.transpose(1, 0, 2).reshape(ga_count, share, slab_rows)
    ionic = ionic.transpose(1, 0, 2).reshape(share, NY)
    place = jnp.stack([band_at * share, lax.axis_index("ga") // halves]).astype(jnp.int32)
    return pl.pallas_call(
        functools.partial(charges_body, planes, slab_rows),
        in_specs=[
            pl.BlockSpec(memory_space=pltpu.SMEM),
            pl.BlockSpec(memory_space=pltpu.VMEM),
            pl.BlockSpec(memory_space=pltpu.VMEM),
        ],
        out_specs=pl.BlockSpec(memory_space=pltpu.VMEM),
        out_shape=jax.ShapeDtypeStruct((share, NY), jnp.float32),
        scratch_shapes=[pltpu.VMEM((NY, LANES), jnp.float32)],
        compiler_params=pltpu.CompilerParams(vmem_limit_bytes=56 << 20),
        cost_estimate=lasting(0.01),
        name="charge_potential",
    )(place, message, ionic)


def shards(waves, ionic_field, point_charge, charge_place, charge_slab):
    ga_count = lax.axis_size("ga")
    band_groups = lax.axis_size("band")
    bands = waves.shape[1]
    planes = waves.shape[2]
    rows = NX // ga_count
    halves = ga_count // planes
    own_bands = bands // halves
    half = own_bands // 2
    chunks = [(0, half), (half, half)]
    per = 2 * bands
    pairs = [[p * halves + h for h in range(halves)] for p in range(planes)]
    ga_at, band_at = lax.axis_index("ga"), lax.axis_index("band")
    place = ga_at.astype(jnp.int32)[None]

    packed = [pack(waves, place, first, count, rows, ga_count) for first, count in chunks]
    message = potential_message(
        ionic_field, point_charge, charge_place, charge_slab, planes, halves
    )

    arrived = [shifted(packed[0])]
    message = lax.all_to_all(message, ("band", "ga"), 0, 0, tiled=True)
    mixed = mix_waves(waves, rows, band_groups)
    message, packed[1], mixed = lax.optimization_barrier((message, packed[1], mixed))
    own_potential = own_share(message, planes, halves)
    copies = jnp.broadcast_to(own_potential[None], (band_groups,) + own_potential.shape)
    potential = lax.all_to_all(copies, "band", 0, 0, tiled=True).reshape(NX, NY)
    cells = jnp.arange(NX, dtype=jnp.int32)
    arrived[0], potential, packed[1], mixed, cells = lax.optimization_barrier(
        (arrived[0], potential, packed[1], mixed, cells)
    )

    arrived.append(shifted(packed[1]))
    met_waves = lax.all_to_all(mixed, "band", 0, 0, tiled=True)
    cosine, sine = tables(cells)
    forth = jnp.concatenate(
        [jnp.concatenate([cosine, sine], axis=1), jnp.concatenate([-sine, cosine], axis=1)], axis=0
    )
    back = jnp.concatenate(
        [jnp.concatenate([cosine, -sine], axis=1), jnp.concatenate([sine, cosine], axis=1)], axis=0
    )
    in_space = [forward(arrived[0], place, forth, back)]
    shares = band_groups * halves
    mixed = mix_space(in_space[0], 0, None, shares)
    result = inverse(arrived[0], 0, half, place, in_space[0], potential, forth, back)
    arrived[1], met_waves, result, mixed = lax.optimization_barrier(
        (arrived[1], met_waves, result, mixed)
    )

    returned = [shifted(result)]
    in_space.append(forward(arrived[1], place, forth, back))
    mixed = mix_space(in_space[1], 1, mixed, shares)
    middle = ga_count // 2
    mixed, returned[0][middle] = lax.optimization_barrier((mixed, returned[0][middle]))
    if halves > 1:
        mixed = mixed.reshape(band_groups, halves, -1, NY)
        mixed = lax.all_to_all(mixed, "ga", 1, 1, axis_index_groups=pairs, tiled=True)
    met_space = lax.all_to_all(mixed, "band", 0, 0, tiled=True)
    if halves > 1:
        met_space = met_space.reshape(band_groups, halves, 2, -1, 2, half, NY)
        met_space = met_space.transpose(0, 3, 4, 1, 2, 5, 6)
        met_space = met_space.reshape(band_groups, 1, -1, NY)
    space_weights = own_potential
    if halves > 1:
        space_weights = lax.dynamic_slice_in_dim(
            own_potential, ga_at % halves * (NX // band_groups // halves),
            NX // band_groups // halves, 0,
        )

    share = rows // band_groups
    own_x = ga_at * rows + band_at * share + jnp.arange(share, dtype=jnp.int32)
    freq_x, freq_y = frequency(own_x, NX), frequency(jnp.arange(NY, dtype=jnp.int32), NY)
    kinetic = 2.0 * (
        freq_x[:, None] * freq_x[:, None] / (NX * NX)
        + freq_y[None, :] * freq_y[None, :] / (NY * NY)
    )
    kinetic = jnp.broadcast_to(kinetic[None], (planes, share, NY)).reshape(planes * share, NY)

    scale = 1.0 / (planes * NX * NY)
    applied_waves = unpack(returned[0], place, None, 0, bands, planes)
    grams = overlap(met_waves[:, None], kinetic, per, scale)
    spectrum = (in_space[1], potential, forth, back)
    returned.append(shifted(inverse(arrived[1], 0, half - 1, place, *spectrum)))
    grams, place = lax.optimization_barrier((grams, place))
    returned.append(shifted(inverse(arrived[1], half - 1, 1, place, *spectrum)))
    grams, applied_waves = lax.optimization_barrier((grams, applied_waves))
    full_matrix = overlap(
        met_space, space_weights, per // met_space.shape[1], scale, grams
    )
    all_bands = bands * band_groups
    col_width = all_bands // ga_count
    blocks = full_matrix.reshape(2, band_groups, bands, ga_count, col_width)
    blocks = blocks.transpose(1, 3, 0, 2, 4).reshape(
        band_groups * ga_count, 2, bands, col_width
    )
    subspace = lax.all_to_all(blocks, ("band", "ga"), 0, 0, tiled=True).sum(0)

    applied_waves = unpack(returned[1], place, applied_waves, half, bands, planes)
    applied_waves = unpack(returned[2], place, applied_waves, own_bands - 1, bands, planes)
    return (applied_waves, subspace)


def solution(mesh):
    placed = (
        P(None, "band", None, "ga"),
        P("ga", None),
        P(("band", "ga")),
        P(None, ("band", "ga")),
        P(("band", "ga"), None),
    )
    return jax.shard_map(
        shards,
        mesh=mesh,
        in_specs=placed,
        out_specs=(P(None, "band", None, "ga"), P(None, "band", "ga")),
        check_vma=False,
    )
```

```python
import functools

import jax
import jax.numpy as jnp
from jax import lax
from jax.experimental import pallas as pl
from jax.experimental.pallas import tpu as pltpu
from jax.sharding import PartitionSpec as P

NX = 384
NY = 384
LANES = 128
UNIT = 48

width_cells = 1.5


def tables(indices):
    length = indices.shape[0]
    phases = indices[:, None] * indices[None, :] % length
    angles = phases.astype(jnp.float32) * (2.0 * jnp.pi / length)
    factor = 1.0 / jnp.sqrt(jnp.float32(length))
    return (
        (jnp.cos(angles) * factor).astype(jnp.bfloat16),
        (jnp.sin(angles) * factor).astype(jnp.bfloat16),
    )


def gaussian(distance):
    return jnp.exp(-distance * distance / (2.0 * width_cells * width_cells))


def frequency(indices, length):
    return jnp.where(indices < length // 2, indices, indices - length).astype(jnp.float32)


def dot(left, right):
    return jnp.dot(left, right, preferred_element_type=jnp.float32)


def step_of(count):
    return 1 if count % 2 else 2


def lasting(microseconds):
    return pl.CostEstimate(
        flops=0, bytes_accessed=int(microseconds * 3.69e6), transcendentals=0
    )


def pack_body(place, *refs):
    halves = len(refs) - 1 - refs[-1].shape[0]
    sources, messages, held = refs[:halves], refs[halves:-1], refs[-1]
    groups, count, rows, _ = held.shape
    planes = groups // halves
    for h, source in enumerate(sources):
        for i in range(count):
            split = source[0, i].reshape(planes, rows, NY)
            for p in range(planes):
                held[p * halves + h, i] = split[p]
    for s, message in enumerate(messages):
        message[0] = held[place[0] ^ s]


def pack(waves, place, first, count, rows, groups):
    planes = waves.shape[2]
    halves = groups // planes
    own = waves.shape[1] // halves
    return pl.pallas_call(
        pack_body,
        grid=(2, 1),
        in_specs=[pl.BlockSpec(memory_space=pltpu.SMEM)]
        + [
            pl.BlockSpec(
                (1, count, planes, rows * NY),
                functools.partial(block_at, (h * own + first) // count),
            )
            for h in range(halves)
        ],
        out_specs=[pl.BlockSpec((1, count, rows, NY), lambda c, n: (c, n, 0, 0))] * groups,
        out_shape=[jax.ShapeDtypeStruct((2, count, rows, NY), jnp.bfloat16)] * groups,
        scratch_shapes=[pltpu.VMEM((groups, count, rows, NY), jnp.bfloat16)],
        compiler_params=pltpu.CompilerParams(vmem_limit_bytes=56 << 20),
        cost_estimate=lasting(0.01),
        name="pack_planes",
    )(place, *[waves] * halves)


def block_at(base, c, n):
    return (c, base + n, 0, 0)


def mix_waves_body(w_ref, z_ref, mixed):
    _, bands, planes, width = w_ref.shape
    rows = width // NY
    per = 2 * bands
    for c in range(2):
        for n in range(bands):
            wide = w_ref[c, n].reshape(planes, rows, NY).astype(jnp.float32)
            for p in range(planes):
                at = pl.ds(p * rows * per + c * bands + n, rows, stride=per)
                for t in range(NY // LANES):
                    mixed[t, at, :] = wide[p, :, t * LANES : (t + 1) * LANES]
    for t in range(NY // LANES):
        z_ref[0, :, t * LANES : (t + 1) * LANES] = mixed[t].astype(jnp.bfloat16)


def mix_waves(waves, rows, shares):
    _, bands, planes, _ = waves.shape
    own = rows // shares
    depth = planes * own * 2 * bands
    return pl.pallas_call(
        mix_waves_body,
        grid=(shares,),
        in_specs=[pl.BlockSpec((2, bands, planes, own * NY), lambda d: (0, 0, 0, d))],
        out_specs=pl.BlockSpec((1, depth, NY), lambda d: (d, 0, 0)),
        out_shape=jax.ShapeDtypeStruct((shares, depth, NY), jnp.bfloat16),
        scratch_shapes=[pltpu.VMEM((NY // LANES, depth, LANES), jnp.float32)],
        compiler_params=pltpu.CompilerParams(vmem_limit_bytes=56 << 20),
        cost_estimate=lasting(0.01),
        name="mix_waves",
    )(waves)


def mix_space_body(s_ref, *refs):
    z_ref = refs[-1]
    bands, _, rows, _ = s_ref.shape
    size = 2 * bands * UNIT
    to = lax.broadcasted_iota(jnp.int32, (size, size), 0)
    at = lax.broadcasted_iota(jnp.int32, (size, size), 1)
    band, part, row = at // (2 * UNIT), at // UNIT % 2, at % UNIT
    chosen = (to == row * 2 * bands + part * bands + band).astype(jnp.bfloat16)
    shares, _, depth, _ = z_ref.shape
    each = shares * UNIT // rows
    for unit in range(rows // UNIT):
        cut = slice(unit * UNIT, (unit + 1) * UNIT)
        stacked = jnp.concatenate(
            [s_ref[n, c, cut] for n in range(bands) for c in range(2)], axis=0
        )
        mixed = dot(chosen, stacked).astype(jnp.bfloat16)
        z_ref[unit * each : (unit + 1) * each, 0] = mixed.reshape(each, depth, NY)


def mix_space(in_space, part, base, shares):
    bands = in_space.shape[0]
    own = NX // shares
    depth = own * 2 * bands
    rows = 2 * UNIT
    in_specs = [pl.BlockSpec((bands, 2, rows, NY), lambda d: (0, 0, d, 0))]
    operands = [in_space]
    aliases = {}
    if base is not None:
        in_specs.append(pl.BlockSpec(memory_space=pl.ANY))
        operands.append(base)
        aliases = {1: 0}
    return pl.pallas_call(
        mix_space_body,
        grid=(NX // rows,),
        in_specs=in_specs,
        out_specs=pl.BlockSpec((rows // own, 1, depth, NY), lambda d: (d, part, 0, 0)),
        out_shape=jax.ShapeDtypeStruct((shares, 2, depth, NY), jnp.bfloat16),
        input_output_aliases=aliases,
        compiler_params=pltpu.CompilerParams(vmem_limit_bytes=56 << 20),
        cost_estimate=lasting(0.01),
        name="mix_space",
    )(*operands)


def unpack_body(groups, place, *refs):
    messages, o_ref, held = refs[:groups], refs[-2], refs[-1]
    halves, planes, count, rows, _ = held.shape
    for s, message in enumerate(messages):
        source = place[0] ^ s
        held[lax.rem(source, halves), source // halves] = message[0]
    half = pl.program_id(1)
    for i in range(count):
        o_ref[0, i] = held[half, :, i].reshape(planes, rows * NY)


def unpack(messages, place, base, first, bands, planes):
    groups = len(messages)
    _, count, rows, _ = messages[0].shape
    halves = groups // planes
    step = step_of(count)
    own = bands // halves
    in_specs = [pl.BlockSpec(memory_space=pltpu.SMEM)] + [
        pl.BlockSpec((1, step, rows, NY), lambda c, h, n: (c, n, 0, 0))
    ] * groups
    operands = [place, *messages]
    aliases = {}
    if base is not None:
        in_specs.append(pl.BlockSpec(memory_space=pl.ANY))
        operands.append(base)
        aliases = {groups + 1: 0}
    return pl.pallas_call(
        functools.partial(unpack_body, groups),
        grid=(2, halves, count // step),
        in_specs=in_specs,
        out_specs=pl.BlockSpec(
            (1, step, planes, rows * NY), lambda c, h, n: (c, (h * own + first) // step + n, 0, 0)
        ),
        out_shape=jax.ShapeDtypeStruct((2, bands, planes, rows * NY), jnp.bfloat16),
        scratch_shapes=[pltpu.VMEM((halves, planes, step, rows, NY), jnp.bfloat16)],
        input_output_aliases=aliases,
        compiler_params=pltpu.CompilerParams(vmem_limit_bytes=56 << 20),
        cost_estimate=lasting(1.2 * count),
        name="unpack_planes",
    )(*operands)


def forward_body(groups, place, *refs):
    messages, (f_ref, b_ref, s_ref, held) = refs[:groups], refs[groups:]
    for s, message in enumerate(messages):
        held[place[0] ^ s] = message[...]
    for i in range(held.shape[2]):
        parts = [held[:, c, i].reshape(NX, NY) for c in range(2)]
        first = dot(jnp.concatenate(parts, axis=1), f_ref[...]).astype(jnp.bfloat16)
        first = jnp.concatenate([first[:, :NY], first[:, NY:]], axis=0)
        in_space = dot(b_ref[...], first).astype(jnp.bfloat16)
        s_ref[i, 0] = in_space[:NX]
        s_ref[i, 1] = in_space[NX:]


def forward(messages, place, forth, back):
    groups = len(messages)
    _, bands, rows, _ = messages[0].shape
    step = step_of(bands)
    square = pl.BlockSpec((2 * NX, 2 * NX), lambda n: (0, 0))
    return pl.pallas_call(
        functools.partial(forward_body, groups),
        grid=(bands // step,),
        in_specs=[pl.BlockSpec(memory_space=pltpu.SMEM)]
        + [pl.BlockSpec((2, step, rows, NY), lambda n: (0, n, 0, 0))] * groups
        + [square, square],
        out_specs=pl.BlockSpec((step, 2, NX, NY), lambda n: (n, 0, 0, 0)),
        out_shape=jax.ShapeDtypeStruct((bands, 2, NX, NY), jnp.bfloat16),
        scratch_shapes=[pltpu.VMEM((groups, 2, step, rows, NY), jnp.bfloat16)],
        compiler_params=pltpu.CompilerParams(vmem_limit_bytes=56 << 20),
        cost_estimate=lasting(0.01),
        name="forward",
    )(place, *messages, forth, back)


def inverse_body(groups, place, *refs):
    messages, (s_ref, v_ref, f_ref, b_ref) = refs[:groups], refs[groups : groups + 4]
    held = refs[-1]
    results = refs[-1 - groups : -1]
    rows = held.shape[3]
    freq_x = frequency(lax.broadcasted_iota(jnp.int32, (NX, 1), 0), NX)
    freq_y = frequency(lax.broadcasted_iota(jnp.int32, (1, NY), 1), NY)
    kinetic = 2.0 * (freq_x * freq_x / (NX * NX) + freq_y * freq_y / (NY * NY))
    for s, message in enumerate(messages):
        held[place[0] ^ s] = message[...]
    for i in range(held.shape[2]):
        weighted = jnp.concatenate(
            [v_ref[...] * s_ref[i, c].astype(jnp.float32) for c in range(2)], axis=0
        ).astype(jnp.bfloat16)
        back = dot(f_ref[...], weighted).astype(jnp.bfloat16)
        recip = dot(jnp.concatenate([back[:NX], back[NX:]], axis=1), b_ref[...])
        for c in range(2):
            wide = held[:, c, i].reshape(NX, NY).astype(jnp.float32)
            applied = kinetic * wide + recip[:, c * NY : (c + 1) * NY]
            held[:, c, i] = applied.astype(jnp.bfloat16).reshape(groups, rows, NY)
    for s, result in enumerate(results):
        result[...] = held[place[0] ^ s]


def inverse(messages, base, bands, place, in_space, potential, forth, back):
    groups = len(messages)
    rows = messages[0].shape[2]
    shape = (2, bands, rows, NY)
    step = 1 if base % 2 else step_of(bands)
    square = pl.BlockSpec((2 * NX, 2 * NX), lambda n: (0, 0))
    return pl.pallas_call(
        functools.partial(inverse_body, groups),
        grid=(bands // step,),
        in_specs=[pl.BlockSpec(memory_space=pltpu.SMEM)]
        + [pl.BlockSpec((2, step, rows, NY), lambda n: (0, base // step + n, 0, 0))] * groups
        + [
            pl.BlockSpec((step, 2, NX, NY), lambda n: (base // step + n, 0, 0, 0)),
            pl.BlockSpec((NX, NY), lambda n: (0, 0)),
            square,
            square,
        ],
        out_specs=[pl.BlockSpec((2, step, rows, NY), lambda n: (0, n, 0, 0))] * groups,
        out_shape=[jax.ShapeDtypeStruct(shape, jnp.bfloat16)] * groups,
        scratch_shapes=[pltpu.VMEM((groups, 2, step, rows, NY), jnp.bfloat16)],
        compiler_params=pltpu.CompilerParams(vmem_limit_bytes=56 << 20),
        cost_estimate=lasting(0.01),
        name="inverse",
    )(place, *messages, in_space, potential, forth, back)


def overlap_body(scale, per, z_ref, w_ref, *refs):
    o_ref, total = refs[-2:]
    shares, parts, _, _ = z_ref.shape
    bands = per // 2
    total[...] = jnp.zeros_like(total)
    pieces = [(d, h) for d in range(shares) for h in range(parts)]

    @pl.loop(0, w_ref.shape[0] // 2)
    def _(pair):
        plain, scaled = [], []
        at = pl.multiple_of(pair * 2 * per, 2 * per)
        both = [z_ref[d, h, pl.ds(at, 2 * per), :].astype(jnp.float32) for d, h in pieces]
        for k in range(2):
            wide = jnp.concatenate([rows[k * per : (k + 1) * per] for rows in both], axis=0)
            plain.append(wide.astype(jnp.bfloat16))
            scaled.append((wide * w_ref[pl.ds(pair * 2 + k, 1), :]).astype(jnp.bfloat16))
        total[...] += lax.dot_general(
            jnp.concatenate(plain, axis=1),
            jnp.concatenate(scaled, axis=1),
            (((1,), (1,)), ((), ())),
            preferred_element_type=jnp.float32,
        )

    size = total.shape[0]
    half = size // 2
    to = lax.broadcasted_iota(jnp.int32, (size, size), 0)
    at = lax.broadcasted_iota(jnp.int32, (size, size), 1)
    order = at % per // bands * half + at // per * bands + at % bands
    chosen = (to == order).astype(jnp.float32)
    grams = jnp.dot(
        chosen, total[...], precision=lax.Precision.HIGHEST, preferred_element_type=jnp.float32
    )
    grams = lax.dot_general(
        grams,
        chosen,
        (((1,), (1,)), ((), ())),
        precision=lax.Precision.HIGHEST,
        preferred_element_type=jnp.float32,
    )
    real = (grams[:half, :half] + grams[half:, half:]) * scale
    imaginary = (grams[:half, half:] - grams[half:, :half]) * scale
    if len(refs) == 3:
        real, imaginary = real + refs[0][0], imaginary + refs[0][1]
    o_ref[0] = real
    o_ref[1] = imaginary


def overlap(pieces, weights, per, scale, before=None):
    shares, parts, _, _ = pieces.shape
    size = shares * parts * per
    whole = pl.BlockSpec(memory_space=pltpu.VMEM)
    operands = [pieces, weights] + ([] if before is None else [before])
    return pl.pallas_call(
        functools.partial(overlap_body, scale, per),
        in_specs=[whole] * len(operands),
        out_specs=whole,
        out_shape=jax.ShapeDtypeStruct((2, size // 2, size // 2), jnp.float32),
        scratch_shapes=[pltpu.VMEM((size, size), jnp.float32)],
        compiler_params=pltpu.CompilerParams(vmem_limit_bytes=56 << 20),
        cost_estimate=lasting(8.0),
        name="overlap",
    )(*operands)


def shifted(messages):
    groups = len(messages)
    return [
        lax.ppermute(message, "ga", [(i, i ^ s) for i in range(groups)]) if s else message
        for s, message in enumerate(messages)
    ]


def split(wide):
    high = wide.astype(jnp.bfloat16)
    return high, (wide - high.astype(jnp.float32)).astype(jnp.bfloat16)


def charges_body(planes, slab_rows, place, c_ref, i_ref, o_ref, total):
    first = place[0].astype(jnp.float32)
    plane = place[1].astype(jnp.float32)
    own_x = lax.broadcasted_iota(jnp.int32, (LANES, 1), 0).astype(jnp.float32) + first
    cells_y = lax.broadcasted_iota(jnp.int32, (NY, 1), 0)
    slab_y = (cells_y // slab_rows).astype(jnp.float32)
    cells_y = cells_y.astype(jnp.float32)
    total[...] = jnp.zeros_like(total)

    @pl.loop(0, c_ref.shape[0] // 2)
    def _(pair):
        lefts, rights = [], []
        for k in range(2):
            along_u, along_v, along_w, amount, slab = [
                c_ref[pair * 2 + k, row : row + 1, :] for row in range(5)
            ]
            weight = amount * gaussian(plane - planes * along_w)
            x_high, x_low = split(gaussian(own_x - NX * along_u) * weight)
            kernel_y = gaussian(cells_y - (slab * slab_rows + slab_rows * along_v))
            y_high, y_low = split(jnp.where(slab_y == slab, kernel_y, 0.0))
            lefts += [y_low, y_high, y_high]
            rights += [x_high, x_low, x_high]
        total[...] += lax.dot_general(
            jnp.concatenate(lefts, axis=1),
            jnp.concatenate(rights, axis=1),
            (((1,), (1,)), ((), ())),
            preferred_element_type=jnp.float32,
        )

    o_ref[...] = (total[...] + i_ref[...]).T[: o_ref.shape[0]]


def potential_message(ionic_field, point_charge, charge_place, charge_slab, planes, halves):
    ga_count = lax.axis_size("ga")
    band_groups = lax.axis_size("band")
    devices = band_groups * ga_count
    slab_rows = NY // ga_count
    share = NX // band_groups
    piece = share * slab_rows // band_groups
    atoms = point_charge.shape[0]
    spare = -(-piece // atoms)
    band_at = lax.axis_index("band")
    charges = jnp.concatenate(
        [charge_place, point_charge[None], charge_slab[:, 0][None].astype(jnp.float32)], axis=0
    )
    own_rows = slab_rows // band_groups
    ionic = lax.dynamic_slice_in_dim(ionic_field, band_at * own_rows, own_rows, 0)
    ionic = ionic.reshape(own_rows, planes, band_groups, share).transpose(1, 2, 0, 3)
    ionic = ionic.reshape(planes, band_groups, piece)
    ionic = jnp.broadcast_to(
        ionic.transpose(1, 0, 2)[:, :, None], (band_groups, planes, halves, piece)
    )
    ionic = jnp.pad(ionic.reshape(devices, piece), ((0, 0), (0, spare * atoms - piece)))
    return jnp.concatenate(
        [
            jnp.broadcast_to(charges[None], (devices, 5, atoms)),
            ionic.reshape(devices, spare, atoms),
        ],
        axis=1,
    )


def own_share(message, planes, halves):
    ga_count = lax.axis_size("ga")
    band_groups = lax.axis_size("band")
    slab_rows = NY // ga_count
    share = NX // band_groups
    piece = share * slab_rows // band_groups
    atoms = message.shape[2]
    spare = message.shape[1] - 5
    band_at = lax.axis_index("band")
    ionic = message[:, 5:].reshape(band_groups, ga_count, spare * atoms)[:, :, :piece]
    ionic = ionic.transpose(1, 0, 2).reshape(NY, share)
    ionic = jnp.pad(ionic, ((0, 0), (0, LANES - share)))
    place = jnp.stack([band_at * share, lax.axis_index("ga") // halves]).astype(jnp.int32)
    return pl.pallas_call(
        functools.partial(charges_body, planes, slab_rows),
        in_specs=[
            pl.BlockSpec(memory_space=pltpu.SMEM),
            pl.BlockSpec(memory_space=pltpu.VMEM),
            pl.BlockSpec(memory_space=pltpu.VMEM),
        ],
        out_specs=pl.BlockSpec(memory_space=pltpu.VMEM),
        out_shape=jax.ShapeDtypeStruct((share, NY), jnp.float32),
        scratch_shapes=[pltpu.VMEM((NY, LANES), jnp.float32)],
        compiler_params=pltpu.CompilerParams(vmem_limit_bytes=56 << 20),
        cost_estimate=lasting(0.01),
        name="charge_potential",
    )(place, message, ionic)


def shards(waves, ionic_field, point_charge, charge_place, charge_slab):
    ga_count = lax.axis_size("ga")
    band_groups = lax.axis_size("band")
    bands = waves.shape[1]
    planes = waves.shape[2]
    rows = NX // ga_count
    halves = ga_count // planes
    own_bands = bands // halves
    half = own_bands // 2
    chunks = [(0, half), (half, half)]
    per = 2 * bands
    pairs = [[p * halves + h for h in range(halves)] for p in range(planes)]
    ga_at, band_at = lax.axis_index("ga"), lax.axis_index("band")
    place = ga_at.astype(jnp.int32)[None]

    packed = [pack(waves, place, first, count, rows, ga_count) for first, count in chunks]
    message = potential_message(
        ionic_field, point_charge, charge_place, charge_slab, planes, halves
    )

    arrived = [shifted(packed[0])]
    message = lax.all_to_all(message, ("band", "ga"), 0, 0, tiled=True)
    mixed = mix_waves(waves, rows, band_groups)
    message, packed[1], mixed = lax.optimization_barrier((message, packed[1], mixed))
    own_potential = own_share(message, planes, halves)
    copies = jnp.broadcast_to(own_potential[None], (band_groups,) + own_potential.shape)
    potential = lax.all_to_all(copies, "band", 0, 0, tiled=True).reshape(NX, NY)
    cells = jnp.arange(NX, dtype=jnp.int32)
    arrived[0], potential, packed[1], mixed, cells = lax.optimization_barrier(
        (arrived[0], potential, packed[1], mixed, cells)
    )

    arrived.append(shifted(packed[1]))
    met_waves = lax.all_to_all(mixed, "band", 0, 0, tiled=True)
    cosine, sine = tables(cells)
    forth = jnp.concatenate(
        [jnp.concatenate([cosine, sine], axis=1), jnp.concatenate([-sine, cosine], axis=1)], axis=0
    )
    back = jnp.concatenate(
        [jnp.concatenate([cosine, -sine], axis=1), jnp.concatenate([sine, cosine], axis=1)], axis=0
    )
    in_space = [forward(arrived[0], place, forth, back)]
    shares = band_groups * halves
    mixed = mix_space(in_space[0], 0, None, shares)
    result = inverse(arrived[0], 0, half, place, in_space[0], potential, forth, back)
    arrived[1], met_waves, result, mixed = lax.optimization_barrier(
        (arrived[1], met_waves, result, mixed)
    )

    returned = [shifted(result)]
    in_space.append(forward(arrived[1], place, forth, back))
    mixed = mix_space(in_space[1], 1, mixed, shares)
    middle = ga_count // 2
    mixed, returned[0][middle] = lax.optimization_barrier((mixed, returned[0][middle]))
    if halves > 1:
        mixed = mixed.reshape(band_groups, halves, -1, NY)
        mixed = lax.all_to_all(mixed, "ga", 1, 1, axis_index_groups=pairs, tiled=True)
    met_space = lax.all_to_all(mixed, "band", 0, 0, tiled=True)
    if halves > 1:
        met_space = met_space.reshape(band_groups, halves, 2, -1, 2, half, NY)
        met_space = met_space.transpose(0, 3, 4, 1, 2, 5, 6)
        met_space = met_space.reshape(band_groups, 1, -1, NY)
    space_weights = own_potential
    if halves > 1:
        space_weights = lax.dynamic_slice_in_dim(
            own_potential, ga_at % halves * (NX // band_groups // halves),
            NX // band_groups // halves, 0,
        )

    share = rows // band_groups
    own_x = ga_at * rows + band_at * share + jnp.arange(share, dtype=jnp.int32)
    freq_x, freq_y = frequency(own_x, NX), frequency(jnp.arange(NY, dtype=jnp.int32), NY)
    kinetic = 2.0 * (
        freq_x[:, None] * freq_x[:, None] / (NX * NX)
        + freq_y[None, :] * freq_y[None, :] / (NY * NY)
    )
    kinetic = jnp.broadcast_to(kinetic[None], (planes, share, NY)).reshape(planes * share, NY)

    scale = 1.0 / (planes * NX * NY)
    applied_waves = unpack(returned[0], place, None, 0, bands, planes)
    grams = overlap(met_waves[:, None], kinetic, per, scale)
    spectrum = (in_space[1], potential, forth, back)
    returned.append(shifted(inverse(arrived[1], 0, half - 1, place, *spectrum)))
    grams, place = lax.optimization_barrier((grams, place))
    returned.append(shifted(inverse(arrived[1], half - 1, 1, place, *spectrum)))
    grams, applied_waves = lax.optimization_barrier((grams, applied_waves))
    full_matrix = overlap(
        met_space, space_weights, per // met_space.shape[1], scale, grams
    )
    all_bands = bands * band_groups
    col_width = all_bands // ga_count
    blocks = full_matrix.reshape(2, band_groups, bands, ga_count, col_width)
    blocks = blocks.transpose(1, 3, 0, 2, 4).reshape(
        band_groups * ga_count, 2, bands, col_width
    )
    subspace = lax.all_to_all(blocks, ("band", "ga"), 0, 0, tiled=True).sum(0)

    applied_waves = unpack(returned[1], place, applied_waves, half, bands, planes)
    applied_waves = unpack(returned[2], place, applied_waves, own_bands - 1, bands, planes)
    return (applied_waves, subspace)


def solution(mesh):
    placed = (
        P(None, "band", None, "ga"),
        P("ga", None),
        P(("band", "ga")),
        P(None, ("band", "ga")),
        P(("band", "ga"), None),
    )
    return jax.shard_map(
        shards,
        mesh=mesh,
        in_specs=placed,
        out_specs=(P(None, "band", None, "ga"), P(None, "band", "ga")),
        check_vma=False,
    )
```

```python
import functools

import jax
import jax.numpy as jnp
from jax import lax
from jax.experimental import pallas as pl
from jax.experimental.pallas import tpu as pltpu
from jax.sharding import PartitionSpec as P

NX = 384
NY = 384
LANES = 128
UNIT = 48

width_cells = 1.5


def tables(indices):
    length = indices.shape[0]
    phases = indices[:, None] * indices[None, :] % length
    angles = phases.astype(jnp.float32) * (2.0 * jnp.pi / length)
    factor = 1.0 / jnp.sqrt(jnp.float32(length))
    return (
        (jnp.cos(angles) * factor).astype(jnp.bfloat16),
        (jnp.sin(angles) * factor).astype(jnp.bfloat16),
    )


def gaussian(distance):
    return jnp.exp(-distance * distance / (2.0 * width_cells * width_cells))


def frequency(indices, length):
    return jnp.where(indices < length // 2, indices, indices - length).astype(jnp.float32)


def dot(left, right):
    return jnp.dot(left, right, preferred_element_type=jnp.float32)


def partners(groups):
    return [0, *range(groups // 2, groups), *range(1, groups // 2)]


def step_of(count):
    return 1 if count % 2 else 2


def lasting(microseconds):
    return pl.CostEstimate(
        flops=0, bytes_accessed=int(microseconds * 3.69e6), transcendentals=0
    )


def pack_body(place, *refs):
    halves = len(refs) - 1 - refs[-1].shape[0]
    sources, messages, held = refs[:halves], refs[halves:-1], refs[-1]
    groups, count, rows, _ = held.shape
    planes = groups // halves
    for h, source in enumerate(sources):
        for i in range(count):
            split = source[0, i].reshape(planes, rows, NY)
            for p in range(planes):
                held[p * halves + h, i] = split[p]
    for partner, message in zip(partners(groups), messages):
        message[0] = held[place[0] ^ partner]


def pack(waves, place, first, count, rows, groups):
    planes = waves.shape[2]
    halves = groups // planes
    own = waves.shape[1] // halves
    return pl.pallas_call(
        pack_body,
        grid=(2, 1),
        in_specs=[pl.BlockSpec(memory_space=pltpu.SMEM)]
        + [
            pl.BlockSpec(
                (1, count, planes, rows * NY),
                functools.partial(block_at, (h * own + first) // count),
            )
            for h in range(halves)
        ],
        out_specs=[pl.BlockSpec((1, count, rows, NY), lambda c, n: (c, n, 0, 0))] * groups,
        out_shape=[jax.ShapeDtypeStruct((2, count, rows, NY), jnp.bfloat16)] * groups,
        scratch_shapes=[pltpu.VMEM((groups, count, rows, NY), jnp.bfloat16)],
        compiler_params=pltpu.CompilerParams(vmem_limit_bytes=56 << 20),
        cost_estimate=lasting(0.01),
        name="pack_planes",
    )(place, *[waves] * halves)


def block_at(base, c, n):
    return (c, base + n, 0, 0)


def mix_waves_body(w_ref, z_ref, mixed):
    _, bands, planes, width = w_ref.shape
    rows = width // NY
    per = 2 * bands
    for c in range(2):
        for n in range(bands):
            wide = w_ref[c, n].reshape(planes, rows, NY).astype(jnp.float32)
            for p in range(planes):
                at = pl.ds(p * rows * per + c * bands + n, rows, stride=per)
                for t in range(NY // LANES):
                    mixed[t, at, :] = wide[p, :, t * LANES : (t + 1) * LANES]
    for t in range(NY // LANES):
        z_ref[0, :, t * LANES : (t + 1) * LANES] = mixed[t].astype(jnp.bfloat16)


def mix_waves(waves, rows, shares):
    _, bands, planes, _ = waves.shape
    own = rows // shares
    depth = planes * own * 2 * bands
    return pl.pallas_call(
        mix_waves_body,
        grid=(shares,),
        in_specs=[pl.BlockSpec((2, bands, planes, own * NY), lambda d: (0, 0, 0, d))],
        out_specs=pl.BlockSpec((1, depth, NY), lambda d: (d, 0, 0)),
        out_shape=jax.ShapeDtypeStruct((shares, depth, NY), jnp.bfloat16),
        scratch_shapes=[pltpu.VMEM((NY // LANES, depth, LANES), jnp.float32)],
        compiler_params=pltpu.CompilerParams(vmem_limit_bytes=56 << 20),
        cost_estimate=lasting(0.01),
        name="mix_waves",
    )(waves)


def mix_space_body(s_ref, *refs):
    z_ref = refs[-1]
    bands, _, rows, _ = s_ref.shape
    size = 2 * bands * UNIT
    to = lax.broadcasted_iota(jnp.int32, (size, size), 0)
    at = lax.broadcasted_iota(jnp.int32, (size, size), 1)
    band, part, row = at // (2 * UNIT), at // UNIT % 2, at % UNIT
    chosen = (to == row * 2 * bands + part * bands + band).astype(jnp.bfloat16)
    shares, _, depth, _ = z_ref.shape
    each = shares * UNIT // rows
    for unit in range(rows // UNIT):
        cut = slice(unit * UNIT, (unit + 1) * UNIT)
        stacked = jnp.concatenate(
            [s_ref[n, c, cut] for n in range(bands) for c in range(2)], axis=0
        )
        mixed = dot(chosen, stacked).astype(jnp.bfloat16)
        z_ref[unit * each : (unit + 1) * each, 0] = mixed.reshape(each, depth, NY)


def mix_space(in_space, part, base, shares):
    bands = in_space.shape[0]
    own = NX // shares
    depth = own * 2 * bands
    rows = 2 * UNIT
    in_specs = [pl.BlockSpec((bands, 2, rows, NY), lambda d: (0, 0, d, 0))]
    operands = [in_space]
    aliases = {}
    if base is not None:
        in_specs.append(pl.BlockSpec(memory_space=pl.ANY))
        operands.append(base)
        aliases = {1: 0}
    return pl.pallas_call(
        mix_space_body,
        grid=(NX // rows,),
        in_specs=in_specs,
        out_specs=pl.BlockSpec((rows // own, 1, depth, NY), lambda d: (d, part, 0, 0)),
        out_shape=jax.ShapeDtypeStruct((shares, 2, depth, NY), jnp.bfloat16),
        input_output_aliases=aliases,
        compiler_params=pltpu.CompilerParams(vmem_limit_bytes=56 << 20),
        cost_estimate=lasting(0.01),
        name="mix_space",
    )(*operands)


def unpack_body(groups, place, *refs):
    messages, o_ref, held = refs[:groups], refs[-2], refs[-1]
    halves, planes, count, rows, _ = held.shape
    for partner, message in zip(partners(groups), messages):
        source = place[0] ^ partner
        held[lax.rem(source, halves), source // halves] = message[0]
    half = pl.program_id(1)
    for i in range(count):
        o_ref[0, i] = held[half, :, i].reshape(planes, rows * NY)


def unpack(messages, place, base, first, bands, planes):
    groups = len(messages)
    _, count, rows, _ = messages[0].shape
    halves = groups // planes
    step = step_of(count)
    own = bands // halves
    in_specs = [pl.BlockSpec(memory_space=pltpu.SMEM)] + [
        pl.BlockSpec((1, step, rows, NY), lambda c, h, n: (c, n, 0, 0))
    ] * groups
    operands = [place, *messages]
    aliases = {}
    if base is not None:
        in_specs.append(pl.BlockSpec(memory_space=pl.ANY))
        operands.append(base)
        aliases = {groups + 1: 0}
    return pl.pallas_call(
        functools.partial(unpack_body, groups),
        grid=(2, halves, count // step),
        in_specs=in_specs,
        out_specs=pl.BlockSpec(
            (1, step, planes, rows * NY), lambda c, h, n: (c, (h * own + first) // step + n, 0, 0)
        ),
        out_shape=jax.ShapeDtypeStruct((2, bands, planes, rows * NY), jnp.bfloat16),
        scratch_shapes=[pltpu.VMEM((halves, planes, step, rows, NY), jnp.bfloat16)],
        input_output_aliases=aliases,
        compiler_params=pltpu.CompilerParams(vmem_limit_bytes=56 << 20),
        cost_estimate=lasting(1.2 * count),
        name="unpack_planes",
    )(*operands)


def forward_body(groups, place, *refs):
    messages, (f_ref, b_ref, s_ref, held) = refs[:groups], refs[groups:]
    for partner, message in zip(partners(groups), messages):
        held[place[0] ^ partner] = message[...]
    for i in range(held.shape[2]):
        parts = [held[:, c, i].reshape(NX, NY) for c in range(2)]
        first = dot(jnp.concatenate(parts, axis=1), f_ref[...]).astype(jnp.bfloat16)
        first = jnp.concatenate([first[:, :NY], first[:, NY:]], axis=0)
        in_space = dot(b_ref[...], first).astype(jnp.bfloat16)
        s_ref[i, 0] = in_space[:NX]
        s_ref[i, 1] = in_space[NX:]


def forward(messages, place, forth, back):
    groups = len(messages)
    _, bands, rows, _ = messages[0].shape
    step = step_of(bands)
    square = pl.BlockSpec((2 * NX, 2 * NX), lambda n: (0, 0))
    return pl.pallas_call(
        functools.partial(forward_body, groups),
        grid=(bands // step,),
        in_specs=[pl.BlockSpec(memory_space=pltpu.SMEM)]
        + [pl.BlockSpec((2, step, rows, NY), lambda n: (0, n, 0, 0))] * groups
        + [square, square],
        out_specs=pl.BlockSpec((step, 2, NX, NY), lambda n: (n, 0, 0, 0)),
        out_shape=jax.ShapeDtypeStruct((bands, 2, NX, NY), jnp.bfloat16),
        scratch_shapes=[pltpu.VMEM((groups, 2, step, rows, NY), jnp.bfloat16)],
        compiler_params=pltpu.CompilerParams(vmem_limit_bytes=56 << 20),
        cost_estimate=lasting(0.01),
        name="forward",
    )(place, *messages, forth, back)


def inverse_body(groups, place, *refs):
    messages, (s_ref, v_ref, f_ref, b_ref) = refs[:groups], refs[groups : groups + 4]
    held = refs[-1]
    results = refs[-1 - groups : -1]
    rows = held.shape[3]
    freq_x = frequency(lax.broadcasted_iota(jnp.int32, (NX, 1), 0), NX)
    freq_y = frequency(lax.broadcasted_iota(jnp.int32, (1, NY), 1), NY)
    kinetic = 2.0 * (freq_x * freq_x / (NX * NX) + freq_y * freq_y / (NY * NY))
    for partner, message in zip(partners(groups), messages):
        held[place[0] ^ partner] = message[...]
    for i in range(held.shape[2]):
        weighted = jnp.concatenate(
            [v_ref[...] * s_ref[i, c].astype(jnp.float32) for c in range(2)], axis=0
        ).astype(jnp.bfloat16)
        back = dot(f_ref[...], weighted).astype(jnp.bfloat16)
        recip = dot(jnp.concatenate([back[:NX], back[NX:]], axis=1), b_ref[...])
        for c in range(2):
            wide = held[:, c, i].reshape(NX, NY).astype(jnp.float32)
            applied = kinetic * wide + recip[:, c * NY : (c + 1) * NY]
            held[:, c, i] = applied.astype(jnp.bfloat16).reshape(groups, rows, NY)
    for partner, result in zip(partners(groups), results):
        result[...] = held[place[0] ^ partner]


def inverse(messages, base, bands, place, in_space, potential, forth, back):
    groups = len(messages)
    rows = messages[0].shape[2]
    shape = (2, bands, rows, NY)
    step = 1 if base % 2 else step_of(bands)
    square = pl.BlockSpec((2 * NX, 2 * NX), lambda n: (0, 0))
    return pl.pallas_call(
        functools.partial(inverse_body, groups),
        grid=(bands // step,),
        in_specs=[pl.BlockSpec(memory_space=pltpu.SMEM)]
        + [pl.BlockSpec((2, step, rows, NY), lambda n: (0, base // step + n, 0, 0))] * groups
        + [
            pl.BlockSpec((step, 2, NX, NY), lambda n: (base // step + n, 0, 0, 0)),
            pl.BlockSpec((NX, NY), lambda n: (0, 0)),
            square,
            square,
        ],
        out_specs=[pl.BlockSpec((2, step, rows, NY), lambda n: (0, n, 0, 0))] * groups,
        out_shape=[jax.ShapeDtypeStruct(shape, jnp.bfloat16)] * groups,
        scratch_shapes=[pltpu.VMEM((groups, 2, step, rows, NY), jnp.bfloat16)],
        compiler_params=pltpu.CompilerParams(vmem_limit_bytes=56 << 20),
        cost_estimate=lasting(0.01),
        name="inverse",
    )(place, *messages, in_space, potential, forth, back)


def overlap_body(scale, per, z_ref, w_ref, *refs):
    o_ref, total = refs[-2:]
    shares, parts, _, _ = z_ref.shape
    bands = per // 2
    total[...] = jnp.zeros_like(total)
    pieces = [(d, h) for d in range(shares) for h in range(parts)]

    @pl.loop(0, w_ref.shape[0] // 2)
    def _(pair):
        plain, scaled = [], []
        at = pl.multiple_of(pair * 2 * per, 2 * per)
        both = [z_ref[d, h, pl.ds(at, 2 * per), :].astype(jnp.float32) for d, h in pieces]
        for k in range(2):
            wide = jnp.concatenate([rows[k * per : (k + 1) * per] for rows in both], axis=0)
            plain.append(wide.astype(jnp.bfloat16))
            scaled.append((wide * w_ref[pl.ds(pair * 2 + k, 1), :]).astype(jnp.bfloat16))
        total[...] += lax.dot_general(
            jnp.concatenate(plain, axis=1),
            jnp.concatenate(scaled, axis=1),
            (((1,), (1,)), ((), ())),
            preferred_element_type=jnp.float32,
        )

    size = total.shape[0]
    half = size // 2
    to = lax.broadcasted_iota(jnp.int32, (size, size), 0)
    at = lax.broadcasted_iota(jnp.int32, (size, size), 1)
    order = at % per // bands * half + at // per * bands + at % bands
    chosen = (to == order).astype(jnp.float32)
    grams = jnp.dot(
        chosen, total[...], precision=lax.Precision.HIGHEST, preferred_element_type=jnp.float32
    )
    grams = lax.dot_general(
        grams,
        chosen,
        (((1,), (1,)), ((), ())),
        precision=lax.Precision.HIGHEST,
        preferred_element_type=jnp.float32,
    )
    real = (grams[:half, :half] + grams[half:, half:]) * scale
    imaginary = (grams[:half, half:] - grams[half:, :half]) * scale
    if len(refs) == 3:
        real, imaginary = real + refs[0][0], imaginary + refs[0][1]
    o_ref[0] = real
    o_ref[1] = imaginary


def overlap(pieces, weights, per, scale, before=None):
    shares, parts, _, _ = pieces.shape
    size = shares * parts * per
    whole = pl.BlockSpec(memory_space=pltpu.VMEM)
    operands = [pieces, weights] + ([] if before is None else [before])
    return pl.pallas_call(
        functools.partial(overlap_body, scale, per),
        in_specs=[whole] * len(operands),
        out_specs=whole,
        out_shape=jax.ShapeDtypeStruct((2, size // 2, size // 2), jnp.float32),
        scratch_shapes=[pltpu.VMEM((size, size), jnp.float32)],
        compiler_params=pltpu.CompilerParams(vmem_limit_bytes=56 << 20),
        cost_estimate=lasting(8.0),
        name="overlap",
    )(*operands)


def shifted(messages):
    groups = len(messages)
    return [
        lax.ppermute(message, "ga", [(i, i ^ partner) for i in range(groups)])
        if partner
        else message
        for partner, message in zip(partners(groups), messages)
    ]


def split(wide):
    high = wide.astype(jnp.bfloat16)
    return high, (wide - high.astype(jnp.float32)).astype(jnp.bfloat16)


def charges_body(planes, slab_rows, place, c_ref, i_ref, o_ref, total):
    first = place[0].astype(jnp.float32)
    plane = place[1].astype(jnp.float32)
    own_x = lax.broadcasted_iota(jnp.int32, (LANES, 1), 0).astype(jnp.float32) + first
    cells_y = lax.broadcasted_iota(jnp.int32, (NY, 1), 0)
    slab_y = (cells_y // slab_rows).astype(jnp.float32)
    cells_y = cells_y.astype(jnp.float32)
    total[...] = jnp.zeros_like(total)

    @pl.loop(0, c_ref.shape[0] // 2)
    def _(pair):
        lefts, rights = [], []
        for k in range(2):
            along_u, along_v, along_w, amount, slab = [
                c_ref[pair * 2 + k, row : row + 1, :] for row in range(5)
            ]
            weight = amount * gaussian(plane - planes * along_w)
            x_high, x_low = split(gaussian(own_x - NX * along_u) * weight)
            kernel_y = gaussian(cells_y - (slab * slab_rows + slab_rows * along_v))
            y_high, y_low = split(jnp.where(slab_y == slab, kernel_y, 0.0))
            lefts += [y_low, y_high, y_high]
            rights += [x_high, x_low, x_high]
        total[...] += lax.dot_general(
            jnp.concatenate(lefts, axis=1),
            jnp.concatenate(rights, axis=1),
            (((1,), (1,)), ((), ())),
            preferred_element_type=jnp.float32,
        )

    o_ref[...] = i_ref[...] + total[...].T[: o_ref.shape[0]]


def potential_message(ionic_field, point_charge, charge_place, charge_slab, planes, halves):
    ga_count = lax.axis_size("ga")
    band_groups = lax.axis_size("band")
    devices = band_groups * ga_count
    slab_rows = NY // ga_count
    share = NX // band_groups
    piece = share * slab_rows // band_groups
    atoms = point_charge.shape[0]
    spare = -(-piece // atoms)
    band_at = lax.axis_index("band")
    charges = jnp.concatenate(
        [charge_place, point_charge[None], charge_slab[:, 0][None].astype(jnp.float32)], axis=0
    )
    ionic = ionic_field.T.reshape(planes, band_groups, band_groups, piece)
    ionic = lax.dynamic_index_in_dim(ionic, band_at, 2, keepdims=False)
    ionic = jnp.broadcast_to(
        ionic.transpose(1, 0, 2)[:, :, None], (band_groups, planes, halves, piece)
    )
    ionic = jnp.pad(ionic.reshape(devices, piece), ((0, 0), (0, spare * atoms - piece)))
    return jnp.concatenate(
        [
            jnp.broadcast_to(charges[None], (devices, 5, atoms)),
            ionic.reshape(devices, spare, atoms),
        ],
        axis=1,
    )


def own_share(message, planes, halves):
    ga_count = lax.axis_size("ga")
    band_groups = lax.axis_size("band")
    slab_rows = NY // ga_count
    share = NX // band_groups
    piece = share * slab_rows // band_groups
    atoms = message.shape[2]
    spare = message.shape[1] - 5
    band_at = lax.axis_index("band")
    ionic = message[:, 5:].reshape(band_groups, ga_count, spare * atoms)[:, :, :piece]
    ionic = ionic.transpose(1, 0, 2).reshape(ga_count, share, slab_rows)
    ionic = ionic.transpose(1, 0, 2).reshape(share, NY)
    place = jnp.stack([band_at * share, lax.axis_index("ga") // halves]).astype(jnp.int32)
    return pl.pallas_call(
        functools.partial(charges_body, planes, slab_rows),
        in_specs=[
            pl.BlockSpec(memory_space=pltpu.SMEM),
            pl.BlockSpec(memory_space=pltpu.VMEM),
            pl.BlockSpec(memory_space=pltpu.VMEM),
        ],
        out_specs=pl.BlockSpec(memory_space=pltpu.VMEM),
        out_shape=jax.ShapeDtypeStruct((share, NY), jnp.float32),
        scratch_shapes=[pltpu.VMEM((NY, LANES), jnp.float32)],
        compiler_params=pltpu.CompilerParams(vmem_limit_bytes=56 << 20),
        cost_estimate=lasting(0.01),
        name="charge_potential",
    )(place, message, ionic)


def shards(waves, ionic_field, point_charge, charge_place, charge_slab):
    ga_count = lax.axis_size("ga")
    band_groups = lax.axis_size("band")
    bands = waves.shape[1]
    planes = waves.shape[2]
    rows = NX // ga_count
    halves = ga_count // planes
    own_bands = bands // halves
    half = own_bands // 2
    chunks = [(0, half), (half, half)]
    per = 2 * bands
    pairs = [[p * halves + h for h in range(halves)] for p in range(planes)]
    ga_at, band_at = lax.axis_index("ga"), lax.axis_index("band")
    place = ga_at.astype(jnp.int32)[None]

    packed = [pack(waves, place, first, count, rows, ga_count) for first, count in chunks]
    message = potential_message(
        ionic_field, point_charge, charge_place, charge_slab, planes, halves
    )

    arrived = [shifted(packed[0])]
    message = lax.all_to_all(message, ("band", "ga"), 0, 0, tiled=True)
    mixed = mix_waves(waves, rows, band_groups)
    message, packed[1], mixed = lax.optimization_barrier((message, packed[1], mixed))
    own_potential = own_share(message, planes, halves)
    copies = jnp.broadcast_to(own_potential[None], (band_groups,) + own_potential.shape)
    potential = lax.all_to_all(copies, "band", 0, 0, tiled=True).reshape(NX, NY)
    cells = jnp.arange(NX, dtype=jnp.int32)
    arrived[0], potential, packed[1], mixed, cells = lax.optimization_barrier(
        (arrived[0], potential, packed[1], mixed, cells)
    )

    arrived.append(shifted(packed[1]))
    met_waves = lax.all_to_all(mixed, "band", 0, 0, tiled=True)
    cosine, sine = tables(cells)
    forth = jnp.concatenate(
        [jnp.concatenate([cosine, sine], axis=1), jnp.concatenate([-sine, cosine], axis=1)], axis=0
    )
    back = jnp.concatenate(
        [jnp.concatenate([cosine, -sine], axis=1), jnp.concatenate([sine, cosine], axis=1)], axis=0
    )
    in_space = [forward(arrived[0], place, forth, back)]
    shares = band_groups * halves
    mixed = mix_space(in_space[0], 0, None, shares)
    result = inverse(arrived[0], 0, half, place, in_space[0], potential, forth, back)
    arrived[1], met_waves, result, mixed = lax.optimization_barrier(
        (arrived[1], met_waves, result, mixed)
    )

    returned = [shifted(result)]
    in_space.append(forward(arrived[1], place, forth, back))
    mixed = mix_space(in_space[1], 1, mixed, shares)
    mixed, returned[0][1] = lax.optimization_barrier((mixed, returned[0][1]))
    if halves > 1:
        mixed = mixed.reshape(band_groups, halves, -1, NY)
        mixed = lax.all_to_all(mixed, "ga", 1, 1, axis_index_groups=pairs, tiled=True)
    met_space = lax.all_to_all(mixed, "band", 0, 0, tiled=True)
    if halves > 1:
        met_space = met_space.reshape(band_groups, halves, 2, -1, 2, half, NY)
        met_space = met_space.transpose(0, 3, 4, 1, 2, 5, 6)
        met_space = met_space.reshape(band_groups, 1, -1, NY)
    space_weights = own_potential
    if halves > 1:
        space_weights = lax.dynamic_slice_in_dim(
            own_potential, ga_at % halves * (NX // band_groups // halves),
            NX // band_groups // halves, 0,
        )

    share = rows // band_groups
    own_x = ga_at * rows + band_at * share + jnp.arange(share, dtype=jnp.int32)
    freq_x, freq_y = frequency(own_x, NX), frequency(jnp.arange(NY, dtype=jnp.int32), NY)
    kinetic = 2.0 * (
        freq_x[:, None] * freq_x[:, None] / (NX * NX)
        + freq_y[None, :] * freq_y[None, :] / (NY * NY)
    )
    kinetic = jnp.broadcast_to(kinetic[None], (planes, share, NY)).reshape(planes * share, NY)

    scale = 1.0 / (planes * NX * NY)
    applied_waves = unpack(returned[0], place, None, 0, bands, planes)
    grams = overlap(met_waves[:, None], kinetic, per, scale)
    spectrum = (in_space[1], potential, forth, back)
    returned.append(shifted(inverse(arrived[1], 0, half - 1, place, *spectrum)))
    grams, place = lax.optimization_barrier((grams, place))
    returned.append(shifted(inverse(arrived[1], half - 1, 1, place, *spectrum)))
    grams, applied_waves = lax.optimization_barrier((grams, applied_waves))
    full_matrix = overlap(
        met_space, space_weights, per // met_space.shape[1], scale, grams
    )
    all_bands = bands * band_groups
    col_width = all_bands // ga_count
    blocks = full_matrix.reshape(2, band_groups, bands, ga_count, col_width)
    blocks = blocks.transpose(1, 3, 0, 2, 4).reshape(
        band_groups * ga_count, 2, bands, col_width
    )
    subspace = lax.all_to_all(blocks, ("band", "ga"), 0, 0, tiled=True).sum(0)

    applied_waves = unpack(returned[1], place, applied_waves, half, bands, planes)
    applied_waves = unpack(returned[2], place, applied_waves, own_bands - 1, bands, planes)
    return (applied_waves, subspace)


def solution(mesh):
    placed = (
        P(None, "band", None, "ga"),
        P("ga", None),
        P(("band", "ga")),
        P(None, ("band", "ga")),
        P(("band", "ga"), None),
    )
    return jax.shard_map(
        shards,
        mesh=mesh,
        in_specs=placed,
        out_specs=(P(None, "band", None, "ga"), P(None, "band", "ga")),
        check_vma=False,
    )
```

```python
import functools

import jax
import jax.numpy as jnp
from jax import lax
from jax.experimental import pallas as pl
from jax.experimental.pallas import tpu as pltpu
from jax.sharding import PartitionSpec as P

NX = 384
NY = 384
LANES = 128
UNIT = 48

width_cells = 1.5


def tables(indices):
    length = indices.shape[0]
    phases = indices[:, None] * indices[None, :] % length
    angles = phases.astype(jnp.float32) * (2.0 * jnp.pi / length)
    factor = 1.0 / jnp.sqrt(jnp.float32(length))
    return (
        (jnp.cos(angles) * factor).astype(jnp.bfloat16),
        (jnp.sin(angles) * factor).astype(jnp.bfloat16),
    )


def gaussian(distance):
    return jnp.exp(-distance * distance / (2.0 * width_cells * width_cells))


def frequency(indices, length):
    return jnp.where(indices < length // 2, indices, indices - length).astype(jnp.float32)


def dot(left, right):
    return jnp.dot(left, right, preferred_element_type=jnp.float32)


def step_of(count):
    return 1 if count % 2 else 2


def lasting(microseconds):
    return pl.CostEstimate(
        flops=0, bytes_accessed=int(microseconds * 3.69e6), transcendentals=0
    )


def pack_body(place, *refs):
    halves = len(refs) - 1 - refs[-1].shape[0]
    sources, messages, held = refs[:halves], refs[halves:-1], refs[-1]
    groups, count, rows, _ = held.shape
    planes = groups // halves
    for h, source in enumerate(sources):
        for i in range(count):
            split = source[0, i].reshape(planes, rows, NY)
            for p in range(planes):
                held[p * halves + h, i] = split[p]
    for s, message in enumerate(messages):
        message[0] = held[place[0] ^ s]


def pack(waves, place, first, count, rows, groups):
    planes = waves.shape[2]
    halves = groups // planes
    own = waves.shape[1] // halves
    return pl.pallas_call(
        pack_body,
        grid=(2, 1),
        in_specs=[pl.BlockSpec(memory_space=pltpu.SMEM)]
        + [
            pl.BlockSpec(
                (1, count, planes, rows * NY),
                functools.partial(block_at, (h * own + first) // count),
            )
            for h in range(halves)
        ],
        out_specs=[pl.BlockSpec((1, count, rows, NY), lambda c, n: (c, n, 0, 0))] * groups,
        out_shape=[jax.ShapeDtypeStruct((2, count, rows, NY), jnp.bfloat16)] * groups,
        scratch_shapes=[pltpu.VMEM((groups, count, rows, NY), jnp.bfloat16)],
        compiler_params=pltpu.CompilerParams(vmem_limit_bytes=56 << 20),
        cost_estimate=lasting(0.01),
        name="pack_planes",
    )(place, *[waves] * halves)


def block_at(base, c, n):
    return (c, base + n, 0, 0)


def mix_waves_body(w_ref, z_ref, mixed):
    _, bands, planes, width = w_ref.shape
    rows = width // NY
    per = 2 * bands
    for c in range(2):
        for n in range(bands):
            wide = w_ref[c, n].reshape(planes, rows, NY).astype(jnp.float32)
            for p in range(planes):
                at = pl.ds(p * rows * per + c * bands + n, rows, stride=per)
                for t in range(NY // LANES):
                    mixed[t, at, :] = wide[p, :, t * LANES : (t + 1) * LANES]
    for t in range(NY // LANES):
        z_ref[0, :, t * LANES : (t + 1) * LANES] = mixed[t].astype(jnp.bfloat16)


def mix_waves(waves, rows, shares):
    _, bands, planes, _ = waves.shape
    own = rows // shares
    depth = planes * own * 2 * bands
    return pl.pallas_call(
        mix_waves_body,
        grid=(shares,),
        in_specs=[pl.BlockSpec((2, bands, planes, own * NY), lambda d: (0, 0, 0, d))],
        out_specs=pl.BlockSpec((1, depth, NY), lambda d: (d, 0, 0)),
        out_shape=jax.ShapeDtypeStruct((shares, depth, NY), jnp.bfloat16),
        scratch_shapes=[pltpu.VMEM((NY // LANES, depth, LANES), jnp.float32)],
        compiler_params=pltpu.CompilerParams(vmem_limit_bytes=56 << 20),
        cost_estimate=lasting(0.01),
        name="mix_waves",
    )(waves)


def mix_space_body(s_ref, *refs):
    z_ref = refs[-1]
    bands, _, rows, _ = s_ref.shape
    size = 2 * bands * UNIT
    to = lax.broadcasted_iota(jnp.int32, (size, size), 0)
    at = lax.broadcasted_iota(jnp.int32, (size, size), 1)
    band, part, row = at // (2 * UNIT), at // UNIT % 2, at % UNIT
    chosen = (to == row * 2 * bands + part * bands + band).astype(jnp.bfloat16)
    shares, _, depth, _ = z_ref.shape
    each = shares * UNIT // rows
    for unit in range(rows // UNIT):
        cut = slice(unit * UNIT, (unit + 1) * UNIT)
        stacked = jnp.concatenate(
            [s_ref[n, c, cut] for n in range(bands) for c in range(2)], axis=0
        )
        mixed = dot(chosen, stacked).astype(jnp.bfloat16)
        z_ref[unit * each : (unit + 1) * each, 0] = mixed.reshape(each, depth, NY)


def mix_space(in_space, part, base, shares):
    bands = in_space.shape[0]
    own = NX // shares
    depth = own * 2 * bands
    rows = 2 * UNIT
    in_specs = [pl.BlockSpec((bands, 2, rows, NY), lambda d: (0, 0, d, 0))]
    operands = [in_space]
    aliases = {}
    if base is not None:
        in_specs.append(pl.BlockSpec(memory_space=pl.ANY))
        operands.append(base)
        aliases = {1: 0}
    return pl.pallas_call(
        mix_space_body,
        grid=(NX // rows,),
        in_specs=in_specs,
        out_specs=pl.BlockSpec((rows // own, 1, depth, NY), lambda d: (d, part, 0, 0)),
        out_shape=jax.ShapeDtypeStruct((shares, 2, depth, NY), jnp.bfloat16),
        input_output_aliases=aliases,
        compiler_params=pltpu.CompilerParams(vmem_limit_bytes=56 << 20),
        cost_estimate=lasting(0.01),
        name="mix_space",
    )(*operands)


def unpack_body(groups, place, *refs):
    messages, o_ref, held = refs[:groups], refs[-2], refs[-1]
    halves, planes, count, rows, _ = held.shape
    for s, message in enumerate(messages):
        source = place[0] ^ s
        held[lax.rem(source, halves), source // halves] = message[0]
    half = pl.program_id(1)
    for i in range(count):
        o_ref[0, i] = held[half, :, i].reshape(planes, rows * NY)


def unpack(messages, place, base, first, bands, planes):
    groups = len(messages)
    _, count, rows, _ = messages[0].shape
    halves = groups // planes
    step = step_of(count)
    own = bands // halves
    in_specs = [pl.BlockSpec(memory_space=pltpu.SMEM)] + [
        pl.BlockSpec((1, step, rows, NY), lambda c, h, n: (c, n, 0, 0))
    ] * groups
    operands = [place, *messages]
    aliases = {}
    if base is not None:
        in_specs.append(pl.BlockSpec(memory_space=pl.ANY))
        operands.append(base)
        aliases = {groups + 1: 0}
    return pl.pallas_call(
        functools.partial(unpack_body, groups),
        grid=(2, halves, count // step),
        in_specs=in_specs,
        out_specs=pl.BlockSpec(
            (1, step, planes, rows * NY), lambda c, h, n: (c, (h * own + first) // step + n, 0, 0)
        ),
        out_shape=jax.ShapeDtypeStruct((2, bands, planes, rows * NY), jnp.bfloat16),
        scratch_shapes=[pltpu.VMEM((halves, planes, step, rows, NY), jnp.bfloat16)],
        input_output_aliases=aliases,
        compiler_params=pltpu.CompilerParams(vmem_limit_bytes=12 << 20),
        cost_estimate=lasting(1.2 * count),
        name="unpack_planes",
    )(*operands)


def forward_body(groups, place, *refs):
    messages, (f_ref, b_ref, s_ref, held) = refs[:groups], refs[groups:]
    for s, message in enumerate(messages):
        held[place[0] ^ s] = message[...]
    for i in range(held.shape[2]):
        parts = [held[:, c, i].reshape(NX, NY) for c in range(2)]
        first = dot(jnp.concatenate(parts, axis=1), f_ref[...]).astype(jnp.bfloat16)
        first = jnp.concatenate([first[:, :NY], first[:, NY:]], axis=0)
        in_space = dot(b_ref[...], first).astype(jnp.bfloat16)
        s_ref[i, 0] = in_space[:NX]
        s_ref[i, 1] = in_space[NX:]


def forward(messages, place, forth, back):
    groups = len(messages)
    _, bands, rows, _ = messages[0].shape
    step = step_of(bands)
    square = pl.BlockSpec((2 * NX, 2 * NX), lambda n: (0, 0))
    return pl.pallas_call(
        functools.partial(forward_body, groups),
        grid=(bands // step,),
        in_specs=[pl.BlockSpec(memory_space=pltpu.SMEM)]
        + [pl.BlockSpec((2, step, rows, NY), lambda n: (0, n, 0, 0))] * groups
        + [square, square],
        out_specs=pl.BlockSpec((step, 2, NX, NY), lambda n: (n, 0, 0, 0)),
        out_shape=jax.ShapeDtypeStruct((bands, 2, NX, NY), jnp.bfloat16),
        scratch_shapes=[pltpu.VMEM((groups, 2, step, rows, NY), jnp.bfloat16)],
        compiler_params=pltpu.CompilerParams(vmem_limit_bytes=56 << 20),
        cost_estimate=lasting(0.01),
        name="forward",
    )(place, *messages, forth, back)


def inverse_body(groups, place, *refs):
    messages, (s_ref, v_ref, f_ref, b_ref) = refs[:groups], refs[groups : groups + 4]
    held = refs[-1]
    results = refs[-1 - groups : -1]
    rows = held.shape[3]
    freq_x = frequency(lax.broadcasted_iota(jnp.int32, (NX, 1), 0), NX)
    freq_y = frequency(lax.broadcasted_iota(jnp.int32, (1, NY), 1), NY)
    kinetic = 2.0 * (freq_x * freq_x / (NX * NX) + freq_y * freq_y / (NY * NY))
    for s, message in enumerate(messages):
        held[place[0] ^ s] = message[...]
    for i in range(held.shape[2]):
        weighted = jnp.concatenate(
            [v_ref[...] * s_ref[i, c].astype(jnp.float32) for c in range(2)], axis=0
        ).astype(jnp.bfloat16)
        back = dot(f_ref[...], weighted).astype(jnp.bfloat16)
        recip = dot(jnp.concatenate([back[:NX], back[NX:]], axis=1), b_ref[...])
        for c in range(2):
            wide = held[:, c, i].reshape(NX, NY).astype(jnp.float32)
            applied = kinetic * wide + recip[:, c * NY : (c + 1) * NY]
            held[:, c, i] = applied.astype(jnp.bfloat16).reshape(groups, rows, NY)
    for s, result in enumerate(results):
        result[...] = held[place[0] ^ s]


def inverse(messages, base, bands, place, in_space, potential, forth, back):
    groups = len(messages)
    rows = messages[0].shape[2]
    shape = (2, bands, rows, NY)
    step = 1 if base % 2 else step_of(bands)
    square = pl.BlockSpec((2 * NX, 2 * NX), lambda n: (0, 0))
    return pl.pallas_call(
        functools.partial(inverse_body, groups),
        grid=(bands // step,),
        in_specs=[pl.BlockSpec(memory_space=pltpu.SMEM)]
        + [pl.BlockSpec((2, step, rows, NY), lambda n: (0, base // step + n, 0, 0))] * groups
        + [
            pl.BlockSpec((step, 2, NX, NY), lambda n: (base // step + n, 0, 0, 0)),
            pl.BlockSpec((NX, NY), lambda n: (0, 0)),
            square,
            square,
        ],
        out_specs=[pl.BlockSpec((2, step, rows, NY), lambda n: (0, n, 0, 0))] * groups,
        out_shape=[jax.ShapeDtypeStruct(shape, jnp.bfloat16)] * groups,
        scratch_shapes=[pltpu.VMEM((groups, 2, step, rows, NY), jnp.bfloat16)],
        compiler_params=pltpu.CompilerParams(vmem_limit_bytes=56 << 20),
        cost_estimate=lasting(0.01),
        name="inverse",
    )(place, *messages, in_space, potential, forth, back)


def overlap_body(scale, per, z_ref, w_ref, *refs):
    o_ref, total = refs[-2:]
    shares, parts, _, _ = z_ref.shape
    bands = per // 2
    total[...] = jnp.zeros_like(total)
    pieces = [(d, h) for d in range(shares) for h in range(parts)]

    @pl.loop(0, w_ref.shape[0] // 2)
    def _(pair):
        plain, scaled = [], []
        at = pl.multiple_of(pair * 2 * per, 2 * per)
        both = [z_ref[d, h, pl.ds(at, 2 * per), :].astype(jnp.float32) for d, h in pieces]
        for k in range(2):
            wide = jnp.concatenate([rows[k * per : (k + 1) * per] for rows in both], axis=0)
            plain.append(wide.astype(jnp.bfloat16))
            scaled.append((wide * w_ref[pl.ds(pair * 2 + k, 1), :]).astype(jnp.bfloat16))
        total[...] += lax.dot_general(
            jnp.concatenate(plain, axis=1),
            jnp.concatenate(scaled, axis=1),
            (((1,), (1,)), ((), ())),
            preferred_element_type=jnp.float32,
        )

    size = total.shape[0]
    half = size // 2
    to = lax.broadcasted_iota(jnp.int32, (size, size), 0)
    at = lax.broadcasted_iota(jnp.int32, (size, size), 1)
    order = at % per // bands * half + at // per * bands + at % bands
    chosen = (to == order).astype(jnp.float32)
    grams = jnp.dot(
        chosen, total[...], precision=lax.Precision.HIGHEST, preferred_element_type=jnp.float32
    )
    grams = lax.dot_general(
        grams,
        chosen,
        (((1,), (1,)), ((), ())),
        precision=lax.Precision.HIGHEST,
        preferred_element_type=jnp.float32,
    )
    real = (grams[:half, :half] + grams[half:, half:]) * scale
    imaginary = (grams[:half, half:] - grams[half:, :half]) * scale
    if len(refs) == 3:
        real, imaginary = real + refs[0][0], imaginary + refs[0][1]
    o_ref[0] = real
    o_ref[1] = imaginary


def overlap(pieces, weights, per, scale, before=None):
    shares, parts, _, _ = pieces.shape
    size = shares * parts * per
    whole = pl.BlockSpec(memory_space=pltpu.VMEM)
    operands = [pieces, weights] + ([] if before is None else [before])
    return pl.pallas_call(
        functools.partial(overlap_body, scale, per),
        in_specs=[whole] * len(operands),
        out_specs=whole,
        out_shape=jax.ShapeDtypeStruct((2, size // 2, size // 2), jnp.float32),
        scratch_shapes=[pltpu.VMEM((size, size), jnp.float32)],
        compiler_params=pltpu.CompilerParams(vmem_limit_bytes=56 << 20),
        cost_estimate=lasting(8.0),
        name="overlap",
    )(*operands)


def shifted(messages):
    groups = len(messages)
    return [
        lax.ppermute(message, "ga", [(i, i ^ s) for i in range(groups)]) if s else message
        for s, message in enumerate(messages)
    ]


def split(wide):
    high = wide.astype(jnp.bfloat16)
    return high, (wide - high.astype(jnp.float32)).astype(jnp.bfloat16)


def charges_body(planes, slab_rows, place, c_ref, i_ref, o_ref, total):
    first = place[0].astype(jnp.float32)
    plane = place[1].astype(jnp.float32)
    own_x = lax.broadcasted_iota(jnp.int32, (LANES, 1), 0).astype(jnp.float32) + first
    cells_y = lax.broadcasted_iota(jnp.int32, (NY, 1), 0)
    slab_y = (cells_y // slab_rows).astype(jnp.float32)
    cells_y = cells_y.astype(jnp.float32)
    total[...] = jnp.zeros_like(total)

    @pl.loop(0, c_ref.shape[0] // 2)
    def _(pair):
        lefts, rights = [], []
        for k in range(2):
            along_u, along_v, along_w, amount, slab = [
                c_ref[pair * 2 + k, row : row + 1, :] for row in range(5)
            ]
            weight = amount * gaussian(plane - planes * along_w)
            x_high, x_low = split(gaussian(own_x - NX * along_u) * weight)
            kernel_y = gaussian(cells_y - (slab * slab_rows + slab_rows * along_v))
            y_high, y_low = split(jnp.where(slab_y == slab, kernel_y, 0.0))
            lefts += [y_low, y_high, y_high]
            rights += [x_high, x_low, x_high]
        total[...] += lax.dot_general(
            jnp.concatenate(lefts, axis=1),
            jnp.concatenate(rights, axis=1),
            (((1,), (1,)), ((), ())),
            preferred_element_type=jnp.float32,
        )

    o_ref[...] = i_ref[...] + total[...].T[: o_ref.shape[0]]


def potential_message(ionic_field, point_charge, charge_place, charge_slab, planes, halves):
    ga_count = lax.axis_size("ga")
    band_groups = lax.axis_size("band")
    devices = band_groups * ga_count
    slab_rows = NY // ga_count
    share = NX // band_groups
    piece = share * slab_rows // band_groups
    atoms = point_charge.shape[0]
    spare = -(-piece // atoms)
    band_at = lax.axis_index("band")
    charges = jnp.concatenate(
        [charge_place, point_charge[None], charge_slab[:, 0][None].astype(jnp.float32)], axis=0
    )
    ionic = ionic_field.T.reshape(planes, band_groups, band_groups, piece)
    ionic = lax.dynamic_index_in_dim(ionic, band_at, 2, keepdims=False)
    ionic = jnp.broadcast_to(
        ionic.transpose(1, 0, 2)[:, :, None], (band_groups, planes, halves, piece)
    )
    ionic = jnp.pad(ionic.reshape(devices, piece), ((0, 0), (0, spare * atoms - piece)))
    return jnp.concatenate(
        [
            jnp.broadcast_to(charges[None], (devices, 5, atoms)),
            ionic.reshape(devices, spare, atoms),
        ],
        axis=1,
    )


def own_share(message, planes, halves):
    ga_count = lax.axis_size("ga")
    band_groups = lax.axis_size("band")
    slab_rows = NY // ga_count
    share = NX // band_groups
    piece = share * slab_rows // band_groups
    atoms = message.shape[2]
    spare = message.shape[1] - 5
    band_at = lax.axis_index("band")
    ionic = message[:, 5:].reshape(band_groups, ga_count, spare * atoms)[:, :, :piece]
    ionic = ionic.transpose(1, 0, 2).reshape(ga_count, share, slab_rows)
    ionic = ionic.transpose(1, 0, 2).reshape(share, NY)
    place = jnp.stack([band_at * share, lax.axis_index("ga") // halves]).astype(jnp.int32)
    return pl.pallas_call(
        functools.partial(charges_body, planes, slab_rows),
        in_specs=[
            pl.BlockSpec(memory_space=pltpu.SMEM),
            pl.BlockSpec(memory_space=pltpu.VMEM),
            pl.BlockSpec(memory_space=pltpu.VMEM),
        ],
        out_specs=pl.BlockSpec(memory_space=pltpu.VMEM),
        out_shape=jax.ShapeDtypeStruct((share, NY), jnp.float32),
        scratch_shapes=[pltpu.VMEM((NY, LANES), jnp.float32)],
        compiler_params=pltpu.CompilerParams(vmem_limit_bytes=56 << 20),
        cost_estimate=lasting(0.01),
        name="charge_potential",
    )(place, message, ionic)


def shards(waves, ionic_field, point_charge, charge_place, charge_slab):
    ga_count = lax.axis_size("ga")
    band_groups = lax.axis_size("band")
    bands = waves.shape[1]
    planes = waves.shape[2]
    rows = NX // ga_count
    halves = ga_count // planes
    own_bands = bands // halves
    half = own_bands // 2
    chunks = [(0, half), (half, half)]
    per = 2 * bands
    pairs = [[p * halves + h for h in range(halves)] for p in range(planes)]
    ga_at, band_at = lax.axis_index("ga"), lax.axis_index("band")
    place = ga_at.astype(jnp.int32)[None]

    packed = [pack(waves, place, first, count, rows, ga_count) for first, count in chunks]
    message = potential_message(
        ionic_field, point_charge, charge_place, charge_slab, planes, halves
    )

    arrived = [shifted(packed[0])]
    message = lax.all_to_all(message, ("band", "ga"), 0, 0, tiled=True)
    mixed = mix_waves(waves, rows, band_groups)
    message, packed[1], mixed = lax.optimization_barrier((message, packed[1], mixed))
    own_potential = own_share(message, planes, halves)
    copies = jnp.broadcast_to(own_potential[None], (band_groups,) + own_potential.shape)
    potential = lax.all_to_all(copies, "band", 0, 0, tiled=True).reshape(NX, NY)
    cells = jnp.arange(NX, dtype=jnp.int32)
    arrived[0], potential, packed[1], mixed, cells = lax.optimization_barrier(
        (arrived[0], potential, packed[1], mixed, cells)
    )

    arrived.append(shifted(packed[1]))
    met_waves = lax.all_to_all(mixed, "band", 0, 0, tiled=True)
    cosine, sine = tables(cells)
    forth = jnp.concatenate(
        [jnp.concatenate([cosine, sine], axis=1), jnp.concatenate([-sine, cosine], axis=1)], axis=0
    )
    back = jnp.concatenate(
        [jnp.concatenate([cosine, -sine], axis=1), jnp.concatenate([sine, cosine], axis=1)], axis=0
    )
    in_space = [forward(arrived[0], place, forth, back)]
    shares = band_groups * halves
    mixed = mix_space(in_space[0], 0, None, shares)
    result = inverse(arrived[0], 0, half, place, in_space[0], potential, forth, back)
    arrived[1], met_waves, result, mixed = lax.optimization_barrier(
        (arrived[1], met_waves, result, mixed)
    )

    returned = [shifted(result)]
    in_space.append(forward(arrived[1], place, forth, back))
    mixed = mix_space(in_space[1], 1, mixed, shares)
    middle = ga_count // 2
    mixed, returned[0][middle] = lax.optimization_barrier((mixed, returned[0][middle]))
    if halves > 1:
        mixed = mixed.reshape(band_groups, halves, -1, NY)
        mixed = lax.all_to_all(mixed, "ga", 1, 1, axis_index_groups=pairs, tiled=True)
    met_space = lax.all_to_all(mixed, "band", 0, 0, tiled=True)
    if halves > 1:
        met_space = met_space.reshape(band_groups, halves, 2, -1, 2, half, NY)
        met_space = met_space.transpose(0, 3, 4, 1, 2, 5, 6)
        met_space = met_space.reshape(band_groups, 1, -1, NY)
    space_weights = own_potential
    if halves > 1:
        space_weights = lax.dynamic_slice_in_dim(
            own_potential, ga_at % halves * (NX // band_groups // halves),
            NX // band_groups // halves, 0,
        )

    share = rows // band_groups
    own_x = ga_at * rows + band_at * share + jnp.arange(share, dtype=jnp.int32)
    freq_x, freq_y = frequency(own_x, NX), frequency(jnp.arange(NY, dtype=jnp.int32), NY)
    kinetic = 2.0 * (
        freq_x[:, None] * freq_x[:, None] / (NX * NX)
        + freq_y[None, :] * freq_y[None, :] / (NY * NY)
    )
    kinetic = jnp.broadcast_to(kinetic[None], (planes, share, NY)).reshape(planes * share, NY)

    scale = 1.0 / (planes * NX * NY)
    applied_waves = unpack(returned[0], place, None, 0, bands, planes)
    grams = overlap(met_waves[:, None], kinetic, per, scale)
    spectrum = (in_space[1], potential, forth, back)
    returned.append(shifted(inverse(arrived[1], 0, half - 1, place, *spectrum)))
    grams, place = lax.optimization_barrier((grams, place))
    returned.append(shifted(inverse(arrived[1], half - 1, 1, place, *spectrum)))
    grams, applied_waves = lax.optimization_barrier((grams, applied_waves))
    full_matrix = overlap(
        met_space, space_weights, per // met_space.shape[1], scale, grams
    )
    all_bands = bands * band_groups
    col_width = all_bands // ga_count
    blocks = full_matrix.reshape(2, band_groups, bands, ga_count, col_width)
    blocks = blocks.transpose(1, 3, 0, 2, 4).reshape(
        band_groups * ga_count, 2, bands * col_width
    )
    subspace = lax.all_to_all(blocks, ("band", "ga"), 0, 0, tiled=True).sum(0)
    subspace = subspace.reshape(2, bands, col_width)

    applied_waves = unpack(returned[1], place, applied_waves, half, bands, planes)
    applied_waves = unpack(returned[2], place, applied_waves, own_bands - 1, bands, planes)
    return (applied_waves, subspace)


def solution(mesh):
    placed = (
        P(None, "band", None, "ga"),
        P("ga", None),
        P(("band", "ga")),
        P(None, ("band", "ga")),
        P(("band", "ga"), None),
    )
    return jax.shard_map(
        shards,
        mesh=mesh,
        in_specs=placed,
        out_specs=(P(None, "band", None, "ga"), P(None, "band", "ga")),
        check_vma=False,
    )
```

```python
import functools

import jax
import jax.numpy as jnp
from jax import lax
from jax.experimental import pallas as pl
from jax.experimental.pallas import tpu as pltpu
from jax.sharding import PartitionSpec as P

NX = 384
NY = 384
LANES = 128
UNIT = 48

width_cells = 1.5


def tables(indices):
    length = indices.shape[0]
    phases = indices[:, None] * indices[None, :] % length
    angles = phases.astype(jnp.float32) * (2.0 * jnp.pi / length)
    factor = 1.0 / jnp.sqrt(jnp.float32(length))
    return (
        (jnp.cos(angles) * factor).astype(jnp.bfloat16),
        (jnp.sin(angles) * factor).astype(jnp.bfloat16),
    )


def gaussian(distance):
    return jnp.exp(-distance * distance / (2.0 * width_cells * width_cells))


def frequency(indices, length):
    return jnp.where(indices < length // 2, indices, indices - length).astype(jnp.float32)


def dot(left, right):
    return jnp.dot(left, right, preferred_element_type=jnp.float32)


def step_of(count):
    return 1 if count % 2 else 2


def lasting(microseconds):
    return pl.CostEstimate(
        flops=0, bytes_accessed=int(microseconds * 3.69e6), transcendentals=0
    )


def pack_body(place, *refs):
    halves = len(refs) - 1 - refs[-1].shape[0]
    sources, messages, held = refs[:halves], refs[halves:-1], refs[-1]
    groups, count, rows, _ = held.shape
    planes = groups // halves
    for h, source in enumerate(sources):
        for i in range(count):
            split = source[0, i].reshape(planes, rows, NY)
            for p in range(planes):
                held[p * halves + h, i] = split[p]
    for s, message in enumerate(messages):
        message[0] = held[place[0] ^ s]


def pack(waves, place, first, count, rows, groups):
    planes = waves.shape[2]
    halves = groups // planes
    own = waves.shape[1] // halves
    return pl.pallas_call(
        pack_body,
        grid=(2, 1),
        in_specs=[pl.BlockSpec(memory_space=pltpu.SMEM)]
        + [
            pl.BlockSpec(
                (1, count, planes, rows * NY),
                functools.partial(block_at, (h * own + first) // count),
            )
            for h in range(halves)
        ],
        out_specs=[pl.BlockSpec((1, count, rows, NY), lambda c, n: (c, n, 0, 0))] * groups,
        out_shape=[jax.ShapeDtypeStruct((2, count, rows, NY), jnp.bfloat16)] * groups,
        scratch_shapes=[pltpu.VMEM((groups, count, rows, NY), jnp.bfloat16)],
        compiler_params=pltpu.CompilerParams(vmem_limit_bytes=56 << 20),
        cost_estimate=lasting(0.01),
        name="pack_planes",
    )(place, *[waves] * halves)


def block_at(base, c, n):
    return (c, base + n, 0, 0)


def mix_waves_body(w_ref, z_ref, mixed):
    _, bands, planes, width = w_ref.shape
    rows = width // NY
    per = 2 * bands
    for c in range(2):
        for n in range(bands):
            wide = w_ref[c, n].reshape(planes, rows, NY).astype(jnp.float32)
            for p in range(planes):
                at = pl.ds(p * rows * per + c * bands + n, rows, stride=per)
                for t in range(NY // LANES):
                    mixed[t, at, :] = wide[p, :, t * LANES : (t + 1) * LANES]
    for t in range(NY // LANES):
        z_ref[0, :, t * LANES : (t + 1) * LANES] = mixed[t].astype(jnp.bfloat16)


def mix_waves(waves, rows, shares):
    _, bands, planes, _ = waves.shape
    own = rows // shares
    depth = planes * own * 2 * bands
    return pl.pallas_call(
        mix_waves_body,
        grid=(shares,),
        in_specs=[pl.BlockSpec((2, bands, planes, own * NY), lambda d: (0, 0, 0, d))],
        out_specs=pl.BlockSpec((1, depth, NY), lambda d: (d, 0, 0)),
        out_shape=jax.ShapeDtypeStruct((shares, depth, NY), jnp.bfloat16),
        scratch_shapes=[pltpu.VMEM((NY // LANES, depth, LANES), jnp.float32)],
        compiler_params=pltpu.CompilerParams(vmem_limit_bytes=56 << 20),
        cost_estimate=lasting(0.01),
        name="mix_waves",
    )(waves)


def mix_space_body(s_ref, *refs):
    z_ref = refs[-1]
    bands, _, rows, _ = s_ref.shape
    size = 2 * bands * UNIT
    to = lax.broadcasted_iota(jnp.int32, (size, size), 0)
    at = lax.broadcasted_iota(jnp.int32, (size, size), 1)
    band, part, row = at // (2 * UNIT), at // UNIT % 2, at % UNIT
    chosen = (to == row * 2 * bands + part * bands + band).astype(jnp.bfloat16)
    shares, _, depth, _ = z_ref.shape
    each = shares * UNIT // rows
    for unit in range(rows // UNIT):
        cut = slice(unit * UNIT, (unit + 1) * UNIT)
        stacked = jnp.concatenate(
            [s_ref[n, c, cut] for n in range(bands) for c in range(2)], axis=0
        )
        mixed = dot(chosen, stacked).astype(jnp.bfloat16)
        z_ref[unit * each : (unit + 1) * each, 0] = mixed.reshape(each, depth, NY)


def mix_space(in_space, part, base, shares):
    bands = in_space.shape[0]
    own = NX // shares
    depth = own * 2 * bands
    rows = 2 * UNIT
    in_specs = [pl.BlockSpec((bands, 2, rows, NY), lambda d: (0, 0, d, 0))]
    operands = [in_space]
    aliases = {}
    if base is not None:
        in_specs.append(pl.BlockSpec(memory_space=pl.ANY))
        operands.append(base)
        aliases = {1: 0}
    return pl.pallas_call(
        mix_space_body,
        grid=(NX // rows,),
        in_specs=in_specs,
        out_specs=pl.BlockSpec((rows // own, 1, depth, NY), lambda d: (d, part, 0, 0)),
        out_shape=jax.ShapeDtypeStruct((shares, 2, depth, NY), jnp.bfloat16),
        input_output_aliases=aliases,
        compiler_params=pltpu.CompilerParams(vmem_limit_bytes=56 << 20),
        cost_estimate=lasting(0.01),
        name="mix_space",
    )(*operands)


def unpack_body(groups, place, *refs):
    messages, o_ref, held = refs[:groups], refs[-2], refs[-1]
    halves, planes, count, rows, _ = held.shape
    for s, message in enumerate(messages):
        source = place[0] ^ s
        held[lax.rem(source, halves), source // halves] = message[0]
    half = pl.program_id(1)
    for i in range(count):
        o_ref[0, i] = held[half, :, i].reshape(planes, rows * NY)


def unpack(messages, place, base, first, bands, planes):
    groups = len(messages)
    _, count, rows, _ = messages[0].shape
    halves = groups // planes
    step = step_of(count)
    own = bands // halves
    in_specs = [pl.BlockSpec(memory_space=pltpu.SMEM)] + [
        pl.BlockSpec((1, step, rows, NY), lambda c, h, n: (c, n, 0, 0))
    ] * groups
    operands = [place, *messages]
    aliases = {}
    if base is not None:
        in_specs.append(pl.BlockSpec(memory_space=pl.ANY))
        operands.append(base)
        aliases = {groups + 1: 0}
    return pl.pallas_call(
        functools.partial(unpack_body, groups),
        grid=(2, halves, count // step),
        in_specs=in_specs,
        out_specs=pl.BlockSpec(
            (1, step, planes, rows * NY), lambda c, h, n: (c, (h * own + first) // step + n, 0, 0)
        ),
        out_shape=jax.ShapeDtypeStruct((2, bands, planes, rows * NY), jnp.bfloat16),
        scratch_shapes=[pltpu.VMEM((halves, planes, step, rows, NY), jnp.bfloat16)],
        input_output_aliases=aliases,
        compiler_params=pltpu.CompilerParams(vmem_limit_bytes=12 << 20),
        cost_estimate=lasting(1.2 * count),
        name="unpack_planes",
    )(*operands)


def forward_body(groups, place, *refs):
    messages, (f_ref, b_ref, s_ref, held) = refs[:groups], refs[groups:]
    for s, message in enumerate(messages):
        held[place[0] ^ s] = message[...]
    for i in range(held.shape[2]):
        parts = [held[:, c, i].reshape(NX, NY) for c in range(2)]
        first = dot(jnp.concatenate(parts, axis=1), f_ref[...]).astype(jnp.bfloat16)
        first = jnp.concatenate([first[:, :NY], first[:, NY:]], axis=0)
        in_space = dot(b_ref[...], first).astype(jnp.bfloat16)
        s_ref[i, 0] = in_space[:NX]
        s_ref[i, 1] = in_space[NX:]


def forward(messages, place, forth, back):
    groups = len(messages)
    _, bands, rows, _ = messages[0].shape
    step = step_of(bands)
    square = pl.BlockSpec((2 * NX, 2 * NX), lambda n: (0, 0))
    return pl.pallas_call(
        functools.partial(forward_body, groups),
        grid=(bands // step,),
        in_specs=[pl.BlockSpec(memory_space=pltpu.SMEM)]
        + [pl.BlockSpec((2, step, rows, NY), lambda n: (0, n, 0, 0))] * groups
        + [square, square],
        out_specs=pl.BlockSpec((step, 2, NX, NY), lambda n: (n, 0, 0, 0)),
        out_shape=jax.ShapeDtypeStruct((bands, 2, NX, NY), jnp.bfloat16),
        scratch_shapes=[pltpu.VMEM((groups, 2, step, rows, NY), jnp.bfloat16)],
        compiler_params=pltpu.CompilerParams(vmem_limit_bytes=56 << 20),
        cost_estimate=lasting(0.01),
        name="forward",
    )(place, *messages, forth, back)


def inverse_body(groups, place, *refs):
    messages, (s_ref, v_ref, f_ref, b_ref) = refs[:groups], refs[groups : groups + 4]
    held = refs[-1]
    results = refs[-1 - groups : -1]
    rows = held.shape[3]
    freq_x = frequency(lax.broadcasted_iota(jnp.int32, (NX, 1), 0), NX)
    freq_y = frequency(lax.broadcasted_iota(jnp.int32, (1, NY), 1), NY)
    kinetic = 2.0 * (freq_x * freq_x / (NX * NX) + freq_y * freq_y / (NY * NY))
    for s, message in enumerate(messages):
        held[place[0] ^ s] = message[...]
    for i in range(held.shape[2]):
        weighted = jnp.concatenate(
            [v_ref[...] * s_ref[i, c].astype(jnp.float32) for c in range(2)], axis=0
        ).astype(jnp.bfloat16)
        back = dot(f_ref[...], weighted).astype(jnp.bfloat16)
        recip = dot(jnp.concatenate([back[:NX], back[NX:]], axis=1), b_ref[...])
        for c in range(2):
            wide = held[:, c, i].reshape(NX, NY).astype(jnp.float32)
            applied = kinetic * wide + recip[:, c * NY : (c + 1) * NY]
            held[:, c, i] = applied.astype(jnp.bfloat16).reshape(groups, rows, NY)
    for s, result in enumerate(results):
        result[...] = held[place[0] ^ s]


def inverse(messages, base, bands, place, in_space, potential, forth, back):
    groups = len(messages)
    rows = messages[0].shape[2]
    shape = (2, bands, rows, NY)
    step = 1 if base % 2 else step_of(bands)
    square = pl.BlockSpec((2 * NX, 2 * NX), lambda n: (0, 0))
    return pl.pallas_call(
        functools.partial(inverse_body, groups),
        grid=(bands // step,),
        in_specs=[pl.BlockSpec(memory_space=pltpu.SMEM)]
        + [pl.BlockSpec((2, step, rows, NY), lambda n: (0, base // step + n, 0, 0))] * groups
        + [
            pl.BlockSpec((step, 2, NX, NY), lambda n: (base // step + n, 0, 0, 0)),
            pl.BlockSpec((NX, NY), lambda n: (0, 0)),
            square,
            square,
        ],
        out_specs=[pl.BlockSpec((2, step, rows, NY), lambda n: (0, n, 0, 0))] * groups,
        out_shape=[jax.ShapeDtypeStruct(shape, jnp.bfloat16)] * groups,
        scratch_shapes=[pltpu.VMEM((groups, 2, step, rows, NY), jnp.bfloat16)],
        compiler_params=pltpu.CompilerParams(vmem_limit_bytes=56 << 20),
        cost_estimate=lasting(0.01),
        name="inverse",
    )(place, *messages, in_space, potential, forth, back)


def overlap_body(scale, per, z_ref, w_ref, *refs):
    o_ref, total = refs[-2:]
    shares, parts, _, _ = z_ref.shape
    bands = per // 2
    total[...] = jnp.zeros_like(total)
    pieces = [(d, h) for d in range(shares) for h in range(parts)]

    @pl.loop(0, w_ref.shape[0] // 2)
    def _(pair):
        plain, scaled = [], []
        at = pl.multiple_of(pair * 2 * per, 2 * per)
        both = [z_ref[d, h, pl.ds(at, 2 * per), :].astype(jnp.float32) for d, h in pieces]
        for k in range(2):
            wide = jnp.concatenate([rows[k * per : (k + 1) * per] for rows in both], axis=0)
            plain.append(wide.astype(jnp.bfloat16))
            scaled.append((wide * w_ref[pl.ds(pair * 2 + k, 1), :]).astype(jnp.bfloat16))
        total[...] += lax.dot_general(
            jnp.concatenate(plain, axis=1),
            jnp.concatenate(scaled, axis=1),
            (((1,), (1,)), ((), ())),
            preferred_element_type=jnp.float32,
        )

    size = total.shape[0]
    half = size // 2
    to = lax.broadcasted_iota(jnp.int32, (size, size), 0)
    at = lax.broadcasted_iota(jnp.int32, (size, size), 1)
    order = at % per // bands * half + at // per * bands + at % bands
    chosen = (to == order).astype(jnp.float32)
    grams = jnp.dot(
        chosen, total[...], precision=lax.Precision.HIGHEST, preferred_element_type=jnp.float32
    )
    grams = lax.dot_general(
        grams,
        chosen,
        (((1,), (1,)), ((), ())),
        precision=lax.Precision.HIGHEST,
        preferred_element_type=jnp.float32,
    )
    real = (grams[:half, :half] + grams[half:, half:]) * scale
    imaginary = (grams[:half, half:] - grams[half:, :half]) * scale
    if len(refs) == 3:
        real, imaginary = real + refs[0][0], imaginary + refs[0][1]
    o_ref[0] = real
    o_ref[1] = imaginary


def overlap(pieces, weights, per, scale, before=None):
    shares, parts, _, _ = pieces.shape
    size = shares * parts * per
    whole = pl.BlockSpec(memory_space=pltpu.VMEM)
    operands = [pieces, weights] + ([] if before is None else [before])
    return pl.pallas_call(
        functools.partial(overlap_body, scale, per),
        in_specs=[whole] * len(operands),
        out_specs=whole,
        out_shape=jax.ShapeDtypeStruct((2, size // 2, size // 2), jnp.float32),
        scratch_shapes=[pltpu.VMEM((size, size), jnp.float32)],
        compiler_params=pltpu.CompilerParams(vmem_limit_bytes=56 << 20),
        cost_estimate=lasting(8.0),
        name="overlap",
    )(*operands)


def shifted(messages):
    groups = len(messages)
    return [
        lax.ppermute(message, "ga", [(i, i ^ s) for i in range(groups)]) if s else message
        for s, message in enumerate(messages)
    ]


def split(wide):
    high = wide.astype(jnp.bfloat16)
    return high, (wide - high.astype(jnp.float32)).astype(jnp.bfloat16)


def charges_body(planes, slab_rows, place, c_ref, i_ref, o_ref, total):
    first = place[0].astype(jnp.float32)
    plane = place[1].astype(jnp.float32)
    own_x = lax.broadcasted_iota(jnp.int32, (LANES, 1), 0).astype(jnp.float32) + first
    cells_y = lax.broadcasted_iota(jnp.int32, (NY, 1), 0)
    slab_y = (cells_y // slab_rows).astype(jnp.float32)
    cells_y = cells_y.astype(jnp.float32)
    total[...] = jnp.zeros_like(total)

    @pl.loop(0, c_ref.shape[0] // 2)
    def _(pair):
        lefts, rights = [], []
        for k in range(2):
            along_u, along_v, along_w, amount, slab = [
                c_ref[pair * 2 + k, row : row + 1, :] for row in range(5)
            ]
            weight = amount * gaussian(plane - planes * along_w)
            x_high, x_low = split(gaussian(own_x - NX * along_u) * weight)
            kernel_y = gaussian(cells_y - (slab * slab_rows + slab_rows * along_v))
            y_high, y_low = split(jnp.where(slab_y == slab, kernel_y, 0.0))
            lefts += [y_low, y_high, y_high]
            rights += [x_high, x_low, x_high]
        total[...] += lax.dot_general(
            jnp.concatenate(lefts, axis=1),
            jnp.concatenate(rights, axis=1),
            (((1,), (1,)), ((), ())),
            preferred_element_type=jnp.float32,
        )

    o_ref[...] = i_ref[...] + total[...].T[: o_ref.shape[0]]


def potential_message(ionic_field, point_charge, charge_place, charge_slab, planes, halves):
    ga_count = lax.axis_size("ga")
    band_groups = lax.axis_size("band")
    devices = band_groups * ga_count
    slab_rows = NY // ga_count
    share = NX // band_groups
    piece = share * slab_rows // band_groups
    atoms = point_charge.shape[0]
    spare = -(-piece // atoms)
    band_at = lax.axis_index("band")
    charges = jnp.concatenate(
        [charge_place, point_charge[None], charge_slab[:, 0][None].astype(jnp.float32)], axis=0
    )
    ionic = ionic_field.T.reshape(planes, band_groups, band_groups, piece)
    ionic = lax.dynamic_index_in_dim(ionic, band_at, 2, keepdims=False)
    ionic = jnp.broadcast_to(
        ionic.transpose(1, 0, 2)[:, :, None], (band_groups, planes, halves, piece)
    )
    ionic = jnp.pad(ionic.reshape(devices, piece), ((0, 0), (0, spare * atoms - piece)))
    return jnp.concatenate(
        [
            jnp.broadcast_to(charges[None], (devices, 5, atoms)),
            ionic.reshape(devices, spare, atoms),
        ],
        axis=1,
    )


def own_share(message, planes, halves):
    ga_count = lax.axis_size("ga")
    band_groups = lax.axis_size("band")
    slab_rows = NY // ga_count
    share = NX // band_groups
    piece = share * slab_rows // band_groups
    atoms = message.shape[2]
    spare = message.shape[1] - 5
    band_at = lax.axis_index("band")
    ionic = message[:, 5:].reshape(band_groups, ga_count, spare * atoms)[:, :, :piece]
    ionic = ionic.transpose(1, 0, 2).reshape(ga_count, share, slab_rows)
    ionic = ionic.transpose(1, 0, 2).reshape(share, NY)
    place = jnp.stack([band_at * share, lax.axis_index("ga") // halves]).astype(jnp.int32)
    return pl.pallas_call(
        functools.partial(charges_body, planes, slab_rows),
        in_specs=[
            pl.BlockSpec(memory_space=pltpu.SMEM),
            pl.BlockSpec(memory_space=pltpu.VMEM),
            pl.BlockSpec(memory_space=pltpu.VMEM),
        ],
        out_specs=pl.BlockSpec(memory_space=pltpu.VMEM),
        out_shape=jax.ShapeDtypeStruct((share, NY), jnp.float32),
        scratch_shapes=[pltpu.VMEM((NY, LANES), jnp.float32)],
        compiler_params=pltpu.CompilerParams(vmem_limit_bytes=56 << 20),
        cost_estimate=lasting(0.01),
        name="charge_potential",
    )(place, message, ionic)


def shards(waves, ionic_field, point_charge, charge_place, charge_slab):
    ga_count = lax.axis_size("ga")
    band_groups = lax.axis_size("band")
    bands = waves.shape[1]
    planes = waves.shape[2]
    rows = NX // ga_count
    halves = ga_count // planes
    own_bands = bands // halves
    half = own_bands // 2
    chunks = [(0, half), (half, half)]
    per = 2 * bands
    pairs = [[p * halves + h for h in range(halves)] for p in range(planes)]
    ga_at, band_at = lax.axis_index("ga"), lax.axis_index("band")
    place = ga_at.astype(jnp.int32)[None]

    packed = [pack(waves, place, first, count, rows, ga_count) for first, count in chunks]
    message = potential_message(
        ionic_field, point_charge, charge_place, charge_slab, planes, halves
    )

    arrived = [shifted(packed[0])]
    message = lax.all_to_all(message, ("band", "ga"), 0, 0, tiled=True)
    mixed = mix_waves(waves, rows, band_groups)
    message, packed[1], mixed = lax.optimization_barrier((message, packed[1], mixed))
    own_potential = own_share(message, planes, halves)
    copies = jnp.broadcast_to(own_potential[None], (band_groups,) + own_potential.shape)
    potential = lax.all_to_all(copies, "band", 0, 0, tiled=True).reshape(NX, NY)
    cells = jnp.arange(NX, dtype=jnp.int32)
    arrived[0], potential, packed[1], mixed, cells = lax.optimization_barrier(
        (arrived[0], potential, packed[1], mixed, cells)
    )

    arrived.append(shifted(packed[1]))
    met_waves = lax.all_to_all(mixed, "band", 0, 0, tiled=True)
    cosine, sine = tables(cells)
    forth = jnp.concatenate(
        [jnp.concatenate([cosine, sine], axis=1), jnp.concatenate([-sine, cosine], axis=1)], axis=0
    )
    back = jnp.concatenate(
        [jnp.concatenate([cosine, -sine], axis=1), jnp.concatenate([sine, cosine], axis=1)], axis=0
    )
    in_space = [forward(arrived[0], place, forth, back)]
    shares = band_groups * halves
    mixed = mix_space(in_space[0], 0, None, shares)
    result = inverse(arrived[0], 0, half, place, in_space[0], potential, forth, back)
    arrived[1], met_waves, result, mixed = lax.optimization_barrier(
        (arrived[1], met_waves, result, mixed)
    )

    returned = [shifted(result)]
    in_space.append(forward(arrived[1], place, forth, back))
    mixed = mix_space(in_space[1], 1, mixed, shares)
    middle = ga_count // 2
    mixed, returned[0][middle] = lax.optimization_barrier((mixed, returned[0][middle]))
    if halves > 1:
        mixed = mixed.reshape(band_groups, halves, -1, NY)
        mixed = lax.all_to_all(mixed, "ga", 1, 1, axis_index_groups=pairs, tiled=True)
    met_space = lax.all_to_all(mixed, "band", 0, 0, tiled=True)
    if halves > 1:
        met_space = met_space.reshape(band_groups, halves, 2, -1, 2, half, NY)
        met_space = met_space.transpose(0, 3, 4, 1, 2, 5, 6)
        met_space = met_space.reshape(band_groups, 1, -1, NY)
    space_weights = own_potential
    if halves > 1:
        space_weights = lax.dynamic_slice_in_dim(
            own_potential, ga_at % halves * (NX // band_groups // halves),
            NX // band_groups // halves, 0,
        )

    share = rows // band_groups
    own_x = ga_at * rows + band_at * share + jnp.arange(share, dtype=jnp.int32)
    freq_x, freq_y = frequency(own_x, NX), frequency(jnp.arange(NY, dtype=jnp.int32), NY)
    kinetic = 2.0 * (
        freq_x[:, None] * freq_x[:, None] / (NX * NX)
        + freq_y[None, :] * freq_y[None, :] / (NY * NY)
    )
    kinetic = jnp.broadcast_to(kinetic[None], (planes, share, NY)).reshape(planes * share, NY)

    scale = 1.0 / (planes * NX * NY)
    applied_waves = unpack(returned[0], place, None, 0, bands, planes)
    grams = overlap(met_waves[:, None], kinetic, per, scale)
    spectrum = (in_space[1], potential, forth, back)
    returned.append(shifted(inverse(arrived[1], 0, half - 1, place, *spectrum)))
    grams, place = lax.optimization_barrier((grams, place))
    returned.append(shifted(inverse(arrived[1], half - 1, 1, place, *spectrum)))
    full_matrix = overlap(
        met_space, space_weights, per // met_space.shape[1], scale, grams
    )
    all_bands = bands * band_groups
    col_width = all_bands // ga_count
    blocks = full_matrix.reshape(2, band_groups, bands, ga_count, col_width)
    blocks = blocks.transpose(1, 3, 0, 2, 4).reshape(
        band_groups * ga_count, 2, bands * col_width
    )
    subspace = lax.all_to_all(blocks, ("band", "ga"), 0, 0, tiled=True).sum(0)
    subspace = subspace.reshape(2, bands, col_width)

    applied_waves = unpack(returned[1], place, applied_waves, half, bands, planes)
    applied_waves = unpack(returned[2], place, applied_waves, own_bands - 1, bands, planes)
    return (applied_waves, subspace)


def solution(mesh):
    placed = (
        P(None, "band", None, "ga"),
        P("ga", None),
        P(("band", "ga")),
        P(None, ("band", "ga")),
        P(("band", "ga"), None),
    )
    return jax.shard_map(
        shards,
        mesh=mesh,
        in_specs=placed,
        out_specs=(P(None, "band", None, "ga"), P(None, "band", "ga")),
        check_vma=False,
    )
```
